32 devices in a mesh: doc: 2 (over core), seq: 4 (over y, x), mp: 4 (over z).
Axes of the slice: x: 2, y: 2, z: 4, core: 2. Of those that a mesh axis runs over, the one named last changes fastest.
Arguments:
- hidden_in: bfloat16 [6144, 2048], P(('doc', 'seq')), may hold values from -6 to 6
- cotangent: bfloat16 [6144, 2048], P(('doc', 'seq')), may hold values from -6 to 6
- segment_ids: int32 [6144], P(('doc', 'seq')), may hold values from 0 to 4, as said below
- padding: int32 [6144], P(('doc', 'seq')), may hold values 0 or 1
- span_order: int32 [8], replicated, may hold values from 0 to 7, as said below
- gain_attn: float32 [2048], replicated, may hold values from 0.1 to 1.9
- gain_mlp: float32 [2048], replicated, may hold values from 0.1 to 1.9
- w_query: bfloat16 [2048, 2048], P(None, 'mp'), may hold values from -0.125 to 0.125
- w_key: bfloat16 [2048, 2048], P(None, 'mp'), may hold values from -0.125 to 0.125
- w_value: bfloat16 [2048, 2048], P(None, 'mp'), may hold values from -0.125 to 0.125
- w_out: bfloat16 [2048, 2048], P('mp'), may hold values from -0.125 to 0.125
- w_gate: bfloat16 [2048, 5632], P(None, 'mp'), may hold values from -0.125 to 0.125
- w_up: bfloat16 [2048, 5632], P(None, 'mp'), may hold values from -0.125 to 0.125
- w_down: bfloat16 [5632, 2048], P('mp'), may hold values from -0.078125 to 0.078125
- a_query: float32 [2048, 16], replicated, may hold values from -0.125 to 0.125
- b_query: float32 [16, 2048], P(None, 'mp'), may hold values from -0.3 to 0.3
- m_query: float32 [2048], P('mp'), may hold values from 0.5 to 2
- a_key: float32 [2048, 16], replicated, may hold values from -0.125 to 0.125
- b_key: float32 [16, 2048], P(None, 'mp'), may hold values from -0.3 to 0.3
- m_key: float32 [2048], P('mp'), may hold values from 0.5 to 2
- a_value: float32 [2048, 16], replicated, may hold values from -0.125 to 0.125
- b_value: float32 [16, 2048], P(None, 'mp'), may hold values from -0.3 to 0.3
- m_value: float32 [2048], P('mp'), may hold values from 0.5 to 2
- a_out: float32 [2048, 16], P('mp'), may hold values from -0.125 to 0.125
- b_out: float32 [16, 2048], replicated, may hold values from -0.3 to 0.3
- m_out: float32 [2048], replicated, may hold values from 8 to 32
- a_gate: float32 [2048, 16], replicated, may hold values from -0.125 to 0.125
- b_gate: float32 [16, 5632], P(None, 'mp'), may hold values from -0.3 to 0.3
- m_gate: float32 [5632], P('mp'), may hold values from 0.5 to 2
- a_up: float32 [2048, 16], replicated, may hold values from -0.125 to 0.125
- b_up: float32 [16, 5632], P(None, 'mp'), may hold values from -0.3 to 0.3
- m_up: float32 [5632], P('mp'), may hold values from 0.5 to 2
- a_down: float32 [5632, 16], P('mp'), may hold values from -0.078125 to 0.078125
- b_down: float32 [16, 2048], replicated, may hold values from -0.3 to 0.3
- m_down: float32 [2048], replicated, may hold values from 0.5 to 2
Outputs:
- result: float32 [6144, 2048], P(('doc', 'seq', 'mp'))
- grad_input: float32 [6144, 2048], P(('doc', 'seq', 'mp'))
- grad_a_query: float32 [2048, 16], replicated
- grad_b_query: float32 [16, 2048], P(None, 'mp')
- grad_m_query: float32 [2048], P('mp')
- grad_a_key: float32 [2048, 16], replicated
- grad_b_key: float32 [16, 2048], P(None, 'mp')
- grad_m_key: float32 [2048], P('mp')
- grad_a_value: float32 [2048, 16], replicated
- grad_b_value: float32 [16, 2048], P(None, 'mp')
- grad_m_value: float32 [2048], P('mp')
- grad_a_out: float32 [2048, 16], P('mp')
- grad_b_out: float32 [16, 2048], replicated
- grad_m_out: float32 [2048], replicated
- grad_a_gate: float32 [2048, 16], replicated
- grad_b_gate: float32 [16, 5632], P(None, 'mp')
- grad_m_gate: float32 [5632], P('mp')
- grad_a_up: float32 [2048, 16], replicated
- grad_b_up: float32 [16, 5632], P(None, 'mp')
- grad_m_up: float32 [5632], P('mp')
- grad_a_down: float32 [5632, 16], P('mp')
- grad_b_down: float32 [16, 2048], replicated
- grad_m_down: float32 [2048], replicated
The draws below stay inside these ranges and needn't reach their ends.
Inputs may be any that keep to these rules, and one draw needn't show every extreme that they name: `span_order`: each slot holds a different span of its group. `segment_ids`: within each group of 3072 rows, read by positions, document numbers never fall; one document of each group has rows in every span.
All inputs are finite; a program needn't handle non-finite values. No bound on the sum of `padding` on one device may be relied on, other than what follows from the above.
Results may differ from the reference program's by a relative error of at most 0.033.
Values may be sent and summed in bfloat16 or wider, within the bound.
No kernel may reach another device: no remote copies, remote signals or barrier semaphores. Data moves between devices by JAX's collectives and lax.ppermute only.
A program may use at most 448 MiB of HBM per device.

```python
import math
import jax
import jax.numpy as jnp
from jax import lax

D = 2048
HEADS = 16
HD = 128
FF = 5632
RANK = 16
ALPHA = 32
GROUP = 3072
SPAN = 384
TOKENS = 6144
N_DOC = 2
N_SEQ = 4


def shared_order(key):
    return jax.random.permutation(jax.random.fold_in(key, 91), 2 * N_SEQ).astype(jnp.int32)


def draw_span_order(key, part):
    order = shared_order(key)
    return order


def draw_segment_ids(key, part):
    order = shared_order(key)
    key = jax.random.fold_in(key, 5)
    key_head, key_tail, key_first, key_last = jax.random.split(key, 4)
    spread = SPAN // 4
    head_len = jax.random.randint(key_head, (N_DOC, 1), 2, spread + 2)
    tail_len = jax.random.randint(key_tail, (N_DOC, 1), 2, spread + 2)
    first_cut = jax.random.randint(key_first, (N_DOC, 1), 1, head_len + 1)
    last_cut = jax.random.randint(key_last, (N_DOC, 1), GROUP - tail_len + 1, GROUP)
    natural = jnp.arange(GROUP, dtype=jnp.int32)[None, :]
    numbers = (natural >= first_cut).astype(jnp.int32) + (natural >= head_len).astype(jnp.int32) + (natural >= GROUP - tail_len).astype(jnp.int32) + (natural >= last_cut).astype(jnp.int32)
    layout = jnp.arange(GROUP, dtype=jnp.int32)
    source = order[layout // SPAN] * SPAN + layout % SPAN
    return numbers[:, source].reshape(TOKENS).astype(jnp.int32)


def set_ends(array, rng, smallest, top_value):
    longest = array.shape.index(max(array.shape))
    spots = []
    for shift in (0, 1):
        where = [jax.random.randint(jax.random.fold_in(rng, axis), (), 0, length) for axis, length in enumerate(array.shape)]
        where[longest] = (where[longest] + shift) % array.shape[longest]
        spots.append(tuple(where))
    return array.at[spots[0]].set(smallest).at[spots[1]].set(top_value)


def steps_of(rng, shape, cuts, least, high):
    def one(dim, shards_of):
        draws = jax.random.uniform(jax.random.fold_in(jax.random.fold_in(rng, 6), dim), (shards_of,), jnp.float32, least / len(cuts), high / len(cuts))
        return jnp.repeat(jnp.exp(draws), shape[dim] // shards_of).reshape((-1,) + (1,) * (len(shape) - dim - 1))

    loudness = one(*cuts[0])
    for cut in cuts[1:]:
        loudness = loudness * one(*cut)
    return loudness


def noise(own_key, extent, scale, bound, cuts=(), kind=jnp.bfloat16):
    values = scale * jax.random.normal(own_key, extent, jnp.float32)
    if cuts:
        values = values * steps_of(own_key, extent, cuts, -0.22, 0.18)
    return jnp.clip(values, -bound, bound).astype(kind)


def setup_inputs(seed: int = 0) -> dict:
    splits = jax.random.split(jax.random.key(seed), 36)
    return {
        "hidden_in": noise(splits[0], (TOKENS, D), 1.0, 6.0, ((0, 8),)),
        "cotangent": noise(splits[1], (TOKENS, D), 1.0, 6.0, ((0, 8),)),
        "segment_ids": draw_segment_ids(jax.random.fold_in(splits[35], 71), 0),
        "padding": set_ends((jax.random.randint(splits[3], (TOKENS,), 0, 8) < 7).astype(jnp.int32), jax.random.fold_in(splits[3], 1), 0, 1),
        "span_order": draw_span_order(jax.random.fold_in(splits[35], 71), 0),
        "gain_attn": jnp.clip(1.0 + 0.18 * jax.random.normal(splits[5], (D,), jnp.float32), 0.1, 1.9),
        "gain_mlp": jnp.clip(1.0 + 0.18 * jax.random.normal(splits[6], (D,), jnp.float32), 0.1, 1.9),
        "w_query": noise(splits[7], (D, D), D ** -0.5, 0.125, ((1, 4),)),
        "w_key": noise(splits[8], (D, D), D ** -0.5, 0.125, ((1, 4),)),
        "w_value": noise(splits[9], (D, D), D ** -0.5, 0.125, ((1, 4),)),
        "w_out": noise(splits[10], (D, D), D ** -0.5, 0.125, ((0, 4),)),
        "w_gate": noise(splits[11], (D, FF), D ** -0.5, 0.125, ((1, 4),)),
        "w_up": noise(splits[12], (D, FF), D ** -0.5, 0.125, ((1, 4),)),
        "w_down": noise(splits[13], (FF, D), FF ** -0.5, 0.078125, ((0, 4),)),
        "a_query": noise(splits[14], (D, RANK), D ** -0.5, 0.125, (), jnp.float32),
        "b_query": noise(splits[15], (RANK, D), 0.05, 0.3, ((1, 4),), jnp.float32),
        "m_query": jnp.clip(jnp.exp(math.log(2.0) - 1.3862944 * jax.random.uniform(splits[16], (D,), jnp.float32) ** steps_of(splits[16], (D,), ((0, 4),), -0.2, 0.2)), 0.5, 2.0),
        "a_key": noise(splits[17], (D, RANK), D ** -0.5, 0.125, (), jnp.float32),
        "b_key": noise(splits[18], (RANK, D), 0.05, 0.3, ((1, 4),), jnp.float32),
        "m_key": jnp.clip(jnp.exp(math.log(2.0) - 1.3862944 * jax.random.uniform(splits[19], (D,), jnp.float32) ** steps_of(splits[19], (D,), ((0, 4),), -0.2, 0.2)), 0.5, 2.0),
        "a_value": noise(splits[20], (D, RANK), D ** -0.5, 0.125, (), jnp.float32),
        "b_value": noise(splits[21], (RANK, D), 0.05, 0.3, ((1, 4),), jnp.float32),
        "m_value": jnp.clip(jnp.exp(math.log(2.0) - 1.3862944 * jax.random.uniform(splits[22], (D,), jnp.float32) ** steps_of(splits[22], (D,), ((0, 4),), -0.2, 0.2)), 0.5, 2.0),
        "a_out": noise(splits[23], (D, RANK), D ** -0.5, 0.125, ((0, 4),), jnp.float32),
        "b_out": noise(splits[24], (RANK, D), 0.05, 0.3, (), jnp.float32),
        "m_out": jnp.clip(jnp.exp(jax.random.uniform(splits[25], (D,), jnp.float32, math.log(8.0), math.log(32.0))), 8.0, 32.0),
        "a_gate": noise(splits[26], (D, RANK), D ** -0.5, 0.125, (), jnp.float32),
        "b_gate": noise(splits[27], (RANK, FF), 0.05, 0.3, ((1, 4),), jnp.float32),
        "m_gate": jnp.clip(jnp.exp(math.log(2.0) - 1.3862944 * jax.random.uniform(splits[28], (FF,), jnp.float32) ** steps_of(splits[28], (FF,), ((0, 4),), -0.2, 0.2)), 0.5, 2.0),
        "a_up": noise(splits[29], (D, RANK), D ** -0.5, 0.125, (), jnp.float32),
        "b_up": noise(splits[30], (RANK, FF), 0.05, 0.3, ((1, 4),), jnp.float32),
        "m_up": jnp.clip(jnp.exp(math.log(2.0) - 1.3862944 * jax.random.uniform(splits[31], (FF,), jnp.float32) ** steps_of(splits[31], (FF,), ((0, 4),), -0.2, 0.2)), 0.5, 2.0),
        "a_down": noise(splits[32], (FF, RANK), FF ** -0.5, 0.078125, ((0, 4),), jnp.float32),
        "b_down": noise(splits[33], (RANK, D), 0.05, 0.3, (), jnp.float32),
        "m_down": jnp.clip(jnp.exp(jax.random.uniform(splits[34], (D,), jnp.float32, math.log(0.5), math.log(2.0))), 0.5, 2.0),
    }


@jax.custom_vjp
def low(v):
    return lax.optimization_barrier(v.astype(jnp.bfloat16)).astype(jnp.float32)

@jax.custom_vjp
def low_back(v):
    return v

def low_keep(v):
    return (low(v), None)

def low_pass(kept, grad):
    return (grad,)

def back_keep(v):
    return (v, None)

def back_low(kept, grad):
    return (low(grad),)
low.defvjp(low_keep, low_pass)
low_back.defvjp(back_keep, back_low)
eps_norm = 1e-05
rope_base = 10000.0
masked_score = -1e+30

def precise(left, right):
    return jnp.dot(left, right, precision=lax.Precision.HIGHEST, preferred_element_type=jnp.float32)

def rms_forward(values, gain_vec):
    inverse = lax.rsqrt(lax.optimization_barrier(jnp.mean(values * values, axis=-1, keepdims=True)) + eps_norm)
    return values * inverse * gain_vec

def rotary_tables(positions):
    half_dim = HD // 2
    frequency = rope_base ** (-2.0 * jnp.arange(half_dim, dtype=jnp.float32) / HD)
    angles = positions.astype(jnp.float32)[:, None] * frequency[None, :]
    cosine = jnp.concatenate([jnp.cos(angles), jnp.cos(angles)], axis=1)
    sine_table = jnp.concatenate([jnp.sin(angles), jnp.sin(angles)], axis=1)
    return (cosine[:, None, :], sine_table[:, None, :])

def apply_rotary(values, cosine, sine_table):
    half_dim = values.shape[-1] // 2
    turned = jnp.concatenate([-values[..., half_dim:], values[..., :half_dim]], axis=-1)
    return values * cosine + turned * sine_table

def dora_apply(inputs, base_weight, down_factor, up_factor, magnitude):
    merged = base_weight + ALPHA / RANK * precise(down_factor, up_factor)
    column = jnp.sqrt(lax.optimization_barrier(jnp.sum(merged * merged, axis=0)))
    raw_value = low_back(precise(inputs, low(merged)))
    return raw_value * (magnitude / column)

def head_attention(item):
    query_rows, key_rows, value_rows, segment_row, padding_row, position_row = item
    scores = low_back(precise(query_rows, key_rows.T) * HD ** (-0.5))
    same_doc = segment_row[:, None] == segment_row[None, :]
    causal = position_row[None, :] <= position_row[:, None]
    itself = position_row[None, :] == position_row[:, None]
    allowed = same_doc & causal & ((padding_row[None, :] == 1) | itself)
    masked = jnp.where(allowed, scores, masked_score)
    peak_score = lax.optimization_barrier(jnp.max(masked, axis=1, keepdims=True))
    weights = jnp.where(allowed, jnp.exp(masked - peak_score), 0.0)
    probs = weights / lax.optimization_barrier(jnp.sum(weights, axis=1, keepdims=True))
    return precise(low(probs), value_rows)

def attention_all(query_all, key_all, value_all, segment_ids, padding, positions):

    def regroup(values):
        shaped = values.reshape(N_DOC, GROUP, HEADS, HD)
        return jnp.transpose(shaped, (0, 2, 1, 3)).reshape(N_DOC * HEADS, GROUP, HD)
    segment_items = jnp.repeat(segment_ids.reshape(N_DOC, GROUP), HEADS, axis=0)
    padding_items = jnp.repeat(padding.reshape(N_DOC, GROUP), HEADS, axis=0)
    position_items = jnp.repeat(positions.reshape(N_DOC, GROUP), HEADS, axis=0)
    outputs = lax.map(jax.checkpoint(head_attention), (regroup(query_all), regroup(key_all), regroup(value_all), segment_items, padding_items, position_items))
    shaped = outputs.reshape(N_DOC, HEADS, GROUP, HD)
    return jnp.transpose(shaped, (0, 2, 1, 3)).reshape(TOKENS, D)

def reference(hidden_in, cotangent, segment_ids, padding, span_order, gain_attn, gain_mlp, w_query, w_key, w_value, w_out, w_gate, w_up, w_down, a_query, b_query, m_query, a_key, b_key, m_key, a_value, b_value, m_value, a_out, b_out, m_out, a_gate, b_gate, m_gate, a_up, b_up, m_up, a_down, b_down, m_down):
    row_ids = jnp.arange(TOKENS, dtype=jnp.int32) % GROUP
    positions = span_order[row_ids // SPAN] * SPAN + row_ids % SPAN
    cosine, sine_table = rotary_tables(positions)
    base_query = w_query.astype(jnp.float32)
    base_key = w_key.astype(jnp.float32)
    base_value = w_value.astype(jnp.float32)
    base_out = w_out.astype(jnp.float32)
    base_gate = w_gate.astype(jnp.float32)
    base_up = w_up.astype(jnp.float32)
    base_down = w_down.astype(jnp.float32)

    def forward(hidden, adapters):
        aq, bq, mq, ak, bk, mk, av, bv, mv, ao, bo, mo, ag, bg, mg, au, bu, mu, ad, bd, md = adapters
        normed = low(rms_forward(hidden, gain_attn))
        query_all = low(apply_rotary(dora_apply(normed, base_query, aq, bq, mq).reshape(TOKENS, HEADS, HD), cosine, sine_table))
        key_all = low(apply_rotary(dora_apply(normed, base_key, ak, bk, mk).reshape(TOKENS, HEADS, HD), cosine, sine_table))
        value_all = low(dora_apply(normed, base_value, av, bv, mv)).reshape(TOKENS, HEADS, HD)
        attended = attention_all(query_all, key_all, value_all, segment_ids, padding, positions)
        attn_low = low(low_back(attended))
        resid = hidden + dora_apply(attn_low, base_out, ao, bo, mo)
        hnorm = low(rms_forward(resid, gain_mlp))
        gate_value = dora_apply(hnorm, base_gate, ag, bg, mg)
        up_value = dora_apply(hnorm, base_up, au, bu, mu)
        act_low = low(jax.nn.silu(gate_value) * up_value)
        return resid + dora_apply(act_low, base_down, ad, bd, md)
    adapters = (a_query, b_query, m_query, a_key, b_key, m_key, a_value, b_value, m_value, a_out, b_out, m_out, a_gate, b_gate, m_gate, a_up, b_up, m_up, a_down, b_down, m_down)
    result, pullback = jax.vjp(forward, hidden_in.astype(jnp.float32), adapters)
    grad_input, grads = pullback(cotangent.astype(jnp.float32))
    return (result, grad_input, grads[0], grads[1], grads[2], grads[3], grads[4], grads[5], grads[6], grads[7], grads[8], grads[9], grads[10], grads[11], grads[12], grads[13], grads[14], grads[15], grads[16], grads[17], grads[18], grads[19], grads[20])
```

```python
import functools
import math

import jax
import jax.numpy as jnp
import numpy as np
from jax import lax
from jax.experimental import pallas as pl
from jax.experimental.pallas import tpu as pltpu
from jax.sharding import PartitionSpec as P

HD = 128
RANK = 16
ALPHA = 32
HALF = HD // 2
SCALING = ALPHA / RANK
INV_ROOT = HD ** (-0.5)
EPS = 1e-05
ROPE_BASE = 10000.0
MASKED = -1e30
CHUNKS = 2
MIB = 1 << 20
VMEM_LIMIT = 56 * MIB

f32 = jnp.float32
bf16 = jnp.bfloat16


def dot(left, right):
    return jnp.dot(left, right, preferred_element_type=f32)


def dot_nt(left, right):
    return lax.dot_general(left, right, (((1,), (1,)), ((), ())), preferred_element_type=f32)


def dot_tn(left, right):
    return lax.dot_general(left, right, (((0,), (0,)), ((), ())), preferred_element_type=f32)


def whole_spec(array):
    rank = len(array.shape)
    return pl.BlockSpec(tuple(array.shape), lambda *_: (0,) * rank)


def cost(flops, moved):
    return pl.CostEstimate(flops=flops, bytes_accessed=moved, transcendentals=0)


def swap(value, axis, distance):
    size = lax.axis_size(axis)
    return lax.ppermute(value, axis, [(i, i ^ distance) for i in range(size)])


def butterfly(value, axes):
    for axis in axes:
        distance = 1
        while distance < lax.axis_size(axis):
            value = lax.optimization_barrier(value + swap(value, axis, distance))
            distance *= 2
    return value


def doc_halve(value):
    doc = lax.axis_index("doc")
    half = value.shape[0] // 2
    mine = lax.dynamic_slice_in_dim(value, doc * half, half, 0)
    other = lax.dynamic_slice_in_dim(value, (1 - doc) * half, half, 0)
    return lax.optimization_barrier(mine + swap(other, "doc", 1))


def doc_join(mine):
    doc = lax.axis_index("doc")
    other = swap(mine, "doc", 1)
    first = jnp.where(doc == 0, mine, other)
    second = jnp.where(doc == 0, other, mine)
    return jnp.concatenate([first, second], axis=0)


def spread_sum(value, peers, axes):
    me = lax.rem(lax.axis_index("seq"), peers)
    parts = value.reshape(peers, -1, value.shape[-1])
    piece = lambda index: lax.dynamic_index_in_dim(parts, index, 0, keepdims=False)
    mine = piece(me).astype(f32)
    for d in range(1, peers):
        mine = mine + swap(piece(me ^ d), "seq", d).astype(f32)
    mine = lax.optimization_barrier(mine.astype(bf16))
    distance = peers
    while distance < lax.axis_size("seq"):
        mine = lax.optimization_barrier(mine + swap(mine, "seq", distance))
        distance *= 2
    return butterfly(mine, axes)


def spread_join(mine, peers):
    me = lax.rem(lax.axis_index("seq"), peers)
    found = [mine] + [swap(mine, "seq", d) for d in range(1, peers)]
    return jnp.concatenate([pick_blocks(found, me ^ i) for i in range(peers)], axis=0)


def after(values, *earlier):
    tied = lax.optimization_barrier((tuple(values), earlier))
    return tied[0]


def line_step(rights, lefts, step, *earlier):
    size = lax.axis_size("mp")
    right, left = rights[-1], lefts[-1]
    if earlier:
        right, left = after([right, left], *earlier)
    right_pairs = [(i, i + 1) for i in range(step - 1, size - 1)]
    left_pairs = [(i, i - 1) for i in range(1, size - step + 1)]
    rights.append(lax.ppermute(right, "mp", right_pairs))
    lefts.append(lax.ppermute(left, "mp", left_pairs))


def line_blocks(rights, lefts):
    size = lax.axis_size("mp")
    k = lax.axis_index("mp")
    return [rights[0]] + [
        jnp.where(k + c < size, lefts[c], rights[size - c]) for c in range(1, size)
    ]


def seq_exchange(blocks):
    return [blocks[0]] + [swap(blocks[d], "seq", d) for d in range(1, len(blocks))]


def key_marks(code):
    lane = lax.broadcasted_iota(jnp.int32, (code.shape[0], HD), 1)
    segment, real = code >> 1, code & 1
    wrong = (lane < 16) & (lane != segment)
    absent = (lane == 16) & (real == 0)
    return jnp.where(wrong | absent, MASKED, 0.0).astype(bf16)


def query_marks(code):
    lane = lax.broadcasted_iota(jnp.int32, (code.shape[0], HD), 1)
    segment = code >> 1
    return jnp.where((lane == segment) | (lane == 16), 1.0, 0.0).astype(bf16)


def diagonal_scores(keys, query):
    marked = dot_nt(keys, query)
    plain = dot_nt(keys[:, :HD], query[:, :HD])
    key_id = lax.broadcasted_iota(jnp.int32, marked.shape, 0)
    query_id = lax.broadcasted_iota(jnp.int32, marked.shape, 1)
    return jnp.where(
        key_id < query_id, marked, jnp.where(key_id == query_id, plain, MASKED)
    )


def block_readers(groups, heads, kv_refs, code_refs):
    if groups == 1:
        return (
            lambda g, d, rows: heads[d][0, rows, :],
            lambda g, d, rows: heads[d][1, rows, :],
            lambda g, d, rows: code_refs[d][rows, :],
        )
    return (
        lambda g, d, rows: kv_refs[0][g, d, 0, rows, :],
        lambda g, d, rows: kv_refs[0][g, d, 1, rows, :],
        lambda g, d, rows: kv_refs[1][g, d, rows, :],
    )


def taker(refs):
    refs = list(refs)

    def take(count):
        taken = refs[:count]
        del refs[:count]
        return taken

    return take


def forward_kernel(meta, scalars, *refs):
    peers, groups, span, pieces, chunks, n_extra = meta
    take = taker(refs)
    heads, code_refs, kv_refs = take(peers), take(peers), take(n_extra)
    o_refs, (lse_ref,) = take(peers), take(1)
    q_all, o_all, k_all, v_turned = take(4)
    key_of, value_of, key_code_of = block_readers(groups, heads, kv_refs, code_refs)
    n_query = 2 * peers

    for g in range(groups):
        for d in range(peers):
            for half in range(2):
                rows = pl.ds(half * span, span)
                place = scalars[n_query + (g * peers + d) * 2 + half]
                at = pl.ds(pl.multiple_of(place * span, HD), span)
                k_all[at, :HD] = key_of(g, d, rows)
                k_all[at, HD:] = key_marks(key_code_of(g, d, rows))
                v_turned[:, at] = value_of(g, d, rows).astype(f32).T.astype(bf16)
    for d in range(peers):
        for half in range(2):
            rows = pl.ds(half * span, span)
            q_all[2 * d + half, :, :HD] = heads[d][2, rows, :]
            q_all[2 * d + half, :, HD:] = query_marks(code_refs[d][rows, :])

    def one_span(i, carry):
        place = scalars[i]
        query = q_all[i]
        at = pl.ds(pl.multiple_of(place * span, HD), span)
        scores = diagonal_scores(k_all[at, :], query)
        peak = jnp.max(scores, axis=0, keepdims=True)
        weights = jnp.exp((scores - peak) * INV_ROOT)
        total = jnp.sum(weights, axis=0, keepdims=True)
        out = dot(v_turned[:, at], weights.astype(bf16))

        def key_span(j, state):
            peak, total, out = state
            at = pl.ds(pl.multiple_of(j * span, HD), span)
            scores = dot_nt(k_all[at, :], query)
            new_peak = jnp.maximum(peak, jnp.max(scores, axis=0, keepdims=True))
            fade = jnp.exp((peak - new_peak) * INV_ROOT)
            weights = jnp.exp((scores - new_peak) * INV_ROOT)
            total = total * fade + jnp.sum(weights, axis=0, keepdims=True)
            out = out * fade + dot(v_turned[:, at], weights.astype(bf16))
            return (new_peak, total, out)

        peak, total, out = lax.fori_loop(0, place, key_span, (peak, total, out))
        lse_ref[i] = peak * INV_ROOT + jnp.log(total)
        o_all[i] = (out / total).T.astype(bf16)
        return carry

    lax.fori_loop(0, n_query, one_span, 0)
    share = 2 * span // pieces
    part = share // chunks
    for d in range(peers):
        for piece in range(pieces):
            for c in range(chunks):
                row = piece * share + c * part
                to = (c * pieces + piece) * part
                o_refs[d][to : to + part, :] = o_all[
                    2 * d + row // span, row % span : row % span + part, :
                ]


def attention_forward(scalars, heads, codes, extra, groups, pieces, chunks):
    peers = len(heads)
    rows = heads[0].shape[1]
    span = rows // 2
    key_rows = groups * peers * rows
    meta = (peers, groups, span, pieces, chunks, len(extra))
    operands = [*heads, *codes, *extra]
    out_shape = [jax.ShapeDtypeStruct((rows, HD), bf16)] * peers
    out_shape.append(jax.ShapeDtypeStruct((2 * peers, 1, span), f32))
    outs = pl.pallas_call(
        functools.partial(forward_kernel, meta),
        grid_spec=pltpu.PrefetchScalarGridSpec(
            num_scalar_prefetch=1,
            grid=(1,),
            in_specs=[whole_spec(x) for x in operands],
            out_specs=[whole_spec(x) for x in out_shape],
            scratch_shapes=[
                pltpu.VMEM((2 * peers, span, 2 * HD), bf16),
                pltpu.VMEM((2 * peers, span, HD), bf16),
                pltpu.VMEM((key_rows, 2 * HD), bf16),
                pltpu.VMEM((HD, key_rows), bf16),
            ],
        ),
        out_shape=out_shape,
        compiler_params=pltpu.CompilerParams(vmem_limit_bytes=VMEM_LIMIT),
        cost_estimate=cost(6 * peers * rows * key_rows // 2 * HD, 8 * key_rows * HD),
        name="attend",
    )(scalars, *operands)
    return outs[:-1], outs[-1]


def backward_kernel(meta, scalars, *refs):
    peers, groups, span, pieces, chunks, n_extra = meta
    take = taker(refs)
    heads, code_refs, kv_refs = take(peers), take(peers), take(n_extra)
    o_refs, do_refs, (lse_ref,) = take(peers), take(peers), take(1)
    grad_refs = take(peers)
    dkv_refs = take(1 if groups > 1 else 0)
    q_all, o_all, do_all, k_all, k_turned, v_all, dk_all, dv_all = take(8)
    key_of, value_of, key_code_of = block_readers(groups, heads, kv_refs, code_refs)
    n_query = 2 * peers
    own_piece = scalars[n_query + 2 * groups * peers]

    for g in range(groups):
        for d in range(peers):
            for half in range(2):
                rows = pl.ds(half * span, span)
                place = scalars[n_query + (g * peers + d) * 2 + half]
                at = pl.ds(pl.multiple_of(place * span, HD), span)
                key = key_of(g, d, rows)
                k_all[at, :HD] = key
                k_all[at, HD:] = key_marks(key_code_of(g, d, rows))
                k_turned[:, at] = key.astype(f32).T.astype(bf16)
                v_all[at, :] = value_of(g, d, rows)
    dk_all[...] = jnp.zeros_like(dk_all)
    dv_all[...] = jnp.zeros_like(dv_all)
    share = 2 * span // pieces
    part = share // chunks
    for d in range(peers):
        for half in range(2):
            rows = pl.ds(half * span, span)
            q_all[2 * d + half, :, :HD] = heads[d][2, rows, :]
            q_all[2 * d + half, :, HD:] = query_marks(code_refs[d][rows, :])
        for piece in range(pieces):
            origin = lax.rem(own_piece + pieces - piece, pieces)
            for c in range(chunks):
                source = pl.ds((c * pieces + piece) * part, part)
                row = (2 * d * span) + piece * share + c * part
                o_all[row : row + part, :] = o_refs[d][source, :]
                row = (2 * d * span) + origin * share + c * part
                do_all[pl.ds(pl.multiple_of(row, 16), part), :] = do_refs[d][source, :]

    def one_span(i, carry):
        place = scalars[i]
        query = q_all[i]
        rows = pl.ds(pl.multiple_of(i * span, HD), span)
        grad = do_all[rows, :]
        product = grad.astype(f32) * o_all[rows, :].astype(f32)
        high = product.astype(bf16)
        rest = (product - high.astype(f32)).astype(bf16)
        ones = jnp.ones((16, HD), bf16)
        delta = (dot_nt(ones, high) + dot_nt(ones, rest))[:1, :]
        lse = lse_ref[i]

        def key_span(at, scores, dq_turned):
            probs = jnp.exp(scores * INV_ROOT - lse)
            grad_prob = dot_nt(v_all[at, :], grad)
            grad_score = (probs * (grad_prob - delta)).astype(bf16)
            dv_all[at, :] += dot(probs.astype(bf16), grad)
            dk_all[at, :] += dot(grad_score, query[:, :HD])
            return dq_turned + dot(k_turned[:, at], grad_score)

        at = pl.ds(pl.multiple_of(place * span, HD), span)
        dq_turned = key_span(
            at, diagonal_scores(k_all[at, :], query), jnp.zeros((HD, span), f32)
        )

        def step(j, dq_turned):
            at = pl.ds(pl.multiple_of(j * span, HD), span)
            return key_span(at, dot_nt(k_all[at, :], query), dq_turned)

        dq_turned = lax.fori_loop(0, place, step, dq_turned)
        o_all[rows, :] = (dq_turned * INV_ROOT).T.astype(bf16)
        return carry

    lax.fori_loop(0, n_query, one_span, 0)
    at_query = 2 if groups == 1 else 0
    for d in range(peers):
        grad_refs[d][at_query] = o_all[2 * d * span : 2 * (d + 1) * span, :]
    for g in range(groups):
        for d in range(peers):
            for half in range(2):
                rows = pl.ds(half * span, span)
                place = scalars[n_query + (g * peers + d) * 2 + half]
                at = pl.ds(pl.multiple_of(place * span, HD), span)
                grad_key = (dk_all[at, :] * INV_ROOT).astype(bf16)
                grad_value = dv_all[at, :].astype(bf16)
                if groups == 1:
                    grad_refs[d][0, rows, :] = grad_key
                    grad_refs[d][1, rows, :] = grad_value
                else:
                    dkv_refs[0][g, d, 0, rows, :] = grad_key
                    dkv_refs[0][g, d, 1, rows, :] = grad_value


def attention_backward(scalars, heads, codes, extra, o, grads, lse, groups, pieces, chunks):
    peers = len(heads)
    rows = heads[0].shape[1]
    span = rows // 2
    key_rows = groups * peers * rows
    meta = (peers, groups, span, pieces, chunks, len(extra))
    operands = [*heads, *codes, *extra, *o, *grads, lse]
    parts = 3 if groups == 1 else 1
    out_shape = [jax.ShapeDtypeStruct((parts, rows, HD), bf16)] * peers
    if groups > 1:
        out_shape.append(jax.ShapeDtypeStruct(extra[0].shape, bf16))
    outs = pl.pallas_call(
        functools.partial(backward_kernel, meta),
        grid_spec=pltpu.PrefetchScalarGridSpec(
            num_scalar_prefetch=1,
            grid=(1,),
            in_specs=[whole_spec(x) for x in operands],
            out_specs=[whole_spec(x) for x in out_shape],
            scratch_shapes=[
                pltpu.VMEM((2 * peers, span, 2 * HD), bf16),
                pltpu.VMEM((peers * rows, HD), bf16),
                pltpu.VMEM((peers * rows, HD), bf16),
                pltpu.VMEM((key_rows, 2 * HD), bf16),
                pltpu.VMEM((HD, key_rows), bf16),
                pltpu.VMEM((key_rows, HD), bf16),
                pltpu.VMEM((key_rows, HD), f32),
                pltpu.VMEM((key_rows, HD), f32),
            ],
        ),
        out_shape=out_shape,
        compiler_params=pltpu.CompilerParams(vmem_limit_bytes=VMEM_LIMIT),
        cost_estimate=cost(14 * peers * rows * key_rows // 2 * HD, 16 * key_rows * HD),
        name="attend_back",
    )(scalars, *operands)
    if groups == 1:
        return outs, None
    return outs[:peers], outs[peers]


def split_low(value):
    high = value.astype(bf16)
    return high, (value - high.astype(f32)).astype(bf16)


def low_rank(a_t, b):
    a_high, a_rest = split_low(a_t)
    b_high, b_rest = split_low(b * SCALING)
    a_cat = jnp.concatenate([a_high, a_rest, a_high], axis=0)
    b_cat = jnp.concatenate([b_high, b_high, b_rest], axis=0)
    return dot_tn(a_cat, b_cat)


def columns_kernel(keep, w_ref, a_ref, b_ref, *outs):
    merged = w_ref[...].astype(f32) + low_rank(a_ref[...], b_ref[...])
    low = merged.astype(bf16)
    if keep:
        outs[2][...] = low
    outs[0][...] = jnp.sum(merged * merged, axis=0, keepdims=True)
    outs[1][...] = dot(a_ref[...].astype(bf16), low)


def merge_columns(w, a_t, b, keep):
    depth, width = w.shape
    step = 2 * HD
    out_specs = [
        pl.BlockSpec((1, step), lambda i: (0, i)),
        pl.BlockSpec((RANK, step), lambda i: (0, i)),
    ]
    out_shape = [
        jax.ShapeDtypeStruct((1, width), f32),
        jax.ShapeDtypeStruct((RANK, width), f32),
    ]
    if keep:
        out_specs.append(pl.BlockSpec((depth, step), lambda i: (0, i)))
        out_shape.append(jax.ShapeDtypeStruct((depth, width), bf16))
    return pl.pallas_call(
        functools.partial(columns_kernel, keep),
        grid=(width // step,),
        in_specs=[
            pl.BlockSpec((depth, step), lambda i: (0, i)),
            pl.BlockSpec((RANK, depth), lambda i: (0, 0)),
            pl.BlockSpec((RANK, step), lambda i: (0, i)),
        ],
        out_specs=out_specs,
        out_shape=out_shape,
        compiler_params=pltpu.CompilerParams(vmem_limit_bytes=VMEM_LIMIT),
        cost_estimate=cost(2 * depth * width * RANK, 2 * depth * width),
        name="merge_columns",
    )(w, a_t, b)


def interleave(gate, up):
    rows, width = gate.shape
    both = jnp.stack([gate.reshape(rows, -1, HD), up.reshape(rows, -1, HD)], axis=2)
    return both.reshape(rows, 2 * width)


def separate(both):
    rows, width = both.shape
    both = both.reshape(rows, -1, 2, HD)
    return both[:, :, 0].reshape(rows, width // 2), both[:, :, 1].reshape(rows, width // 2)


def pair_kernel(gate_ref, up_ref, a_ref, b_ref, low_ref, square_ref, cross_ref):
    width = gate_ref.shape[1]

    @pl.when(pl.program_id(0) == 0)
    def _():
        square_ref[...] = jnp.zeros_like(square_ref)
        cross_ref[...] = jnp.zeros_like(cross_ref)

    for side, w_ref in enumerate((gate_ref, up_ref)):
        a_t = a_ref[side * RANK : (side + 1) * RANK, :]
        b = b_ref[:, side * width : (side + 1) * width]
        merged = w_ref[...].astype(f32) + low_rank(a_t, b)
        low = merged.astype(bf16)
        square = jnp.sum(merged * merged, axis=0, keepdims=True)
        cross = dot(a_t.astype(bf16), low)
        for j in range(width // HD):
            at = pl.ds((2 * j + side) * HD, HD)
            source = slice(j * HD, (j + 1) * HD)
            low_ref[:, at] = low[:, source]
            square_ref[:, at] += square[:, source]
            cross_ref[:, at] += cross[:, source]


def merge_pair(w_gate, w_up, a_t, b):
    depth, width = w_gate.shape
    rows = 2 * HD
    return pl.pallas_call(
        pair_kernel,
        grid=(depth // rows,),
        in_specs=[
            pl.BlockSpec((rows, width), lambda i: (i, 0)),
            pl.BlockSpec((rows, width), lambda i: (i, 0)),
            pl.BlockSpec((2 * RANK, rows), lambda i: (0, i)),
            pl.BlockSpec((RANK, 2 * width), lambda i: (0, 0)),
        ],
        out_specs=[
            pl.BlockSpec((rows, 2 * width), lambda i: (i, 0)),
            pl.BlockSpec((1, 2 * width), lambda i: (0, 0)),
            pl.BlockSpec((RANK, 2 * width), lambda i: (0, 0)),
        ],
        out_shape=[
            jax.ShapeDtypeStruct((depth, 2 * width), bf16),
            jax.ShapeDtypeStruct((1, 2 * width), f32),
            jax.ShapeDtypeStruct((RANK, 2 * width), f32),
        ],
        compiler_params=pltpu.CompilerParams(vmem_limit_bytes=VMEM_LIMIT),
        cost_estimate=cost(4 * depth * width * RANK, 8 * depth * width),
        name="merge_pair",
    )(w_gate, w_up, a_t, b)


def heads_kernel(scalars, x_ref, gain_ref, wk_ref, wv_ref, wq_ref, a_ref, b_ref, m_ref,
                 cos_ref, sin_ref, *refs):
    take = taker(refs)
    peers = len(refs) - 9
    blocks = take(peers)
    normed_ref, low_ref, raw_ref, column_ref, scale_ref, cross_ref = take(6)
    x_all, w_now, merged_now = take(3)
    step_id = pl.program_id(0)
    rows = x_ref.shape[0]
    per_step = w_now.shape[1] // HD
    steps = peers // per_step
    layer = step_id // steps

    @pl.when(step_id == 0)
    def _():
        part = rows // 4
        for i in range(4):
            at = pl.ds(i * part, part)
            x = x_ref[at, :].astype(f32)
            inverse = lax.rsqrt(jnp.mean(x * x, axis=-1, keepdims=True) + EPS)
            normed = (x * inverse * gain_ref[...]).astype(bf16)
            x_all[at, :] = normed
            normed_ref[at, :] = normed

    for number, w_ref in enumerate((wk_ref, wv_ref, wq_ref)):

        @pl.when(layer == number)
        def _(w_ref=w_ref):
            w_now[...] = w_ref[...]

    a_t = a_ref[0]
    x_all[rows:, :] = a_t.astype(bf16)
    merged = w_now[...].astype(f32) + low_rank(a_t, b_ref[...])
    low = merged.astype(bf16)
    merged_now[...] = low
    low_ref[...] = low
    column = jnp.sqrt(jnp.sum(merged * merged, axis=0, keepdims=True))
    scale = m_ref[...] / column
    column_ref[...] = column
    scale_ref[...] = scale
    product = dot(x_all[...], merged_now[...])
    cross_ref[...] = product[rows:, :]
    raw = product[:rows, :]
    raw_ref[...] = raw.astype(bf16)
    value = raw * scale
    turned = layer != 1
    for t in range(per_step):
        head = value[:, t * HD : (t + 1) * HD]
        rotated = head * cos_ref[...] + pltpu.roll(head, HALF, 1) * sin_ref[...]
        head = jnp.where(turned, rotated, head).astype(bf16)
        place = ((step_id % steps) * per_step + t) ^ scalars[0]
        for d, block in enumerate(blocks):

            @pl.when(place == d)
            def _(block=block, head=head):
                block[layer] = head


def project_heads(order, x, gain, weights, a_t, b, m, cosine, sine):
    rows, depth = x.shape
    width = weights[0].shape[1]
    heads = width // HD
    step = 2 * HD
    steps = width // step

    def weight_spec(layer):
        return pl.BlockSpec(
            (depth, step), lambda i, s: (0, jnp.clip(i - layer * steps, 0, steps - 1))
        )

    columns = lambda height: pl.BlockSpec((height, step), lambda i, s: (0, i))
    fixed = lambda *shape: pl.BlockSpec(shape, lambda i, s: (0,) * len(shape))
    out_shape = [jax.ShapeDtypeStruct((3, rows, HD), bf16)] * heads
    out_shape += [
        jax.ShapeDtypeStruct((rows, depth), bf16),
        jax.ShapeDtypeStruct((depth, 3 * width), bf16),
        jax.ShapeDtypeStruct((rows, 3 * width), bf16),
        jax.ShapeDtypeStruct((1, 3 * width), f32),
        jax.ShapeDtypeStruct((1, 3 * width), f32),
        jax.ShapeDtypeStruct((RANK, 3 * width), f32),
    ]
    outs = pl.pallas_call(
        heads_kernel,
        grid_spec=pltpu.PrefetchScalarGridSpec(
            num_scalar_prefetch=1,
            grid=(3 * steps,),
            in_specs=[
                fixed(rows, depth),
                fixed(1, depth),
                weight_spec(0),
                weight_spec(1),
                weight_spec(2),
                pl.BlockSpec((1, RANK, depth), lambda i, s: (i // steps, 0, 0)),
                columns(RANK),
                columns(1),
                fixed(rows, HD),
                fixed(rows, HD),
            ],
            out_specs=[fixed(3, rows, HD)] * heads
            + [
                fixed(rows, depth),
                columns(depth),
                columns(rows),
                columns(1),
                columns(1),
                columns(RANK),
            ],
            scratch_shapes=[
                pltpu.VMEM((rows + RANK, depth), bf16),
                pltpu.VMEM((depth, step), bf16),
                pltpu.VMEM((depth, step), bf16),
            ],
        ),
        out_shape=out_shape,
        compiler_params=pltpu.CompilerParams(vmem_limit_bytes=VMEM_LIMIT),
        cost_estimate=cost(6 * rows * depth * width, 16 * rows * depth),
        name="project_heads",
    )(order, x, gain, *weights, a_t, b, m, cosine, sine)
    return outs[:heads], *outs[heads:]


def out_kernel(scalars, *refs):
    take = taker(refs)
    size = len(refs) - 13
    x_refs = take(size)
    w_ref, a_ref, hid_ref, b_ref, scale_ref, gain_ref = take(6)
    hnorm_ref, resid_ref, raw_own_ref, low_ref = take(4)
    total, through, resid_all = take(3)
    step = pl.program_id(0)

    @pl.when(step == 0)
    def _():
        total[...] = jnp.zeros_like(total)
        through[...] = jnp.zeros_like(through)

    for c, x_ref in enumerate(x_refs):

        @pl.when(step == c)
        def _(x_ref=x_ref):
            x = x_ref[...]
            total[...] += dot(x, w_ref[...])
            through[...] += dot_nt(x, a_ref[...])

    @pl.when(step == size - 1)
    def _():
        part = hid_ref.shape[2]
        for piece in range(size):
            at = pl.ds(piece * part, part)
            low = through[at, :].astype(bf16)
            raw = total[at, :] + dot(low, b_ref[...])
            resid = hid_ref[piece, 0].astype(f32) + raw * scale_ref[...]
            inverse = lax.rsqrt(jnp.mean(resid * resid, axis=-1, keepdims=True) + EPS)
            hnorm_ref[at, :] = (resid * inverse * gain_ref[...]).astype(bf16)

            @pl.when(scalars[0] == piece)
            def _(resid=resid, raw=raw, low=low):
                resid_ref[...] = resid
                raw_own_ref[...] = raw
                low_ref[...] = low


def out_project(k, chunk, x, w, a_t, hidden, b2, scale, gain):
    size = len(x)
    rows, width = x[0].shape
    wide = w.shape[1]
    part = rows // size
    fixed = lambda *shape: pl.BlockSpec(shape, lambda i, s: (0,) * len(shape))
    return pl.pallas_call(
        out_kernel,
        grid_spec=pltpu.PrefetchScalarGridSpec(
            num_scalar_prefetch=1,
            grid=(size,),
            in_specs=[fixed(rows, width)] * size
            + [
                pl.BlockSpec((width, wide), lambda i, s: (lax.rem(i + s[0], size), 0)),
                pl.BlockSpec((RANK, width), lambda i, s: (0, lax.rem(i + s[0], size))),
                pl.BlockSpec((size, 1, part, wide), lambda i, s: (0, chunk, 0, 0)),
                fixed(RANK, wide),
                fixed(1, wide),
                fixed(1, wide),
            ],
            out_specs=[
                fixed(rows, wide),
                fixed(part, wide),
                fixed(part, wide),
                fixed(part, RANK),
            ],
            scratch_shapes=[
                pltpu.VMEM((rows, wide), f32),
                pltpu.VMEM((rows, RANK), f32),
                pltpu.VMEM((8, HD), f32),
            ],
        ),
        out_shape=[
            jax.ShapeDtypeStruct((rows, wide), bf16),
            jax.ShapeDtypeStruct((part, wide), f32),
            jax.ShapeDtypeStruct((part, wide), f32),
            jax.ShapeDtypeStruct((part, RANK), bf16),
        ],
        compiler_params=pltpu.CompilerParams(vmem_limit_bytes=VMEM_LIMIT),
        cost_estimate=cost(2 * rows * width * size * wide, 2 * width * size * wide),
        name="out_project",
    )(k, *x, w, a_t, hidden, b2, scale, gain)


def hidden_kernel(hnorm_ref, w_ref, dact_ref, scale_ref, act_ref, dz_ref, g_ref, dh_ref,
                  total, w_kept, dz_kept):
    step = pl.program_id(0)
    now, before = lax.rem(step, 2), lax.rem(step + 1, 2)

    @pl.when(step == 0)
    def _():
        total[...] = jnp.zeros_like(total)
        w_kept[1] = jnp.zeros_like(w_kept[1])
        dz_kept[1] = jnp.zeros_like(dz_kept[1])

    rows = hnorm_ref.shape[0]
    w = w_ref[...]
    w_kept[now] = w
    v = dot(hnorm_ref[...], w)
    total[...] += dot_nt(dz_kept[before], w_kept[before])
    raw_gate, raw_up = v[:, :HD], v[:, HD:]
    scale_gate, scale_up = scale_ref[:, :HD], scale_ref[:, HD:]
    gate = raw_gate * scale_gate
    up = raw_up * scale_up
    sigmoid = 1.0 / (1.0 + jnp.exp(-gate))
    silu = gate * sigmoid
    dact = dact_ref[...].reshape(rows, HD).astype(f32)
    dgate = dact * up * (sigmoid + silu * (1.0 - sigmoid))
    dup = dact * silu
    act_ref[...] = (silu * up).astype(bf16)
    g_ref[:, :HD] = jnp.sum(dgate * raw_gate, axis=0, keepdims=True)
    g_ref[:, HD:] = jnp.sum(dup * raw_up, axis=0, keepdims=True)
    dz_gate = (dgate * scale_gate).astype(bf16)
    dz_up = (dup * scale_up).astype(bf16)
    dz_ref[:, :HD] = dz_gate
    dz_ref[:, HD:] = dz_up
    dz_kept[now, :, :HD] = dz_gate
    dz_kept[now, :, HD:] = dz_up

    @pl.when(step == pl.num_programs(0) - 1)
    def _():
        dh_ref[...] = total[...].astype(bf16)


def feed_forward(chunk, hnorm, w, dact, scale):
    rows, depth = hnorm.shape
    both = w.shape[1]
    blocks = both // (2 * HD)
    size, _, part, _ = dact.shape
    block = lambda i: jnp.minimum(i, blocks - 1)
    columns = lambda height, wide: pl.BlockSpec((height, wide), lambda i: (0, block(i)))
    return pl.pallas_call(
        hidden_kernel,
        grid=(blocks + 1,),
        in_specs=[
            pl.BlockSpec((rows, depth), lambda i: (0, 0)),
            columns(depth, 2 * HD),
            pl.BlockSpec((size, 1, part, HD), lambda i: (0, chunk, 0, block(i))),
            columns(1, 2 * HD),
        ],
        out_specs=[
            columns(rows, HD),
            columns(rows, 2 * HD),
            columns(1, 2 * HD),
            pl.BlockSpec((rows, depth), lambda i: (0, 0)),
        ],
        out_shape=[
            jax.ShapeDtypeStruct((rows, both // 2), bf16),
            jax.ShapeDtypeStruct((rows, both), bf16),
            jax.ShapeDtypeStruct((1, both), f32),
            jax.ShapeDtypeStruct((rows, depth), bf16),
        ],
        scratch_shapes=[
            pltpu.VMEM((rows, depth), f32),
            pltpu.VMEM((2, depth, 2 * HD), bf16),
            pltpu.VMEM((2, rows, 2 * HD), bf16),
        ],
        compiler_params=pltpu.CompilerParams(vmem_limit_bytes=VMEM_LIMIT),
        cost_estimate=cost(4 * rows * depth * both, 2 * depth * both),
        name="feed_forward",
    )(hnorm, w, dact, scale)


def back_out_kernel(scalars, *refs):
    take = taker(refs)
    (piece_ref,) = take(1)
    cot_ref, resid_ref, raw_ref, gain_ref, scale_ref, b_ref, w_ref, a_ref = take(8)
    dattn_ref, dresid_ref, dz_ref, g_ref, through_ref = take(5)

    @pl.when(pl.program_id(0) == 0)
    def _():
        grad = piece_ref[...].astype(f32)
        resid = resid_ref[...]
        inverse = lax.rsqrt(jnp.mean(resid * resid, axis=-1, keepdims=True) + EPS)
        scaled = grad * gain_ref[...]
        lean = jnp.mean(resid * scaled, axis=-1, keepdims=True)
        dresid = cot_ref[0, 0].astype(f32) + inverse * scaled
        dresid = dresid - resid * (inverse * inverse * inverse * lean)
        dresid_ref[...] = dresid
        g_ref[...] = jnp.sum(dresid * raw_ref[...], axis=0, keepdims=True)
        dz = (dresid * scale_ref[...]).astype(bf16)
        dz_ref[...] = dz
        through_ref[...] = dot_nt(dz, b_ref[...]).astype(bf16)

    dattn = dot_nt(dz_ref[...], w_ref[...]) + dot(through_ref[...], a_ref[...])
    dattn_ref[0] = dattn.astype(bf16)


def back_out(k, chunk, piece, cotangent, resid, raw, gain, scale, b, w, a2_t):
    size = cotangent.shape[0]
    part, wide = resid.shape
    width = w.shape[0] // size
    fixed = lambda *shape: pl.BlockSpec(shape, lambda i, s: (0,) * len(shape))
    return pl.pallas_call(
        back_out_kernel,
        grid_spec=pltpu.PrefetchScalarGridSpec(
            num_scalar_prefetch=1,
            grid=(size,),
            in_specs=[
                fixed(part, wide),
                pl.BlockSpec((1, 1, part, wide), lambda i, s: (s[0], chunk, 0, 0)),
                fixed(part, wide),
                fixed(part, wide),
                fixed(1, wide),
                fixed(1, wide),
                fixed(RANK, wide),
                pl.BlockSpec((width, wide), lambda i, s: (lax.rem(i + s[0], size), 0)),
                pl.BlockSpec((RANK, width), lambda i, s: (0, lax.rem(i + s[0], size))),
            ],
            out_specs=[
                pl.BlockSpec((1, part, width), lambda i, s: (i, 0, 0)),
                fixed(part, wide),
                fixed(part, wide),
                fixed(1, wide),
                fixed(part, RANK),
            ],
        ),
        out_shape=[
            jax.ShapeDtypeStruct((size, part, width), bf16),
            jax.ShapeDtypeStruct((part, wide), f32),
            jax.ShapeDtypeStruct((part, wide), bf16),
            jax.ShapeDtypeStruct((1, wide), f32),
            jax.ShapeDtypeStruct((part, RANK), bf16),
        ],
        compiler_params=pltpu.CompilerParams(vmem_limit_bytes=VMEM_LIMIT),
        cost_estimate=cost(2 * part * width * size * wide, 2 * width * size * wide),
        name="back_out",
    )(k, piece, cotangent, resid, raw, gain, scale, b, w, a2_t)


def unproject_kernel(heads, scalars, cos_ref, sin_ref, raw_ref, scale_ref, w_ref, *refs):
    take = taker(refs)
    grads = take(heads)
    dz_ref, g_ref, out_ref = refs[heads:]
    width = heads * HD

    @pl.when(pl.program_id(0) == 0)
    def _():
        for layer in range(3):
            for d in range(heads):
                at = pl.ds(pl.multiple_of(layer * width + (scalars[0] ^ d) * HD, HD), HD)
                grad = grads[d][layer].astype(f32)
                if layer != 1:
                    grad = grad * cos_ref[...] - pltpu.roll(grad, HALF, 1) * sin_ref[...]
                raw = raw_ref[:, at].astype(f32)
                g_ref[:, at] = jnp.sum(grad * raw, axis=0, keepdims=True)
                dz_ref[:, at] = (grad * scale_ref[:, at]).astype(bf16)

    out_ref[...] = dot_nt(dz_ref[...], w_ref[...]).astype(bf16)


def unproject(order, cosine, sine, raw, scale, w, grads):
    operands = [cosine, sine, raw, scale]
    rows, wide = raw.shape
    depth = w.shape[0]
    step = 2 * HD
    return pl.pallas_call(
        functools.partial(unproject_kernel, len(grads)),
        grid_spec=pltpu.PrefetchScalarGridSpec(
            num_scalar_prefetch=1,
            grid=(depth // step,),
            in_specs=[whole_spec(x) for x in operands]
            + [pl.BlockSpec((step, wide), lambda i, s: (i, 0))]
            + [whole_spec(x) for x in grads],
            out_specs=[
                whole_spec(raw),
                whole_spec(scale),
                pl.BlockSpec((rows, step), lambda i, s: (0, i)),
            ],
        ),
        out_shape=[
            jax.ShapeDtypeStruct(raw.shape, bf16),
            jax.ShapeDtypeStruct(scale.shape, f32),
            jax.ShapeDtypeStruct((rows, depth), bf16),
        ],
        compiler_params=pltpu.CompilerParams(vmem_limit_bytes=VMEM_LIMIT),
        cost_estimate=cost(2 * rows * wide * depth, 2 * wide * depth),
        name="unproject",
    )(order, *operands, w, *grads)


def shares_kernel(count, chunks, span, *refs):
    take = taker(refs)
    x_refs, dz_refs = take(chunks), take(chunks)
    a_ref, b_ref, w_ref, cross_ref, g_ref, m_ref, column_ref = take(7)
    share_a_ref, share_b_ref = take(2)
    low, up, radial = take(3)
    step = pl.program_id(0)
    wide = b_ref.shape[1]

    @pl.when(step == 0)
    def _():
        up[...] = jnp.zeros_like(up)
        radial[...] = jnp.zeros_like(radial)
        for c in range(chunks):
            low[c] = dot_nt(x_refs[c][...], a_ref[...]).astype(bf16)

    shrink = g_ref[...] * m_ref[...] / (column_ref[...] * column_ref[...] * column_ref[...])
    shape = (count * RANK, wide)
    column = lax.broadcasted_iota(jnp.int32, shape, 1) + step * wide
    layer_of = lax.rem(column // span, count)
    own = (lax.broadcasted_iota(jnp.int32, shape, 0) // RANK) == layer_of
    b_pad = jnp.where(own, jnp.concatenate([b_ref[...]] * count, axis=0), 0.0)
    b_low = b_pad.astype(bf16)
    ap = jnp.zeros(shape, f32)
    for c in range(chunks):
        dz = dz_refs[c][...]
        up[c] += dot_nt(dz, b_low)
        ap += dot_tn(low[c], dz)
    radial[...] += dot_nt((b_pad * shrink).astype(bf16), w_ref[...])
    ap = jnp.where(own, ap, 0.0)
    picked = ap[:RANK]
    for i in range(1, count):
        picked = picked + ap[i * RANK : (i + 1) * RANK]
    share_b_ref[...] = (SCALING * (picked - cross_ref[...] * shrink)).astype(bf16)

    @pl.when(step == pl.num_programs(0) - 1)
    def _():
        total = -radial[...]
        for c in range(chunks):
            total = total + dot_tn(up[c].astype(bf16), x_refs[c][...])
        share_a_ref[...] = (SCALING * total).astype(bf16)


def layer_shares(inputs, a_t, dz, b, span, merged, cross, g, magnitude, column):
    chunks = len(inputs)
    rows, depth = inputs[0].shape
    width = dz[0].shape[1]
    count = a_t.shape[0] // RANK
    step = 2 * HD
    columns = lambda height: pl.BlockSpec((height, step), lambda i: (0, i))
    fixed = lambda x: pl.BlockSpec(x.shape, lambda i: (0, 0))
    return pl.pallas_call(
        functools.partial(shares_kernel, count, chunks, span),
        grid=(width // step,),
        in_specs=[fixed(x) for x in inputs]
        + [columns(rows)] * chunks
        + [fixed(a_t), columns(RANK), columns(depth), columns(RANK)]
        + [columns(1)] * 3,
        out_specs=[fixed(a_t), columns(RANK)],
        out_shape=[
            jax.ShapeDtypeStruct(a_t.shape, bf16),
            jax.ShapeDtypeStruct((RANK, width), bf16),
        ],
        scratch_shapes=[
            pltpu.VMEM((chunks, rows, count * RANK), bf16),
            pltpu.VMEM((chunks, rows, count * RANK), f32),
            pltpu.VMEM(a_t.shape, f32),
        ],
        compiler_params=pltpu.CompilerParams(vmem_limit_bytes=VMEM_LIMIT),
        cost_estimate=cost(rows * depth * 64, depth * width),
        name="shares",
    )(*inputs, *dz, a_t.astype(bf16), b, merged, cross, g, magnitude, column)


def down_kernel(chunks, *refs):
    take = taker(refs)
    act_refs = take(chunks)
    w_ref, cot_ref, scale_ref, a_ref, b_ref = take(5)
    raw_ref, g_ref, ap_ref, pb_ref = take(4)
    low, up = take(2)
    step = pl.program_id(0)
    rows = act_refs[0].shape[0]
    size, _, part, wide = cot_ref.shape

    @pl.when(step == 0)
    def _():
        up[...] = jnp.zeros_like(up)
        for c in range(chunks):
            low[c] = dot_nt(act_refs[c][...], a_ref[...]).astype(bf16)

    g = jnp.zeros((1, wide), f32)
    ap = jnp.zeros((RANK, wide), f32)
    b_low = b_ref[...].astype(bf16)
    for c in range(chunks):
        raw = dot(act_refs[c][...], w_ref[...])
        raw_ref[:, c] = raw.astype(bf16).reshape(size, part, wide)
        cot = cot_ref[:, c].reshape(rows, wide).astype(f32)
        g += jnp.sum(cot * raw, axis=0, keepdims=True)
        dz = (cot * scale_ref[...]).astype(bf16)
        up[c] += dot_nt(dz, b_low)
        ap += dot_tn(low[c], dz)
    g_ref[...] = g
    ap_ref[...] = ap.astype(bf16)

    @pl.when(step == pl.num_programs(0) - 1)
    def _():
        total = jnp.zeros(pb_ref.shape, f32)
        for c in range(chunks):
            total = total + dot_tn(up[c].astype(bf16), act_refs[c][...])
        pb_ref[...] = total.astype(bf16)


def down_project(acts, w, cotangent, scale, a_t, b):
    chunks = len(acts)
    rows, ff = acts[0].shape
    wide = w.shape[1]
    step = 2 * HD
    size, _, part, _ = cotangent.shape
    columns = lambda height: pl.BlockSpec((height, step), lambda i: (0, i))
    fixed = lambda *shape: pl.BlockSpec(shape, lambda i: (0,) * len(shape))
    view = pl.BlockSpec((size, chunks, part, step), lambda i: (0, 0, 0, i))
    return pl.pallas_call(
        functools.partial(down_kernel, chunks),
        grid=(wide // step,),
        in_specs=[fixed(rows, ff)] * chunks
        + [columns(ff), view, columns(1), fixed(RANK, ff), columns(RANK)],
        out_specs=[view, columns(1), columns(RANK), fixed(RANK, ff)],
        out_shape=[
            jax.ShapeDtypeStruct(cotangent.shape, bf16),
            jax.ShapeDtypeStruct((1, wide), f32),
            jax.ShapeDtypeStruct((RANK, wide), bf16),
            jax.ShapeDtypeStruct((RANK, ff), bf16),
        ],
        scratch_shapes=[
            pltpu.VMEM((chunks, rows, RANK), bf16),
            pltpu.VMEM((chunks, rows, RANK), f32),
        ],
        compiler_params=pltpu.CompilerParams(vmem_limit_bytes=VMEM_LIMIT),
        cost_estimate=cost(2 * chunks * rows * ff * wide, 2 * ff * wide),
        name="down_project",
    )(*acts, w, cotangent, scale, a_t.astype(bf16), b)


def pack_kernel(plan, scalars, *refs):
    out_ref = refs[-1]
    out_ref[...] = jnp.zeros_like(out_ref)
    row = 0
    for ref, (parts, placed) in zip(refs[:-1], plan):
        height, width = ref.shape
        wide = width // parts
        short = -height % RANK
        lanes = slice(0, wide)
        if placed:
            lanes = pl.ds(pl.multiple_of(scalars[0] * wide, HD), wide)
        if height == 1:
            value = [ref[:, i * wide : (i + 1) * wide].astype(f32) for i in range(parts)]
            value.append(jnp.zeros((RANK - parts, wide), f32))
            out_ref[row : row + RANK, lanes] = jnp.concatenate(value, axis=0).astype(bf16)
            row += RANK
        else:
            for i in range(parts):
                value = ref[:, i * wide : (i + 1) * wide].astype(bf16)
                out_ref[row : row + height, lanes] = value
                row += height


def pack(k, height, width, *entries):
    arrays = [x for x, _, _ in entries]
    plan = [(parts, placed) for _, parts, placed in entries]
    return pl.pallas_call(
        functools.partial(pack_kernel, plan),
        grid_spec=pltpu.PrefetchScalarGridSpec(
            num_scalar_prefetch=1,
            grid=(1,),
            in_specs=[whole_spec(x) for x in arrays],
            out_specs=pl.BlockSpec((height, width), lambda i, s: (0, 0)),
        ),
        out_shape=jax.ShapeDtypeStruct((height, width), bf16),
        compiler_params=pltpu.CompilerParams(vmem_limit_bytes=VMEM_LIMIT),
        cost_estimate=cost(height * width, 4 * height * width),
        name="pack",
    )(k, *arrays)


def span_positions(row_ids, span_order, span_len):
    slot_ids = row_ids // span_len
    slot_table = jnp.arange(span_order.shape[0], dtype=jnp.int32)
    picked = jnp.sum(
        jnp.where(slot_ids[:, None] == slot_table[None, :], span_order[None, :], 0), axis=1
    )
    return picked * span_len + row_ids % span_len


def rotary_tables(positions):
    lane = np.arange(HD)
    frequency = (ROPE_BASE ** (-2.0 * (lane % HALF) / HD)).astype(np.float32)
    sign = np.where(lane < HALF, -1.0, 1.0).astype(np.float32)
    angles = positions.astype(f32)[:, None] * frequency[None, :]
    return jnp.cos(angles), jnp.sin(angles) * sign[None, :]


def pick_blocks(blocks, index):
    out = blocks[0]
    for i in range(1, len(blocks)):
        out = jnp.where(index == i, blocks[i], out)
    return out


def inverse_rms(values):
    return lax.rsqrt(jnp.mean(values * values, axis=-1, keepdims=True) + EPS)


def rms_backward(values, gain_vec, grad_in):
    inverse = inverse_rms(values)
    scaled = grad_in * gain_vec
    return inverse * scaled - values * inverse * inverse * inverse * jnp.mean(
        values * scaled, axis=-1, keepdims=True
    )


def per_device(
    hidden_in,
    cotangent,
    segment_ids,
    padding,
    span_order,
    gain_attn,
    gain_mlp,
    w_query,
    w_key,
    w_value,
    w_out,
    w_gate,
    w_up,
    w_down,
    a_query,
    b_query,
    m_query,
    a_key,
    b_key,
    m_key,
    a_value,
    b_value,
    m_value,
    a_out,
    b_out,
    m_out,
    a_gate,
    b_gate,
    m_gate,
    a_up,
    b_up,
    m_up,
    a_down,
    b_down,
    m_down,
):
    rows, width = hidden_in.shape
    span_len = rows // 2
    near_width = w_query.shape[1]
    peers = near_width // HD
    n_mp = lax.axis_size("mp")
    n_seq = lax.axis_size("seq")
    n_doc = lax.axis_size("doc")
    groups = n_seq // peers
    copies = n_seq * n_doc
    share = rows // n_mp
    chunks = CHUNKS
    part = share // chunks
    k = lax.axis_index("mp")
    doc = lax.axis_index("doc")
    seq = lax.axis_index("seq")
    me = lax.rem(seq, peers)
    my_group = seq // peers
    order = jnp.reshape(me, (1,)).astype(jnp.int32)
    k_scalar = jnp.reshape(k, (1,)).astype(jnp.int32)

    slice_rows = near_width // n_doc
    wo_slice = lax.dynamic_slice_in_dim(w_out, doc * slice_rows, slice_rows, 0)
    wo_all = lax.all_gather(wo_slice, ("mp", "doc"), axis=0, tiled=True)

    slots = [
        2 * (my_group * peers + (me ^ d)) + half for d in range(peers) for half in range(2)
    ]
    slots += [
        2 * (g * peers + (me ^ d)) + half
        for g in range(groups)
        for d in range(peers)
        for half in range(2)
    ]
    slots = jnp.stack(slots)
    table = jnp.arange(span_order.shape[0], dtype=jnp.int32)
    places = jnp.sum(jnp.where(slots[:, None] == table[None, :], span_order[None, :], 0), axis=1)
    scalars = jnp.concatenate([places, k_scalar]).astype(jnp.int32)
    row_ids = jnp.arange(rows, dtype=jnp.int32) + seq * rows
    cosine, sine = rotary_tables(span_positions(row_ids, span_order, span_len))
    codes = seq_exchange([segment_ids * 2 + padding] * peers)
    (hidden_next,) = after([hidden_in], *codes)

    a_heads = jnp.stack([a_key.T, a_value.T, a_query.T])
    b_heads = [b_key, b_value, b_query]
    m_heads = jnp.concatenate([m_key, m_value, m_query])[None, :]
    blocks, normed, wh_low, raw_heads, column_heads, scale_heads, cross_heads = project_heads(
        order,
        hidden_next,
        gain_attn[None, :],
        (w_key, w_value, w_query),
        a_heads,
        jnp.concatenate(b_heads, axis=1),
        m_heads,
        cosine,
        sine,
    )
    heads = seq_exchange(blocks)

    w_out_next, w_down_next = after([w_out, w_down], raw_heads)
    codes = [x.reshape(rows, 1) for x in codes]
    square_out, cross_out = merge_columns(w_out_next, a_out.T, b_out, False)
    square_down, cross_down, wd_low = merge_columns(w_down_next, a_down.T, b_down, True)
    own_a = jnp.where(
        jnp.arange(n_mp * near_width)[None, :] // near_width == k,
        jnp.concatenate([a_out.T] * n_mp, axis=1),
        0.0,
    )
    small = jnp.concatenate([square_out, square_down, own_a], axis=0)

    extra = []
    if groups > 1:
        members = [[g * peers + i for g in range(groups)] for i in range(peers)]
        gather = lambda x: lax.all_gather(
            x[None], "seq", axis=0, tiled=True, axis_index_groups=members
        )
        extra = [gather(jnp.stack([x[:2] for x in heads])), gather(jnp.stack(codes))]
    heads_next = after(heads, square_out, square_down)
    o_blocks, lse = attention_forward(
        scalars, heads_next, codes, extra, groups, n_mp, chunks
    )
    o_heads = seq_exchange(o_blocks)
    near = jnp.concatenate([pick_blocks(o_heads, me ^ h) for h in range(peers)], axis=1)
    near_chunks = [near[c * n_mp * part : (c + 1) * n_mp * part] for c in range(chunks)]

    (small,) = after([small], lse)
    small = butterfly(small, ["mp"])
    column_out = jnp.sqrt(small[:1])
    column_down = jnp.sqrt(small[1:2])
    a_out_all = small[2:]
    scale_out = m_out[None, :] / column_out
    scale_down = m_down[None, :] / column_down

    w_gate_next, w_up_next = after([w_gate, w_up], lse)
    wgu_low, square_gu, cross_gu = merge_pair(
        w_gate_next,
        w_up_next,
        jnp.concatenate([a_gate.T, a_up.T], axis=0),
        jnp.concatenate([b_gate, b_up], axis=1),
    )
    column_gu = jnp.sqrt(square_gu)
    m_gu = interleave(m_gate[None, :], m_up[None, :])
    scale_gu = m_gu / column_gu
    (cotangent_next,) = after([cotangent], square_gu)
    dz_down = (cotangent_next.astype(f32) * scale_down).astype(bf16)
    dact = dot_nt(dz_down, wd_low).astype(bf16)

    def chunked(values):
        return values.reshape(n_mp, chunks, part, values.shape[-1])

    hid_view, cot_view, dact_view = chunked(hidden_in), chunked(cotangent), chunked(dact)
    b_out_low = b_out.astype(bf16)
    a_out_low = a_out_all.astype(bf16)
    acts, hnorms, dz_gus, dh_chunks = [], [], [], []
    resid_own, raw_out_own, out_low_own = [], [], []
    g_gu = 0.0
    lines = ([near_chunks[0]], [near_chunks[0]])
    for step in range(1, n_mp):
        line_step(*lines, step)
    gathered_chunks = [line_blocks(*lines)]
    for c in range(1, chunks):
        (near_next,) = after([near_chunks[c]], *gathered_chunks[0])
        others = lax.all_gather(near_next, "mp", axis=0)
        gathered_chunks.append(
            [near_chunks[c]]
            + [
                lax.dynamic_index_in_dim(others, lax.rem(k + i, n_mp), 0, keepdims=False)
                for i in range(1, n_mp)
            ]
        )
    for c in range(chunks):
        gathered = gathered_chunks[c]
        if c > 0:
            gathered = after(gathered, dh_chunks[-1])
        hnorm, resid, raw_out, out_low = out_project(
            k_scalar,
            c,
            gathered,
            wo_all,
            a_out_low,
            hid_view,
            (SCALING * b_out).astype(bf16),
            scale_out,
            gain_mlp[None, :],
        )
        act, dz_gu, g, dh = feed_forward(c, hnorm, wgu_low, dact_view, scale_gu)
        g_gu = g_gu + g
        dh_chunks.append(dh)
        acts.append(act)
        hnorms.append(hnorm)
        dz_gus.append(dz_gu)
        resid_own.append(resid)
        raw_out_own.append(raw_out)
        out_low_own.append(out_low)

    def scatter(parts):
        return lax.psum_scatter(parts, "mp", scatter_dimension=0, tiled=True)

    pieces = [scatter(x) for x in dh_chunks]

    arrived, dresid_own, dz_out, through_out = [], [], [], []
    g_out = 0.0
    earlier = dh_chunks[-1]
    for c in range(chunks):
        (own_piece,) = after([pieces[c]], earlier)
        dattn, dresid, dz, g, through = back_out(
            k_scalar,
            c,
            own_piece,
            cot_view,
            resid_own[c],
            raw_out_own[c],
            gain_mlp[None, :],
            scale_out,
            b_out_low,
            wo_all,
            (SCALING * a_out_all).astype(bf16),
        )
        g_out = g_out + g
        arrived.append(dattn[0])
        for shift in range(1, n_mp):
            pairs = [(i, (i + shift) % n_mp) for i in range(n_mp)]
            arrived.append(lax.ppermute(dattn[shift], "mp", pairs))
        dresid_own.append(dresid)
        dz_out.append(dz)
        through_out.append(through)
        earlier = dz
        if c == 0:
            acts_next = after(acts, dz)
            raw_down, g_down, ap_down, pb_down = down_project(
                acts_next, wd_low, cot_view, scale_down, a_down.T, b_down
            )
            hnorms_next, dz_gus_next = after(
                [tuple(hnorms), tuple(dz_gus)], g_down, *arrived[1:]
            )
            share_a_gu, share_b_gu = layer_shares(
                hnorms_next,
                jnp.concatenate([a_gate.T, a_up.T], axis=0),
                dz_gus_next,
                interleave(b_gate, b_up),
                HD,
                wgu_low,
                cross_gu,
                g_gu,
                m_gu,
                column_gu,
            )
            earlier = share_a_gu
    arrived = jnp.concatenate(arrived, axis=0)
    by_head = [arrived[:, h * HD : (h + 1) * HD] for h in range(peers)]
    grad_blocks = seq_exchange([pick_blocks(by_head, me ^ d) for d in range(peers)])
    dresid_own = jnp.concatenate(dresid_own, axis=0)
    dz_out = jnp.concatenate(dz_out, axis=0)
    ap_out = dot_tn(jnp.concatenate(out_low_own, axis=0), dz_out)
    early = pack(
        k_scalar,
        128,
        width,
        (share_a_gu, 1, False),
        (ap_down, 1, False),
        (cross_out / copies, 1, False),
        (cross_down / copies, 1, False),
        (ap_out, 1, False),
        (g_down, 1, False),
        (g_out, 1, False),
    )
    early_rows = pack(
        k_scalar,
        48,
        share_b_gu.shape[1],
        (share_b_gu, 1, False),
        (pb_down, 1, False),
        (g_gu, 1, False),
    )
    grads, dkv = attention_backward(
        scalars, heads_next, codes, extra, o_blocks, grad_blocks, lse, groups, n_mp, chunks
    )
    if groups > 1:
        members = [[g * peers + i for g in range(groups)] for i in range(peers)]
        dkv = lax.psum_scatter(
            dkv, "seq", scatter_dimension=0, tiled=True, axis_index_groups=members
        )
        grads = [jnp.concatenate([dkv[0, d], grads[d]], axis=0) for d in range(peers)]
    head_grads = seq_exchange(grads)

    through_all = jnp.concatenate(through_out, axis=0).reshape(chunks, 1, part, RANK)
    through_all = lax.dynamic_update_slice(
        jnp.zeros((chunks, n_mp, part, RANK), bf16), through_all, (0, k, 0, 0)
    ).reshape(rows, RANK)
    early, early_rows, through_all = after([early, early_rows, through_all], grads[0])
    through_all = butterfly(through_all, ["mp"])
    early = spread_sum(doc_halve(early), peers, ["mp"])
    early = doc_join(spread_join(early, peers)).astype(f32)
    early_rows = doc_join(butterfly(doc_halve(early_rows), ["seq"])).astype(f32)
    pb_out = dot_tn(through_all, near)
    (raw_down,) = after([raw_down], dz_out)
    down_own = scatter(raw_down.reshape(rows, width))
    (down_own,) = after([down_own], grads[0])
    result = jnp.concatenate(resid_own, axis=0) + down_own.astype(f32) * scale_down
    hidden_own = lax.dynamic_slice_in_dim(hidden_in, k * share, share, 0).astype(f32)
    head_grads = after(head_grads, result)

    dz_heads, g_heads, dnormed = unproject(
        order, cosine, sine, raw_heads, scale_heads, wh_low, head_grads
    )
    dnormed_own = scatter(dnormed)

    def rank_rows(array, index):
        return array[index * RANK : (index + 1) * RANK]

    ff = w_gate.shape[1]
    total_g_down, total_g_out = early[96:97], early[112:113]
    shrink_out = total_g_out * m_out / (column_out * column_out * column_out)
    shrink_down = total_g_down * m_down / (column_down * column_down * column_down)
    turned_out = (b_out * shrink_out).astype(bf16)
    radial_out = dot_nt(turned_out, w_out) + SCALING * dot(
        dot_nt(turned_out, b_out.astype(bf16)), a_out.T
    )
    radial_down = dot_nt((b_down * shrink_down).astype(bf16), wd_low)
    grad_a_down = SCALING * (early_rows[16:32, :ff] - radial_down)
    grad_b_out = SCALING * (rank_rows(early, 5) - rank_rows(early, 3) * shrink_out)
    grad_b_down = SCALING * (rank_rows(early, 2) - rank_rows(early, 4) * shrink_down)

    share_a_heads, share_b_heads = layer_shares(
        [normed],
        a_heads.reshape(3 * RANK, width),
        [dz_heads],
        jnp.concatenate(b_heads, axis=1),
        near_width,
        wh_low,
        cross_heads,
        g_heads,
        m_heads,
        column_heads,
    )
    late = pack(
        k_scalar,
        128,
        width,
        (share_a_heads, 1, False),
        (share_b_heads, 3, True),
        (pb_out, 1, True),
        (g_heads, 3, True),
    )
    late = spread_sum(doc_halve(late), peers, ["mp"])
    (late,) = after([late], grad_a_down, grad_b_down, radial_out)
    late = doc_join(spread_join(late, peers)).astype(f32)
    late_columns = late[3 * RANK : 8 * RANK]
    late_own = lax.dynamic_slice_in_dim(late_columns, k * near_width, near_width, 1)

    grad_input = dresid_own + rms_backward(
        hidden_own, gain_attn, dnormed_own.astype(f32)
    )

    grad_a_out = SCALING * (rank_rows(late_own, 3) - radial_out)
    g_rows = late_own[4 * RANK : 4 * RANK + 3].reshape(1, -1) / column_heads
    g_rows = [g_rows[0, i * near_width : (i + 1) * near_width] for i in range(3)]
    grad_m_gate, grad_m_up = separate(early_rows[32:33] / column_gu)
    grad_b_gate, grad_b_up = separate(early_rows[:16])
    return (
        result,
        grad_input,
        rank_rows(late, 2).T,
        rank_rows(late_own, 2),
        g_rows[2],
        rank_rows(late, 0).T,
        rank_rows(late_own, 0),
        g_rows[0],
        rank_rows(late, 1).T,
        rank_rows(late_own, 1),
        g_rows[1],
        grad_a_out.T,
        grad_b_out,
        (total_g_out / column_out)[0],
        rank_rows(early, 0).T,
        grad_b_gate,
        grad_m_gate[0],
        rank_rows(early, 1).T,
        grad_b_up,
        grad_m_up[0],
        grad_a_down.T,
        grad_b_down,
        (total_g_down / column_down)[0],
    )


def solution(mesh):
    rows = P(("doc", "seq"))
    split_columns = (P(None, "mp"), P(None, "mp"))
    column_layer = (P(), P(None, "mp"), P("mp"))
    row_layer = (P("mp", None), P(), P())
    in_specs = (
        P(("doc", "seq"), None),
        P(("doc", "seq"), None),
        rows,
        rows,
        P(),
        P(),
        P(),
        P(None, "mp"),
        P(None, "mp"),
        P(None, "mp"),
        P("mp", None),
        *split_columns,
        P("mp", None),
        *column_layer,
        *column_layer,
        *column_layer,
        *row_layer,
        *column_layer,
        *column_layer,
        *row_layer,
    )
    out_specs = (
        P(("doc", "seq", "mp"), None),
        P(("doc", "seq", "mp"), None),
        *column_layer,
        *column_layer,
        *column_layer,
        *row_layer,
        *column_layer,
        *column_layer,
        *row_layer,
    )
    return jax.shard_map(
        per_device, mesh=mesh, in_specs=in_specs, out_specs=out_specs, check_vma=False
    )
```

```python
import functools
import math

import jax
import jax.numpy as jnp
import numpy as np
from jax import lax
from jax.experimental import pallas as pl
from jax.experimental.pallas import tpu as pltpu
from jax.sharding import PartitionSpec as P

HD = 128
RANK = 16
ALPHA = 32
HALF = HD // 2
SCALING = ALPHA / RANK
INV_ROOT = HD ** (-0.5)
EPS = 1e-05
ROPE_BASE = 10000.0
MASKED = -1e30
CHUNKS = 2
MIB = 1 << 20
VMEM_LIMIT = 56 * MIB

f32 = jnp.float32
bf16 = jnp.bfloat16


def dot(left, right):
    return jnp.dot(left, right, preferred_element_type=f32)


def dot_nt(left, right):
    return lax.dot_general(left, right, (((1,), (1,)), ((), ())), preferred_element_type=f32)


def dot_tn(left, right):
    return lax.dot_general(left, right, (((0,), (0,)), ((), ())), preferred_element_type=f32)


def whole_spec(array):
    rank = len(array.shape)
    return pl.BlockSpec(tuple(array.shape), lambda *_: (0,) * rank)


def cost(flops, moved):
    return pl.CostEstimate(flops=1, bytes_accessed=1, transcendentals=0)


def swap(value, axis, distance):
    size = lax.axis_size(axis)
    return lax.ppermute(value, axis, [(i, i ^ distance) for i in range(size)])


def butterfly(value, axes):
    for axis in axes:
        distance = 1
        while distance < lax.axis_size(axis):
            value = lax.optimization_barrier(value + swap(value, axis, distance))
            distance *= 2
    return value


def doc_halve(value):
    doc = lax.axis_index("doc")
    half = value.shape[0] // 2
    mine = lax.dynamic_slice_in_dim(value, doc * half, half, 0)
    other = lax.dynamic_slice_in_dim(value, (1 - doc) * half, half, 0)
    return lax.optimization_barrier(mine + swap(other, "doc", 1))


def doc_join(mine):
    doc = lax.axis_index("doc")
    other = swap(mine, "doc", 1)
    first = jnp.where(doc == 0, mine, other)
    second = jnp.where(doc == 0, other, mine)
    return jnp.concatenate([first, second], axis=0)


def spread_sum(value, peers, axes):
    me = lax.rem(lax.axis_index("seq"), peers)
    parts = value.reshape(peers, -1, value.shape[-1])
    piece = lambda index: lax.dynamic_index_in_dim(parts, index, 0, keepdims=False)
    mine = piece(me).astype(f32)
    for d in range(1, peers):
        mine = mine + swap(piece(me ^ d), "seq", d).astype(f32)
    mine = lax.optimization_barrier(mine.astype(bf16))
    distance = peers
    while distance < lax.axis_size("seq"):
        mine = lax.optimization_barrier(mine + swap(mine, "seq", distance))
        distance *= 2
    return butterfly(mine, axes)


def spread_join(mine, peers):
    me = lax.rem(lax.axis_index("seq"), peers)
    found = [mine] + [swap(mine, "seq", d) for d in range(1, peers)]
    return jnp.concatenate([pick_blocks(found, me ^ i) for i in range(peers)], axis=0)


def after(values, *earlier):
    tied = lax.optimization_barrier((tuple(values), earlier))
    return tied[0]


def line_step(rights, lefts, step, *earlier):
    size = lax.axis_size("mp")
    right, left = rights[-1], lefts[-1]
    if earlier:
        right, left = after([right, left], *earlier)
    right_pairs = [(i, i + 1) for i in range(step - 1, size - 1)]
    left_pairs = [(i, i - 1) for i in range(1, size - step + 1)]
    rights.append(lax.ppermute(right, "mp", right_pairs))
    lefts.append(lax.ppermute(left, "mp", left_pairs))


def line_blocks(rights, lefts):
    size = lax.axis_size("mp")
    k = lax.axis_index("mp")
    return [rights[0]] + [
        jnp.where(k + c < size, lefts[c], rights[size - c]) for c in range(1, size)
    ]


def seq_exchange(blocks):
    return [blocks[0]] + [swap(blocks[d], "seq", d) for d in range(1, len(blocks))]


def key_marks(code):
    lane = lax.broadcasted_iota(jnp.int32, (code.shape[0], HD), 1)
    segment, real = code >> 1, code & 1
    wrong = (lane < 16) & (lane != segment)
    absent = (lane == 16) & (real == 0)
    return jnp.where(wrong | absent, MASKED, 0.0).astype(bf16)


def query_marks(code):
    lane = lax.broadcasted_iota(jnp.int32, (code.shape[0], HD), 1)
    segment = code >> 1
    return jnp.where((lane == segment) | (lane == 16), 1.0, 0.0).astype(bf16)


def diagonal_scores(keys, query, first_key=0):
    marked = dot_nt(keys, query)
    plain = dot_nt(keys[:, :HD], query[:, :HD])
    key_id = lax.broadcasted_iota(jnp.int32, marked.shape, 0) + first_key
    query_id = lax.broadcasted_iota(jnp.int32, marked.shape, 1)
    return jnp.where(
        key_id < query_id, marked, jnp.where(key_id == query_id, plain, MASKED)
    )


def block_readers(groups, heads, kv_refs, code_refs):
    if groups == 1:
        return (
            lambda g, d, rows: heads[d][0, rows, :],
            lambda g, d, rows: heads[d][1, rows, :],
            lambda g, d, rows: code_refs[d][rows, :],
        )
    return (
        lambda g, d, rows: kv_refs[0][g, d, 0, rows, :],
        lambda g, d, rows: kv_refs[0][g, d, 1, rows, :],
        lambda g, d, rows: kv_refs[1][g, d, rows, :],
    )


def taker(refs):
    refs = list(refs)

    def take(count):
        taken = refs[:count]
        del refs[:count]
        return taken

    return take


def forward_kernel(meta, scalars, *refs):
    peers, groups, span, pieces, chunks, n_extra = meta
    take = taker(refs)
    heads, code_refs, kv_refs = take(peers), take(peers), take(n_extra)
    o_refs, (lse_ref,) = take(peers), take(1)
    q_all, o_all, k_all, v_turned = take(4)
    key_of, value_of, key_code_of = block_readers(groups, heads, kv_refs, code_refs)
    n_query = 2 * peers

    for g in range(groups):
        for d in range(peers):
            for half in range(2):
                rows = pl.ds(half * span, span)
                place = scalars[n_query + (g * peers + d) * 2 + half]
                at = pl.ds(pl.multiple_of(place * span, HD), span)
                k_all[at, :HD] = key_of(g, d, rows)
                k_all[at, HD:] = key_marks(key_code_of(g, d, rows))
                v_turned[:, at] = value_of(g, d, rows).astype(f32).T.astype(bf16)
    for d in range(peers):
        for half in range(2):
            rows = pl.ds(half * span, span)
            q_all[2 * d + half, :, :HD] = heads[d][2, rows, :]
            q_all[2 * d + half, :, HD:] = query_marks(code_refs[d][rows, :])

    def one_span(i, carry):
        place = scalars[i]
        query = q_all[i]
        at = pl.ds(pl.multiple_of(place * span, HD), span)
        scores = diagonal_scores(k_all[at, :], query)
        peak = jnp.max(scores, axis=0, keepdims=True)
        weights = jnp.exp((scores - peak) * INV_ROOT)
        total = jnp.sum(weights, axis=0, keepdims=True)
        out = dot(v_turned[:, at], weights.astype(bf16))

        def key_span(j, state):
            peak, total, out = state
            at = pl.ds(pl.multiple_of(j * span, HD), span)
            scores = dot_nt(k_all[at, :], query)
            new_peak = jnp.maximum(peak, jnp.max(scores, axis=0, keepdims=True))
            fade = jnp.exp((peak - new_peak) * INV_ROOT)
            weights = jnp.exp((scores - new_peak) * INV_ROOT)
            total = total * fade + jnp.sum(weights, axis=0, keepdims=True)
            out = out * fade + dot(v_turned[:, at], weights.astype(bf16))
            return (new_peak, total, out)

        peak, total, out = lax.fori_loop(0, place, key_span, (peak, total, out))
        lse_ref[i] = peak * INV_ROOT + jnp.log(total)
        o_all[i] = (out / total).T.astype(bf16)
        return carry

    lax.fori_loop(0, n_query, one_span, 0)
    share = 2 * span // pieces
    part = share // chunks
    for d in range(peers):
        for piece in range(pieces):
            for c in range(chunks):
                row = piece * share + c * part
                to = (c * pieces + piece) * part
                o_refs[d][to : to + part, :] = o_all[
                    2 * d + row // span, row % span : row % span + part, :
                ]


def place_rows(scalars, peers, span):
    for d in range(peers):
        for half in range(2):
            place = scalars[2 * d + half]
            at = pl.ds(pl.multiple_of(place * span, HD), span)
            yield d, half, pl.ds(half * span, span), at


def piece_rows(peers, span, pieces, chunks):
    share = 2 * span // pieces
    part = share // chunks
    for d in range(peers):
        for piece in range(pieces):
            for c in range(chunks):
                row = piece * share + c * part
                yield d, piece, c, pl.ds((c * pieces + piece) * part, part), row, part


def forward_group_kernel(meta, scalars, *refs):
    peers, _, span, pieces, chunks, _ = meta
    take = taker(refs)
    heads, code_refs = take(peers), take(peers)
    o_refs, (lse_ref,) = take(peers), take(1)
    q_all, o_all, k_all, v_turned = take(4)
    tile = 2 * span

    for d, half, rows, at in place_rows(scalars, peers, span):
        code = code_refs[d][rows, :]
        k_all[at, :HD] = heads[d][0, rows, :]
        k_all[at, HD:] = key_marks(code)
        v_turned[:, at] = heads[d][1, rows, :].astype(f32).T.astype(bf16)
        q_all[at, :HD] = heads[d][2, rows, :]
        q_all[at, HD:] = query_marks(code)

    for m in range(peers):
        here = slice(m * tile, (m + 1) * tile)
        query = q_all[here, :]
        scores = diagonal_scores(k_all[here, :], query)
        peak = jnp.max(scores, axis=0, keepdims=True)
        weights = jnp.exp((scores - peak) * INV_ROOT)
        total = jnp.sum(weights, axis=0, keepdims=True)
        out = dot(v_turned[:, here], weights.astype(bf16))

        def key_tile(j, state):
            peak, total, out = state
            at = pl.ds(pl.multiple_of(j * tile, HD), tile)
            scores = dot_nt(k_all[at, :], query)
            new_peak = jnp.maximum(peak, jnp.max(scores, axis=0, keepdims=True))
            fade = jnp.exp((peak - new_peak) * INV_ROOT)
            weights = jnp.exp((scores - new_peak) * INV_ROOT)
            total = total * fade + jnp.sum(weights, axis=0, keepdims=True)
            out = out * fade + dot(v_turned[:, at], weights.astype(bf16))
            return (new_peak, total, out)

        if m:
            steps = m * tile // tile
            peak, total, out = lax.fori_loop(0, steps, key_tile, (peak, total, out))
        lse_ref[m] = peak * INV_ROOT + jnp.log(total)
        o_all[here, :] = (out / total).T.astype(bf16)

    for d, piece, c, to, row, part in piece_rows(peers, span, pieces, chunks):
        place = scalars[2 * d + row // span] * span + row % span
        o_refs[d][to, :] = o_all[pl.ds(pl.multiple_of(place, 32), part), :]


def backward_group_kernel(meta, scalars, *refs):
    peers, groups, span, pieces, chunks, _ = meta
    take = taker(refs)
    heads, code_refs = take(peers), take(peers)
    o_refs, do_refs, (lse_ref,) = take(peers), take(peers), take(1)
    grad_refs = take(peers)
    q_all, o_all, do_all, k_all, k_turned, v_all, dk_all, dv_all = take(8)
    own_piece = scalars[4 * peers]
    tile = 2 * span
    share = 2 * span // pieces

    for d, half, rows, at in place_rows(scalars, peers, span):
        code = code_refs[d][rows, :]
        key = heads[d][0, rows, :]
        k_all[at, :HD] = key
        k_all[at, HD:] = key_marks(code)
        k_turned[:, at] = key.astype(f32).T.astype(bf16)
        v_all[at, :] = heads[d][1, rows, :]
        q_all[at, :HD] = heads[d][2, rows, :]
        q_all[at, HD:] = query_marks(code)
    for d, piece, c, source, row, part in piece_rows(peers, span, pieces, chunks):
        place = scalars[2 * d + row // span] * span + row % span
        o_all[pl.ds(pl.multiple_of(place, 32), part), :] = o_refs[d][source, :]
        row = lax.rem(own_piece + pieces - piece, pieces) * share + c * part
        late = row >= span
        place = scalars[2 * d + late.astype(jnp.int32)] * span + row - jnp.where(late, span, 0)
        do_all[pl.ds(pl.multiple_of(place, 32), part), :] = do_refs[d][source, :]

    for m in range(peers):
        here = slice(m * tile, (m + 1) * tile)
        query = q_all[here, :]
        grad = do_all[here, :]
        product = grad.astype(f32) * o_all[here, :].astype(f32)
        high, rest = split_low(product)
        ones = jnp.ones((16, HD), bf16)
        delta = (dot_nt(ones, high) + dot_nt(ones, rest))[:1, :]
        lse = lse_ref[m]

        def key_tile(at, scores, dq_turned, first):
            probs = jnp.exp(scores * INV_ROOT - lse)
            grad_score = (probs * (dot_nt(v_all[at, :], grad) - delta)).astype(bf16)
            dv = dot(probs.astype(bf16), grad)
            dk = dot(grad_score, query[:, :HD])
            if first:
                dv_all[at, :] = dv
                dk_all[at, :] = dk
            else:
                dv_all[at, :] += dv
                dk_all[at, :] += dk
            return dq_turned + dot(k_turned[:, at], grad_score)

        dq_turned = jnp.zeros((HD, tile), f32)
        for t in range(tile // tile):
            at = pl.ds(m * tile + t * tile, tile)
            scores = diagonal_scores(k_all[at, :], query, t * tile)
            dq_turned = key_tile(at, scores, dq_turned, True)

        def step(j, dq_turned):
            at = pl.ds(pl.multiple_of(j * tile, HD), tile)
            return key_tile(at, dot_nt(k_all[at, :], query), dq_turned, False)

        if m:
            dq_turned = lax.fori_loop(0, m * tile // tile, step, dq_turned)
        o_all[here, :] = (dq_turned * INV_ROOT).T.astype(bf16)

    for d, half, rows, at in place_rows(scalars, peers, span):
        grad_refs[d][0, rows, :] = (dk_all[at, :] * INV_ROOT).astype(bf16)
        grad_refs[d][1, rows, :] = dv_all[at, :].astype(bf16)
        grad_refs[d][2, rows, :] = o_all[at, :]


def attention_forward(scalars, heads, codes, extra, groups, pieces, chunks):
    peers = len(heads)
    rows = heads[0].shape[1]
    span = rows // 2
    key_rows = groups * peers * rows
    meta = (peers, groups, span, pieces, chunks, len(extra))
    operands = [*heads, *codes, *extra]
    out_shape = [jax.ShapeDtypeStruct((rows, HD), bf16)] * peers
    n_query = 2 * peers if groups > 1 else peers
    out_shape.append(jax.ShapeDtypeStruct((n_query, 1, 2 * peers * span // n_query), f32))
    if groups == 1:
        body, q_shape, o_shape = forward_group_kernel, (key_rows, 2 * HD), (key_rows, HD)
    else:
        body, q_shape, o_shape = (
            forward_kernel,
            (2 * peers, span, 2 * HD),
            (2 * peers, span, HD),
        )
    outs = pl.pallas_call(
        functools.partial(body, meta),
        grid_spec=pltpu.PrefetchScalarGridSpec(
            num_scalar_prefetch=1,
            grid=(1,),
            in_specs=[whole_spec(x) for x in operands],
            out_specs=[whole_spec(x) for x in out_shape],
            scratch_shapes=[
                pltpu.VMEM(q_shape, bf16),
                pltpu.VMEM(o_shape, bf16),
                pltpu.VMEM((key_rows, 2 * HD), bf16),
                pltpu.VMEM((HD, key_rows), bf16),
            ],
        ),
        out_shape=out_shape,
        compiler_params=pltpu.CompilerParams(vmem_limit_bytes=VMEM_LIMIT),
        cost_estimate=cost(6 * peers * rows * key_rows // 2 * HD, 8 * key_rows * HD),
        name="attend",
    )(scalars, *operands)
    return outs[:-1], outs[-1]


def backward_kernel(meta, scalars, *refs):
    peers, groups, span, pieces, chunks, n_extra = meta
    take = taker(refs)
    heads, code_refs, kv_refs = take(peers), take(peers), take(n_extra)
    o_refs, do_refs, (lse_ref,) = take(peers), take(peers), take(1)
    grad_refs = take(peers)
    dkv_refs = take(1 if groups > 1 else 0)
    q_all, o_all, do_all, k_all, k_turned, v_all, dk_all, dv_all = take(8)
    key_of, value_of, key_code_of = block_readers(groups, heads, kv_refs, code_refs)
    n_query = 2 * peers
    own_piece = scalars[n_query + 2 * groups * peers]

    for g in range(groups):
        for d in range(peers):
            for half in range(2):
                rows = pl.ds(half * span, span)
                place = scalars[n_query + (g * peers + d) * 2 + half]
                at = pl.ds(pl.multiple_of(place * span, HD), span)
                key = key_of(g, d, rows)
                k_all[at, :HD] = key
                k_all[at, HD:] = key_marks(key_code_of(g, d, rows))
                k_turned[:, at] = key.astype(f32).T.astype(bf16)
                v_all[at, :] = value_of(g, d, rows)
    dk_all[...] = jnp.zeros_like(dk_all)
    dv_all[...] = jnp.zeros_like(dv_all)
    share = 2 * span // pieces
    part = share // chunks
    for d in range(peers):
        for half in range(2):
            rows = pl.ds(half * span, span)
            q_all[2 * d + half, :, :HD] = heads[d][2, rows, :]
            q_all[2 * d + half, :, HD:] = query_marks(code_refs[d][rows, :])
        for piece in range(pieces):
            origin = lax.rem(own_piece + pieces - piece, pieces)
            for c in range(chunks):
                source = pl.ds((c * pieces + piece) * part, part)
                row = (2 * d * span) + piece * share + c * part
                o_all[row : row + part, :] = o_refs[d][source, :]
                row = (2 * d * span) + origin * share + c * part
                do_all[pl.ds(pl.multiple_of(row, 16), part), :] = do_refs[d][source, :]

    def one_span(i, carry):
        place = scalars[i]
        query = q_all[i]
        rows = pl.ds(pl.multiple_of(i * span, HD), span)
        grad = do_all[rows, :]
        product = grad.astype(f32) * o_all[rows, :].astype(f32)
        high = product.astype(bf16)
        rest = (product - high.astype(f32)).astype(bf16)
        ones = jnp.ones((16, HD), bf16)
        delta = (dot_nt(ones, high) + dot_nt(ones, rest))[:1, :]
        lse = lse_ref[i]

        def key_span(at, scores, dq_turned):
            probs = jnp.exp(scores * INV_ROOT - lse)
            grad_prob = dot_nt(v_all[at, :], grad)
            grad_score = (probs * (grad_prob - delta)).astype(bf16)
            dv_all[at, :] += dot(probs.astype(bf16), grad)
            dk_all[at, :] += dot(grad_score, query[:, :HD])
            return dq_turned + dot(k_turned[:, at], grad_score)

        at = pl.ds(pl.multiple_of(place * span, HD), span)
        dq_turned = key_span(
            at, diagonal_scores(k_all[at, :], query), jnp.zeros((HD, span), f32)
        )

        def step(j, dq_turned):
            at = pl.ds(pl.multiple_of(j * span, HD), span)
            return key_span(at, dot_nt(k_all[at, :], query), dq_turned)

        dq_turned = lax.fori_loop(0, place, step, dq_turned)
        o_all[rows, :] = (dq_turned * INV_ROOT).T.astype(bf16)
        return carry

    lax.fori_loop(0, n_query, one_span, 0)
    at_query = 2 if groups == 1 else 0
    for d in range(peers):
        grad_refs[d][at_query] = o_all[2 * d * span : 2 * (d + 1) * span, :]
    for g in range(groups):
        for d in range(peers):
            for half in range(2):
                rows = pl.ds(half * span, span)
                place = scalars[n_query + (g * peers + d) * 2 + half]
                at = pl.ds(pl.multiple_of(place * span, HD), span)
                grad_key = (dk_all[at, :] * INV_ROOT).astype(bf16)
                grad_value = dv_all[at, :].astype(bf16)
                if groups == 1:
                    grad_refs[d][0, rows, :] = grad_key
                    grad_refs[d][1, rows, :] = grad_value
                else:
                    dkv_refs[0][g, d, 0, rows, :] = grad_key
                    dkv_refs[0][g, d, 1, rows, :] = grad_value


def attention_backward(scalars, heads, codes, extra, o, grads, lse, groups, pieces, chunks):
    peers = len(heads)
    rows = heads[0].shape[1]
    span = rows // 2
    key_rows = groups * peers * rows
    meta = (peers, groups, span, pieces, chunks, len(extra))
    operands = [*heads, *codes, *extra, *o, *grads, lse]
    parts = 3 if groups == 1 else 1
    out_shape = [jax.ShapeDtypeStruct((parts, rows, HD), bf16)] * peers
    if groups > 1:
        out_shape.append(jax.ShapeDtypeStruct(extra[0].shape, bf16))
    if groups == 1:
        body, q_shape = backward_group_kernel, (key_rows, 2 * HD)
    else:
        body, q_shape = backward_kernel, (2 * peers, span, 2 * HD)
    outs = pl.pallas_call(
        functools.partial(body, meta),
        grid_spec=pltpu.PrefetchScalarGridSpec(
            num_scalar_prefetch=1,
            grid=(1,),
            in_specs=[whole_spec(x) for x in operands],
            out_specs=[whole_spec(x) for x in out_shape],
            scratch_shapes=[
                pltpu.VMEM(q_shape, bf16),
                pltpu.VMEM((peers * rows, HD), bf16),
                pltpu.VMEM((peers * rows, HD), bf16),
                pltpu.VMEM((key_rows, 2 * HD), bf16),
                pltpu.VMEM((HD, key_rows), bf16),
                pltpu.VMEM((key_rows, HD), bf16),
                pltpu.VMEM((key_rows, HD), f32),
                pltpu.VMEM((key_rows, HD), f32),
            ],
        ),
        out_shape=out_shape,
        compiler_params=pltpu.CompilerParams(vmem_limit_bytes=VMEM_LIMIT),
        cost_estimate=cost(14 * peers * rows * key_rows // 2 * HD, 16 * key_rows * HD),
        name="attend_back",
    )(scalars, *operands)
    if groups == 1:
        return outs, None
    return outs[:peers], outs[peers]


def split_low(value):
    high = value.astype(bf16)
    return high, (value - high.astype(f32)).astype(bf16)


def low_rank(a_t, b):
    a_high, a_rest = split_low(a_t)
    b_high, b_rest = split_low(b * SCALING)
    a_cat = jnp.concatenate([a_high, a_rest, a_high], axis=0)
    b_cat = jnp.concatenate([b_high, b_high, b_rest], axis=0)
    return dot_tn(a_cat, b_cat)


def separate(both):
    rows, width = both.shape
    both = both.reshape(rows, -1, 2, HD)
    return both[:, :, 0].reshape(rows, width // 2), both[:, :, 1].reshape(rows, width // 2)


def merge_kernel(starts, out_w, out_a, out_b, down_w, down_a, down_b, gate_w, up_w, gate_a, up_a,
                 gate_b, up_b, gate_m, up_m, out_square, out_cross, down_square, down_cross,
                 down_low, pair_low, pair_cross, pair_column, pair_scale, mixed_m, mixed_b):
    step = pl.program_id(0)
    down_start, pair_start = starts

    def columns(w_ref, a_ref, b_ref, square_ref, cross_ref, low_ref):
        merged = w_ref[...].astype(f32) + low_rank(a_ref[...], b_ref[...])
        low = merged.astype(bf16)
        if low_ref is not None:
            low_ref[...] = low
        square_ref[...] = jnp.sum(merged * merged, axis=0, keepdims=True)
        cross_ref[...] = dot(a_ref[...].astype(bf16), low)

    @pl.when(step < down_start)
    def _():
        columns(out_w, out_a, out_b, out_square, out_cross, None)

    @pl.when((step >= down_start) & (step < pair_start))
    def _():
        columns(down_w, down_a, down_b, down_square, down_cross, down_low)

    sides = ((gate_w, gate_a, gate_b, gate_m), (up_w, up_a, up_b, up_m))
    blocks = [
        (side, slice(j * HD, (j + 1) * HD), pl.ds((2 * j + side) * HD, HD))
        for side in range(2)
        for j in range(gate_w.shape[1] // HD)
    ]

    @pl.when(step == pair_start)
    def _():
        pair_column[...] = jnp.zeros_like(pair_column)
        pair_cross[...] = jnp.zeros_like(pair_cross)
        for side, source, at in blocks:
            mixed_b[:, at] = sides[side][2][:, source]
            mixed_m[:, at] = sides[side][3][:, source]

    @pl.when(step >= pair_start)
    def _():
        results = []
        for w_ref, a_ref, b_ref, _ in sides:
            merged = w_ref[...].astype(f32) + low_rank(a_ref[...], b_ref[...])
            low = merged.astype(bf16)
            square = jnp.sum(merged * merged, axis=0, keepdims=True)
            results.append((low, square, dot(a_ref[...].astype(bf16), low)))
        for side, source, at in blocks:
            low, square, cross = results[side]
            pair_low[:, at] = low[:, source]
            pair_column[:, at] += square[:, source]
            pair_cross[:, at] += cross[:, source]

    @pl.when(step == pl.num_programs(0) - 1)
    def _():
        column = jnp.sqrt(pair_column[...])
        pair_column[...] = column
        pair_scale[...] = mixed_m[...] / column


def merge_others(out, down, gate, up):
    step = 8 * HD
    rows = 2 * HD
    near, wide = out[0].shape
    ff = down[0].shape[0]
    depth, width = gate[0].shape
    n_columns = wide // step
    starts = (n_columns, 2 * n_columns)
    n_pair = depth // rows
    at_out = lambda i: jnp.minimum(i, n_columns - 1)
    at_down = lambda i: jnp.clip(i - starts[0], 0, n_columns - 1)
    at_pair = lambda i: jnp.clip(i - starts[1], 0, n_pair - 1)
    cut = lambda height, at: pl.BlockSpec((height, step), lambda i: (0, at(i)))
    fixed = lambda *shape: pl.BlockSpec(shape, lambda i: (0,) * len(shape))
    pair_rows = lambda lanes: pl.BlockSpec((rows, lanes), lambda i: (at_pair(i), 0))
    turned = pl.BlockSpec((RANK, rows), lambda i: (0, at_pair(i)))
    shape = jax.ShapeDtypeStruct
    return pl.pallas_call(
        functools.partial(merge_kernel, starts),
        grid=(starts[1] + n_pair,),
        in_specs=[
            cut(near, at_out),
            fixed(RANK, near),
            cut(RANK, at_out),
            cut(ff, at_down),
            fixed(RANK, ff),
            cut(RANK, at_down),
            pair_rows(width),
            pair_rows(width),
            turned,
            turned,
            fixed(RANK, width),
            fixed(RANK, width),
            fixed(1, width),
            fixed(1, width),
        ],
        out_specs=[
            cut(1, at_out),
            cut(RANK, at_out),
            cut(1, at_down),
            cut(RANK, at_down),
            cut(ff, at_down),
            pair_rows(2 * width),
            fixed(RANK, 2 * width),
            fixed(1, 2 * width),
            fixed(1, 2 * width),
            fixed(1, 2 * width),
            fixed(RANK, 2 * width),
        ],
        out_shape=[
            shape((1, wide), f32),
            shape((RANK, wide), f32),
            shape((1, wide), f32),
            shape((RANK, wide), f32),
            shape((ff, wide), bf16),
            shape((depth, 2 * width), bf16),
            shape((RANK, 2 * width), f32),
            shape((1, 2 * width), f32),
            shape((1, 2 * width), f32),
            shape((1, 2 * width), f32),
            shape((RANK, 2 * width), f32),
        ],
        compiler_params=pltpu.CompilerParams(vmem_limit_bytes=VMEM_LIMIT),
        cost_estimate=cost(4 * depth * width * RANK, 8 * depth * width),
        name="merge_others",
    )(*out, *down, gate[0], up[0], gate[1], up[1], gate[2], up[2], gate[3], up[3])


def heads_kernel(scalars, x_ref, gain_ref, a_ref, b_ref, m_ref, cos_ref, sin_ref,
                 wk_hbm, wv_hbm, wq_hbm, *refs):
    take = taker(refs)
    peers = len(refs) - 12
    blocks = take(peers)
    normed_ref, low_ref, raw_ref, column_ref, scale_ref, cross_ref = take(6)
    x_all, w_all, merged_all, column_now, scale_now, sem = take(6)
    step = pl.program_id(0)
    rows = x_ref.shape[0]
    sources = (wk_hbm, wv_hbm, wq_hbm)

    def copy(number):
        return pltpu.make_async_copy(sources[number], w_all.at[number], sem.at[number])

    def merge(layer):
        slot = lax.rem(layer, 2)
        merged = w_all[layer].astype(f32) + low_rank(a_ref[layer], b_ref[layer])
        low = merged.astype(bf16)
        merged_all[slot] = low
        low_ref[...] = low
        column = jnp.sqrt(jnp.sum(merged * merged, axis=0, keepdims=True))
        scale = m_ref[layer] / column
        column_ref[...] = column
        scale_ref[...] = scale
        scale_now[slot] = scale

    @pl.when(step == 0)
    def _():
        for number in range(3):
            copy(number).start()
        part = rows // 4
        for i in range(4):
            at = pl.ds(i * part, part)
            x = x_ref[at, :].astype(f32)
            inverse = lax.rsqrt(jnp.mean(x * x, axis=-1, keepdims=True) + EPS)
            normed = (x * inverse * gain_ref[...]).astype(bf16)
            x_all[at, :] = normed
            normed_ref[at, :] = normed
        x_all[rows:, :] = a_ref[0].astype(bf16)
        copy(0).wait()
        merge(0)

    for number in (1, 2):

        @pl.when(step == number)
        def _(number=number):
            copy(number).wait()

    @pl.when(step > 0)
    def _():
        layer = step - 1
        slot = lax.rem(layer, 2)
        product = dot(x_all[...], merged_all[slot])
        scale = scale_now[slot]
        x_next = a_ref[jnp.minimum(step, 2)].astype(bf16)
        merge(jnp.minimum(step, 2))
        cross_ref[...] = product[rows:, :]
        raw = product[:rows, :]
        raw_ref[...] = raw.astype(bf16)
        value = raw * scale
        for t in range(peers):
            head = value[:, t * HD : (t + 1) * HD]
            rotated = head * cos_ref[...] + pltpu.roll(head, HALF, 1) * sin_ref[...]
            head = jnp.where(layer != 1, rotated, head).astype(bf16)
            place = t ^ scalars[0]
            for d, block in enumerate(blocks):

                @pl.when(place == d)
                def _(block=block, head=head):
                    block[layer] = head

        x_all[rows:, :] = x_next


def project_heads(order, x, gain, weights, a_t, b, m, cosine, sine):
    rows, depth = x.shape
    width = weights[0].shape[1]
    heads = width // HD
    merged_at = lambda i, s: (0, jnp.minimum(i, 2))
    done_at = lambda i, s: (0, jnp.maximum(i - 1, 0))
    fixed = lambda *shape: pl.BlockSpec(shape, lambda i, s: (0,) * len(shape))
    out_shape = [jax.ShapeDtypeStruct((3, rows, HD), bf16)] * heads
    out_shape += [
        jax.ShapeDtypeStruct((rows, depth), bf16),
        jax.ShapeDtypeStruct((depth, 3 * width), bf16),
        jax.ShapeDtypeStruct((rows, 3 * width), bf16),
        jax.ShapeDtypeStruct((1, 3 * width), f32),
        jax.ShapeDtypeStruct((1, 3 * width), f32),
        jax.ShapeDtypeStruct((RANK, 3 * width), f32),
    ]
    outs = pl.pallas_call(
        heads_kernel,
        grid_spec=pltpu.PrefetchScalarGridSpec(
            num_scalar_prefetch=1,
            grid=(4,),
            in_specs=[
                fixed(rows, depth),
                fixed(1, depth),
                fixed(3, RANK, depth),
                fixed(3, RANK, width),
                fixed(3, 1, width),
                fixed(rows, HD),
                fixed(rows, HD),
            ]
            + [pl.BlockSpec(memory_space=pl.ANY)] * 3,
            out_specs=[fixed(3, rows, HD)] * heads
            + [
                fixed(rows, depth),
                pl.BlockSpec((depth, width), merged_at),
                pl.BlockSpec((rows, width), done_at),
                pl.BlockSpec((1, width), merged_at),
                pl.BlockSpec((1, width), merged_at),
                pl.BlockSpec((RANK, width), done_at),
            ],
            scratch_shapes=[
                pltpu.VMEM((rows + RANK, depth), bf16),
                pltpu.VMEM((3, depth, width), bf16),
                pltpu.VMEM((2, depth, width), bf16),
                pltpu.VMEM((2, 1, width), f32),
                pltpu.VMEM((2, 1, width), f32),
                pltpu.SemaphoreType.DMA((3,)),
            ],
        ),
        out_shape=out_shape,
        compiler_params=pltpu.CompilerParams(vmem_limit_bytes=VMEM_LIMIT),
        cost_estimate=cost(6 * rows * depth * width, 16 * rows * depth),
        name="project_heads",
    )(order, x, gain, a_t, b, m, cosine, sine, *weights)
    return outs[:heads], *outs[heads:]


def assemble_kernel(peers, chunks, scalars, *refs):
    take = taker(refs)
    heads = take(peers)
    out_ref, down_ref, a_ref = take(3)
    near_refs = refs[peers + 3 :]
    width = a_ref.shape[1]
    parts = out_ref.shape[1] // width
    part = heads[0].shape[0] // chunks
    for d in range(peers):
        at = pl.ds(pl.multiple_of((scalars[0] ^ d) * HD, HD), HD)
        for c in range(chunks):
            near_refs[c][:part, at] = heads[d][c * part : (c + 1) * part, :]
    rows = []
    for ref in (out_ref, down_ref):
        high = ref[...].astype(bf16).astype(f32)
        for value in (high, ref[...] - high):
            rows += [value[:, j * width : (j + 1) * width] for j in range(parts)]
    near_refs[0][part : part + RANK, :] = jnp.concatenate(rows, axis=0).astype(bf16)
    near_refs[0][part + RANK :, :] = a_ref[...].astype(bf16)


def assemble(order, heads, square_out, square_down, a_t, chunks):
    peers = len(heads)
    part = heads[0].shape[0] // chunks
    width = peers * HD
    operands = [*heads, square_out, square_down, a_t]
    heights = [part + 2 * RANK] + [part] * (chunks - 1)
    out_shape = [jax.ShapeDtypeStruct((height, width), bf16) for height in heights]
    return pl.pallas_call(
        functools.partial(assemble_kernel, peers, chunks),
        grid_spec=pltpu.PrefetchScalarGridSpec(
            num_scalar_prefetch=1,
            grid=(1,),
            in_specs=[whole_spec(x) for x in operands],
            out_specs=[whole_spec(x) for x in out_shape],
        ),
        out_shape=out_shape,
        compiler_params=pltpu.CompilerParams(vmem_limit_bytes=VMEM_LIMIT),
        cost_estimate=cost(0, 0),
        name="assemble",
    )(order, *operands)


def unpack_kernel(size, scalars, *refs):
    take = taker(refs)
    blocks, m_refs = take(size), take(2)
    column_refs, scale_refs, (a_ref,) = take(2), take(2), take(1)
    width = blocks[0].shape[1]
    total = jnp.zeros((RANK, width), f32)
    for device in range(size):
        value = blocks[0][:RANK, :]
        for c in range(1, size):
            here = lax.rem(scalars[0] + c, size) == device
            value = jnp.where(here, blocks[c][:RANK, :], value)
        total = total + value.astype(f32)
    for side in range(2):
        for j in range(size):
            row = 2 * side * size + j
            square = total[row : row + 1, :] + total[row + size : row + size + 1, :]
            at = slice(j * width, (j + 1) * width)
            column = jnp.sqrt(square)
            column_refs[side][:, at] = column
            scale_refs[side][:, at] = m_refs[side][:, at] / column
    for c in range(size):
        device = lax.rem(scalars[0] + c, size)
        at = pl.ds(pl.multiple_of(device * width, HD), width)
        a_ref[:, at] = blocks[c][RANK:, :]


def unpack(k, blocks, rows, m_out, m_down):
    size = len(blocks)
    width = blocks[0].shape[1]
    wide = size * width
    row = jax.ShapeDtypeStruct((1, wide), f32)
    out_shape = [row] * 4 + [jax.ShapeDtypeStruct((RANK, wide), bf16)]
    tail = pl.BlockSpec((2 * RANK, width), lambda i, s: (rows // (2 * RANK), 0))
    return pl.pallas_call(
        functools.partial(unpack_kernel, size),
        grid_spec=pltpu.PrefetchScalarGridSpec(
            num_scalar_prefetch=1,
            grid=(1,),
            in_specs=[tail] * size + [whole_spec(m_out), whole_spec(m_down)],
            out_specs=[whole_spec(x) for x in out_shape],
        ),
        out_shape=out_shape,
        compiler_params=pltpu.CompilerParams(vmem_limit_bytes=VMEM_LIMIT),
        cost_estimate=cost(0, 0),
        name="unpack",
    )(k, *blocks, m_out, m_down)


def out_kernel(scalars, *refs):
    take = taker(refs)
    size = len(refs) - 13
    x_refs = take(size)
    w_ref, a_ref, hid_ref, b_ref, scale_ref, gain_ref = take(6)
    hnorm_ref, resid_ref, raw_own_ref, low_ref, own_ref = take(5)
    total, through = take(2)
    step = pl.program_id(0)

    @pl.when(step == 0)
    def _():
        total[...] = jnp.zeros_like(total)
        through[...] = jnp.zeros_like(through)

    for c, x_ref in enumerate(x_refs):

        @pl.when(step == c)
        def _(x_ref=x_ref):
            x = x_ref[...]
            total[...] += dot(x, w_ref[...])
            through[...] += dot_nt(x, a_ref[...])
            part, width = own_ref.shape[0], x_ref.shape[1]
            mine = pl.ds(pl.multiple_of(scalars[0] * part, 16), part)
            device = lax.rem(scalars[0] + c, size)
            at = pl.ds(pl.multiple_of(device * width, HD), width)
            own_ref[:, at] = x_ref[mine, :]

    @pl.when(step == size - 1)
    def _():
        part = hid_ref.shape[2]
        for piece in range(size):
            at = pl.ds(piece * part, part)
            low = through[at, :].astype(bf16)
            raw = total[at, :] + dot(low, b_ref[...])
            resid = hid_ref[piece, 0].astype(f32) + raw * scale_ref[...]
            inverse = lax.rsqrt(jnp.mean(resid * resid, axis=-1, keepdims=True) + EPS)
            hnorm_ref[at, :] = (resid * inverse * gain_ref[...]).astype(bf16)

            @pl.when(scalars[0] == piece)
            def _(resid=resid, raw=raw, low=low):
                resid_ref[...] = resid
                raw_own_ref[...] = raw
                low_ref[...] = low


def out_project(k, chunk, x, w, a_t, hidden, b2, scale, gain):
    size = len(x)
    width, wide = x[0].shape[1], w.shape[1]
    part = hidden.shape[2]
    rows = size * part
    fixed = lambda *shape: pl.BlockSpec(shape, lambda i, s: (0,) * len(shape))
    return pl.pallas_call(
        out_kernel,
        grid_spec=pltpu.PrefetchScalarGridSpec(
            num_scalar_prefetch=1,
            grid=(size,),
            in_specs=[fixed(rows, width)] * size
            + [
                pl.BlockSpec((width, wide), lambda i, s: (lax.rem(i + s[0], size), 0)),
                pl.BlockSpec((RANK, width), lambda i, s: (0, lax.rem(i + s[0], size))),
                pl.BlockSpec((size, 1, part, wide), lambda i, s: (0, chunk, 0, 0)),
                fixed(RANK, wide),
                fixed(1, wide),
                fixed(1, wide),
            ],
            out_specs=[
                fixed(rows, wide),
                fixed(part, wide),
                fixed(part, wide),
                fixed(part, RANK),
                fixed(part, size * width),
            ],
            scratch_shapes=[
                pltpu.VMEM((rows, wide), f32),
                pltpu.VMEM((rows, RANK), f32),
            ],
        ),
        out_shape=[
            jax.ShapeDtypeStruct((rows, wide), bf16),
            jax.ShapeDtypeStruct((part, wide), f32),
            jax.ShapeDtypeStruct((part, wide), f32),
            jax.ShapeDtypeStruct((part, RANK), bf16),
            jax.ShapeDtypeStruct((part, size * width), bf16),
        ],
        compiler_params=pltpu.CompilerParams(vmem_limit_bytes=VMEM_LIMIT),
        cost_estimate=cost(2 * rows * width * size * wide, 2 * width * size * wide),
        name="out_project",
    )(k, *x, w, a_t, hidden, b2, scale, gain)


def hidden_kernel(sizes, hnorm_ref, cot_ref, down_scale_ref, scale_ref, w_hbm, wd_hbm,
                  act_ref, dz_ref, g_ref, dh_ref, total, w_all, wd_all, dz_down, sem, down_sem):
    rows = hnorm_ref.shape[0]
    starts = [sum(sizes[:j]) for j in range(len(sizes))]

    def copies(j):
        both = pl.ds(2 * starts[j], 2 * sizes[j])
        one = pl.ds(starts[j], sizes[j])
        return (
            pltpu.make_async_copy(wd_hbm.at[one, :], wd_all.at[one, :], down_sem.at[j]),
            pltpu.make_async_copy(w_hbm.at[:, both], w_all.at[:, both], sem.at[j]),
        )

    for j in range(len(sizes)):
        for copy in copies(j):
            copy.start()
    part = rows // cot_ref.shape[0]
    for i in range(cot_ref.shape[0]):
        cot = cot_ref[i, 0].astype(f32)
        dz_down[i * part : (i + 1) * part, :] = (cot * down_scale_ref[...]).astype(bf16)

    def products(j):
        for copy in copies(j):
            copy.wait()
        both = slice(2 * starts[j], 2 * (starts[j] + sizes[j]))
        one = slice(starts[j], starts[j] + sizes[j])
        return dot(hnorm_ref[...], w_all[:, both]), dot_nt(dz_down[...], wd_all[one, :])

    ready = products(0)
    for j in range(len(sizes)):
        v, dact_all = ready
        if j + 1 < len(sizes):
            ready = products(j + 1)
        for i in range(sizes[j] // HD):
            hidden = starts[j] + i * HD
            gate_at = slice(2 * hidden, 2 * hidden + HD)
            up_at = slice(2 * hidden + HD, 2 * hidden + 2 * HD)
            raw_gate = v[:, 2 * i * HD : (2 * i + 1) * HD]
            raw_up = v[:, (2 * i + 1) * HD : (2 * i + 2) * HD]
            dact = dact_all[:, i * HD : (i + 1) * HD]
            scale_gate, scale_up = scale_ref[:, gate_at], scale_ref[:, up_at]
            gate = raw_gate * scale_gate
            up = raw_up * scale_up
            sigmoid = 1.0 / (1.0 + jnp.exp(-gate))
            silu = gate * sigmoid
            dgate = dact * up * (sigmoid + silu * (1.0 - sigmoid))
            dup = dact * silu
            act_ref[:, hidden : hidden + HD] = (silu * up).astype(bf16)
            g_ref[:, gate_at] = jnp.sum(dgate * raw_gate, axis=0, keepdims=True)
            g_ref[:, up_at] = jnp.sum(dup * raw_up, axis=0, keepdims=True)
            dz_ref[:, gate_at] = (dgate * scale_gate).astype(bf16)
            dz_ref[:, up_at] = (dup * scale_up).astype(bf16)
        both = slice(2 * starts[j], 2 * (starts[j] + sizes[j]))
        product = dot_nt(dz_ref[:, both], w_all[:, both])
        if j == 0:
            total[...] = product
        elif j + 1 < len(sizes):
            total[...] += product
        else:
            dh_ref[...] = (total[...] + product).astype(bf16)


def feed_forward(chunk, hnorm, cotangent, down_scale, scale, w, wd):
    rows, depth = hnorm.shape
    ff = wd.shape[0]
    size, _, part, _ = cotangent.shape
    sizes = [2 * HD] * (ff // (2 * HD)) + [HD] * (ff // HD % 2)
    fixed = lambda *shape: pl.BlockSpec(shape, lambda i: (0,) * len(shape))
    return pl.pallas_call(
        functools.partial(hidden_kernel, sizes),
        grid=(1,),
        in_specs=[
            fixed(rows, depth),
            pl.BlockSpec((size, 1, part, depth), lambda i: (0, chunk, 0, 0)),
            fixed(1, depth),
            fixed(1, 2 * ff),
            pl.BlockSpec(memory_space=pl.ANY),
            pl.BlockSpec(memory_space=pl.ANY),
        ],
        out_specs=[fixed(rows, ff), fixed(rows, 2 * ff), fixed(1, 2 * ff), fixed(rows, depth)],
        out_shape=[
            jax.ShapeDtypeStruct((rows, ff), bf16),
            jax.ShapeDtypeStruct((rows, 2 * ff), bf16),
            jax.ShapeDtypeStruct((1, 2 * ff), f32),
            jax.ShapeDtypeStruct((rows, depth), bf16),
        ],
        scratch_shapes=[
            pltpu.VMEM((rows, depth), f32),
            pltpu.VMEM((depth, 2 * ff), bf16),
            pltpu.VMEM((ff, depth), bf16),
            pltpu.VMEM((rows, depth), bf16),
            pltpu.SemaphoreType.DMA((len(sizes),)),
            pltpu.SemaphoreType.DMA((len(sizes),)),
        ],
        compiler_params=pltpu.CompilerParams(vmem_limit_bytes=VMEM_LIMIT),
        cost_estimate=cost(10 * rows * depth * ff, 6 * depth * ff),
        name="feed_forward",
    )(hnorm, cotangent, down_scale, scale, w, wd)


def back_out_kernel(scalars, *refs):
    take = taker(refs)
    earlier = take(len(refs) - 18)
    piece_ref, cot_ref, resid_ref, raw_ref, gain_ref, scale_ref = take(6)
    b_ref, own_ref, low_ref, w_ref, a_ref = take(5)
    dattn_ref, dresid_ref, dz_ref, g_ref, ap_ref, pb_ref = take(6)
    (through,) = take(1)

    @pl.when(pl.program_id(0) == 0)
    def _():
        grad = piece_ref[...].astype(f32)
        resid = resid_ref[...]
        inverse = lax.rsqrt(jnp.mean(resid * resid, axis=-1, keepdims=True) + EPS)
        scaled = grad * gain_ref[...]
        lean = jnp.mean(resid * scaled, axis=-1, keepdims=True)
        dresid = cot_ref[0, 0].astype(f32) + inverse * scaled
        dresid = dresid - resid * (inverse * inverse * inverse * lean)
        dresid_ref[...] = dresid
        dz = (dresid * scale_ref[...]).astype(bf16)
        dz_ref[...] = dz
        through[...] = dot_nt(dz, b_ref[...]).astype(bf16)
        sums = [
            jnp.sum(dresid * raw_ref[...], axis=0, keepdims=True),
            dot_tn(low_ref[...], dz),
            dot_tn(through[...], own_ref[...]),
        ]
        for i, ref in enumerate((g_ref, ap_ref, pb_ref)):
            ref[...] = sums[i] + earlier[i][...] if earlier else sums[i]

    dattn = dot_nt(dz_ref[...], w_ref[...]) + dot(through[...], a_ref[...])
    dattn_ref[0] = dattn.astype(bf16)


def back_out(k, chunk, piece, cotangent, resid, raw, gain, scale, b, own, low, w, a2_t, earlier):
    size = cotangent.shape[0]
    part, wide = resid.shape
    width = w.shape[0] // size
    fixed = lambda *shape: pl.BlockSpec(shape, lambda i, s: (0,) * len(shape))
    return pl.pallas_call(
        back_out_kernel,
        grid_spec=pltpu.PrefetchScalarGridSpec(
            num_scalar_prefetch=1,
            grid=(size,),
            in_specs=[fixed(*x.shape) for x in earlier]
            + [
                fixed(part, wide),
                pl.BlockSpec((1, 1, part, wide), lambda i, s: (s[0], chunk, 0, 0)),
                fixed(part, wide),
                fixed(part, wide),
                fixed(1, wide),
                fixed(1, wide),
                fixed(RANK, wide),
                fixed(*own.shape),
                fixed(part, RANK),
                pl.BlockSpec((width, wide), lambda i, s: (lax.rem(i + s[0], size), 0)),
                pl.BlockSpec((RANK, width), lambda i, s: (0, lax.rem(i + s[0], size))),
            ],
            out_specs=[
                pl.BlockSpec((1, part, width), lambda i, s: (i, 0, 0)),
                fixed(part, wide),
                fixed(part, wide),
                fixed(1, wide),
                fixed(RANK, wide),
                fixed(RANK, size * width),
            ],
            scratch_shapes=[pltpu.VMEM((part, RANK), bf16)],
        ),
        out_shape=[
            jax.ShapeDtypeStruct((size, part, width), bf16),
            jax.ShapeDtypeStruct((part, wide), f32),
            jax.ShapeDtypeStruct((part, wide), bf16),
            jax.ShapeDtypeStruct((1, wide), f32),
            jax.ShapeDtypeStruct((RANK, wide), f32),
            jax.ShapeDtypeStruct((RANK, size * width), f32),
        ],
        compiler_params=pltpu.CompilerParams(vmem_limit_bytes=VMEM_LIMIT),
        cost_estimate=cost(2 * part * width * size * wide, 2 * width * size * wide),
        name="back_out",
    )(k, *earlier, piece, cotangent, resid, raw, gain, scale, b, own, low, w, a2_t)


def unproject_kernel(heads, scalars, cos_ref, sin_ref, raw_ref, scale_ref, w_ref, *refs):
    take = taker(refs)
    grads = take(heads)
    dz_ref, g_ref, out_ref = refs[heads:]
    width = heads * HD

    @pl.when(pl.program_id(0) == 0)
    def _():
        for layer in range(3):
            for d in range(heads):
                at = pl.ds(pl.multiple_of(layer * width + (scalars[0] ^ d) * HD, HD), HD)
                grad = grads[d][layer].astype(f32)
                if layer != 1:
                    grad = grad * cos_ref[...] - pltpu.roll(grad, HALF, 1) * sin_ref[...]
                raw = raw_ref[:, at].astype(f32)
                g_ref[:, at] = jnp.sum(grad * raw, axis=0, keepdims=True)
                dz_ref[:, at] = (grad * scale_ref[:, at]).astype(bf16)

    out_ref[...] = dot_nt(dz_ref[...], w_ref[...]).astype(bf16)


def unproject(order, cosine, sine, raw, scale, w, grads):
    operands = [cosine, sine, raw, scale]
    rows, wide = raw.shape
    depth = w.shape[0]
    step = 2 * HD
    return pl.pallas_call(
        functools.partial(unproject_kernel, len(grads)),
        grid_spec=pltpu.PrefetchScalarGridSpec(
            num_scalar_prefetch=1,
            grid=(depth // step,),
            in_specs=[whole_spec(x) for x in operands]
            + [pl.BlockSpec((step, wide), lambda i, s: (i, 0))]
            + [whole_spec(x) for x in grads],
            out_specs=[
                whole_spec(raw),
                whole_spec(scale),
                pl.BlockSpec((rows, step), lambda i, s: (0, i)),
            ],
        ),
        out_shape=[
            jax.ShapeDtypeStruct(raw.shape, bf16),
            jax.ShapeDtypeStruct(scale.shape, f32),
            jax.ShapeDtypeStruct((rows, depth), bf16),
        ],
        compiler_params=pltpu.CompilerParams(vmem_limit_bytes=VMEM_LIMIT),
        cost_estimate=cost(2 * rows * wide * depth, 2 * wide * depth),
        name="unproject",
    )(order, *operands, w, *grads)


def shares_kernel(count, chunks, span, *refs):
    take = taker(refs)
    x_refs, dz_refs = take(chunks), take(chunks)
    a_ref, b_ref, w_ref, cross_ref, g_ref, m_ref, column_ref = take(7)
    share_a_ref, share_b_ref = take(2)
    low, up, radial = take(3)
    step = pl.program_id(0)
    wide = b_ref.shape[1]

    @pl.when(step == 0)
    def _():
        up[...] = jnp.zeros_like(up)
        radial[...] = jnp.zeros_like(radial)
        for c in range(chunks):
            low[c] = dot_nt(x_refs[c][...], a_ref[...]).astype(bf16)

    shrink = g_ref[...] * m_ref[...] / (column_ref[...] * column_ref[...] * column_ref[...])
    shape = (count * RANK, wide)
    column = lax.broadcasted_iota(jnp.int32, shape, 1) + step * wide
    layer_of = lax.rem(column // span, count)
    own = (lax.broadcasted_iota(jnp.int32, shape, 0) // RANK) == layer_of
    b_pad = jnp.where(own, jnp.concatenate([b_ref[...]] * count, axis=0), 0.0)
    b_low = b_pad.astype(bf16)
    ap = jnp.zeros(shape, f32)
    for c in range(chunks):
        dz = dz_refs[c][...]
        up[c] += dot_nt(dz, b_low)
        ap += dot_tn(low[c], dz)
    radial[...] += dot_nt((b_pad * shrink).astype(bf16), w_ref[...])
    ap = jnp.where(own, ap, 0.0)
    picked = ap[:RANK]
    for i in range(1, count):
        picked = picked + ap[i * RANK : (i + 1) * RANK]
    share_b_ref[...] = (SCALING * (picked - cross_ref[...] * shrink)).astype(bf16)

    @pl.when(step == pl.num_programs(0) - 1)
    def _():
        total = -radial[...]
        for c in range(chunks):
            total = total + dot_tn(up[c].astype(bf16), x_refs[c][...])
        share_a_ref[...] = (SCALING * total).astype(bf16)


def layer_shares(inputs, a_t, dz, b, span, merged, cross, g, magnitude, column):
    chunks = len(inputs)
    rows, depth = inputs[0].shape
    width = dz[0].shape[1]
    count = a_t.shape[0] // RANK
    step = 2 * HD
    columns = lambda height: pl.BlockSpec((height, step), lambda i: (0, i))
    fixed = lambda x: pl.BlockSpec(x.shape, lambda i: (0, 0))
    return pl.pallas_call(
        functools.partial(shares_kernel, count, chunks, span),
        grid=(width // step,),
        in_specs=[fixed(x) for x in inputs]
        + [columns(rows)] * chunks
        + [fixed(a_t), columns(RANK), columns(depth), columns(RANK)]
        + [columns(1)] * 3,
        out_specs=[fixed(a_t), columns(RANK)],
        out_shape=[
            jax.ShapeDtypeStruct(a_t.shape, bf16),
            jax.ShapeDtypeStruct((RANK, width), bf16),
        ],
        scratch_shapes=[
            pltpu.VMEM((chunks, rows, count * RANK), bf16),
            pltpu.VMEM((chunks, rows, count * RANK), f32),
            pltpu.VMEM(a_t.shape, f32),
        ],
        compiler_params=pltpu.CompilerParams(vmem_limit_bytes=VMEM_LIMIT),
        cost_estimate=cost(rows * depth * 64, depth * width),
        name="shares",
    )(*inputs, *dz, a_t.astype(bf16), b, merged, cross, g, magnitude, column)


def down_kernel(chunks, *refs):
    take = taker(refs)
    act_refs = take(chunks)
    w_ref, cot_ref, scale_ref, a_ref, b_ref = take(5)
    raw_ref, g_ref, ap_ref, pb_ref = take(4)
    low, up = take(2)
    step = pl.program_id(0)
    rows = act_refs[0].shape[0]
    size, _, part, wide = cot_ref.shape

    @pl.when(step == 0)
    def _():
        up[...] = jnp.zeros_like(up)
        for c in range(chunks):
            low[c] = dot_nt(act_refs[c][...], a_ref[...]).astype(bf16)

    g = jnp.zeros((1, wide), f32)
    ap = jnp.zeros((RANK, wide), f32)
    b_low = b_ref[...].astype(bf16)
    for c in range(chunks):
        raw = dot(act_refs[c][...], w_ref[...])
        raw_ref[:, c] = raw.astype(bf16).reshape(size, part, wide)
        cot = cot_ref[:, c].reshape(rows, wide).astype(f32)
        g += jnp.sum(cot * raw, axis=0, keepdims=True)
        dz = (cot * scale_ref[...]).astype(bf16)
        up[c] += dot_nt(dz, b_low)
        ap += dot_tn(low[c], dz)
    g_ref[...] = g
    ap_ref[...] = ap.astype(bf16)

    @pl.when(step == pl.num_programs(0) - 1)
    def _():
        total = jnp.zeros(pb_ref.shape, f32)
        for c in range(chunks):
            total = total + dot_tn(up[c].astype(bf16), act_refs[c][...])
        pb_ref[...] = total.astype(bf16)


def down_project(acts, w, cotangent, scale, a_t, b):
    chunks = len(acts)
    rows, ff = acts[0].shape
    wide = w.shape[1]
    step = 2 * HD
    size, _, part, _ = cotangent.shape
    columns = lambda height: pl.BlockSpec((height, step), lambda i: (0, i))
    fixed = lambda *shape: pl.BlockSpec(shape, lambda i: (0,) * len(shape))
    view = pl.BlockSpec((size, chunks, part, step), lambda i: (0, 0, 0, i))
    return pl.pallas_call(
        functools.partial(down_kernel, chunks),
        grid=(wide // step,),
        in_specs=[fixed(rows, ff)] * chunks
        + [columns(ff), view, columns(1), fixed(RANK, ff), columns(RANK)],
        out_specs=[view, columns(1), columns(RANK), fixed(RANK, ff)],
        out_shape=[
            jax.ShapeDtypeStruct(cotangent.shape, bf16),
            jax.ShapeDtypeStruct((1, wide), f32),
            jax.ShapeDtypeStruct((RANK, wide), bf16),
            jax.ShapeDtypeStruct((RANK, ff), bf16),
        ],
        scratch_shapes=[
            pltpu.VMEM((chunks, rows, RANK), bf16),
            pltpu.VMEM((chunks, rows, RANK), f32),
        ],
        compiler_params=pltpu.CompilerParams(vmem_limit_bytes=VMEM_LIMIT),
        cost_estimate=cost(2 * chunks * rows * ff * wide, 2 * ff * wide),
        name="down_project",
    )(*acts, w, cotangent, scale, a_t.astype(bf16), b)


def pack_kernel(plan, scalars, *refs):
    out_ref = refs[-1]
    out_ref[...] = jnp.zeros_like(out_ref)
    row = 0
    for ref, (parts, placed) in zip(refs[:-1], plan):
        height, width = ref.shape
        wide = width // parts
        short = -height % RANK
        lanes = slice(0, wide)
        if placed:
            lanes = pl.ds(pl.multiple_of(scalars[0] * wide, HD), wide)
        if height == 1:
            value = [ref[:, i * wide : (i + 1) * wide].astype(f32) for i in range(parts)]
            value.append(jnp.zeros((RANK - parts, wide), f32))
            out_ref[row : row + RANK, lanes] = jnp.concatenate(value, axis=0).astype(bf16)
            row += RANK
        else:
            for i in range(parts):
                value = ref[:, i * wide : (i + 1) * wide].astype(bf16)
                out_ref[row : row + height, lanes] = value
                row += height


def pack(k, height, width, *entries):
    arrays = [x for x, _, _ in entries]
    plan = [(parts, placed) for _, parts, placed in entries]
    return pl.pallas_call(
        functools.partial(pack_kernel, plan),
        grid_spec=pltpu.PrefetchScalarGridSpec(
            num_scalar_prefetch=1,
            grid=(1,),
            in_specs=[whole_spec(x) for x in arrays],
            out_specs=pl.BlockSpec((height, width), lambda i, s: (0, 0)),
        ),
        out_shape=jax.ShapeDtypeStruct((height, width), bf16),
        compiler_params=pltpu.CompilerParams(vmem_limit_bytes=VMEM_LIMIT),
        cost_estimate=cost(height * width, 4 * height * width),
        name="pack",
    )(k, *arrays)


def span_positions(row_ids, span_order, span_len):
    slot_ids = row_ids // span_len
    slot_table = jnp.arange(span_order.shape[0], dtype=jnp.int32)
    picked = jnp.sum(
        jnp.where(slot_ids[:, None] == slot_table[None, :], span_order[None, :], 0), axis=1
    )
    return picked * span_len + row_ids % span_len


def rotary_tables(positions):
    lane = np.arange(HD)
    frequency = (ROPE_BASE ** (-2.0 * (lane % HALF) / HD)).astype(np.float32)
    sign = np.where(lane < HALF, -1.0, 1.0).astype(np.float32)
    angles = positions.astype(f32)[:, None] * frequency[None, :]
    return jnp.cos(angles), jnp.sin(angles) * sign[None, :]


def pick_blocks(blocks, index):
    out = blocks[0]
    for i in range(1, len(blocks)):
        out = jnp.where(index == i, blocks[i], out)
    return out


def inverse_rms(values):
    return lax.rsqrt(jnp.mean(values * values, axis=-1, keepdims=True) + EPS)


def rms_backward(values, gain_vec, grad_in):
    inverse = inverse_rms(values)
    scaled = grad_in * gain_vec
    return inverse * scaled - values * inverse * inverse * inverse * jnp.mean(
        values * scaled, axis=-1, keepdims=True
    )


def per_device(
    hidden_in,
    cotangent,
    segment_ids,
    padding,
    span_order,
    gain_attn,
    gain_mlp,
    w_query,
    w_key,
    w_value,
    w_out,
    w_gate,
    w_up,
    w_down,
    a_query,
    b_query,
    m_query,
    a_key,
    b_key,
    m_key,
    a_value,
    b_value,
    m_value,
    a_out,
    b_out,
    m_out,
    a_gate,
    b_gate,
    m_gate,
    a_up,
    b_up,
    m_up,
    a_down,
    b_down,
    m_down,
):
    rows, width = hidden_in.shape
    span_len = rows // 2
    near_width = w_query.shape[1]
    peers = near_width // HD
    n_mp = lax.axis_size("mp")
    n_seq = lax.axis_size("seq")
    n_doc = lax.axis_size("doc")
    groups = n_seq // peers
    copies = n_seq * n_doc
    share = rows // n_mp
    chunks = CHUNKS
    part = share // chunks
    k = lax.axis_index("mp")
    doc = lax.axis_index("doc")
    seq = lax.axis_index("seq")
    me = lax.rem(seq, peers)
    my_group = seq // peers
    order = jnp.reshape(me, (1,)).astype(jnp.int32)
    k_scalar = jnp.reshape(k, (1,)).astype(jnp.int32)

    slice_rows = near_width // n_doc
    wo_slice = lax.dynamic_slice_in_dim(w_out, doc * slice_rows, slice_rows, 0)
    wo_all = lax.all_gather(wo_slice, ("mp", "doc"), axis=0, tiled=True)

    slots = [
        2 * (my_group * peers + (me ^ d)) + half for d in range(peers) for half in range(2)
    ]
    slots += [
        2 * (g * peers + (me ^ d)) + half
        for g in range(groups)
        for d in range(peers)
        for half in range(2)
    ]
    slots = jnp.stack(slots)
    table = jnp.arange(span_order.shape[0], dtype=jnp.int32)
    places = jnp.sum(jnp.where(slots[:, None] == table[None, :], span_order[None, :], 0), axis=1)
    scalars = jnp.concatenate([places, k_scalar]).astype(jnp.int32)
    row_ids = jnp.arange(rows, dtype=jnp.int32) + seq * rows
    cosine, sine = rotary_tables(span_positions(row_ids, span_order, span_len))
    codes = seq_exchange([segment_ids * 2 + padding] * peers)
    (hidden_next,) = after([hidden_in], *codes)

    a_heads = jnp.stack([a_key.T, a_value.T, a_query.T])
    b_heads = [b_key, b_value, b_query]
    m_heads = jnp.concatenate([m_key, m_value, m_query])[None, :]
    blocks, normed, wh_low, raw_heads, column_heads, scale_heads, cross_heads = project_heads(
        order,
        hidden_next,
        gain_attn[None, :],
        (w_key, w_value, w_query),
        a_heads,
        jnp.stack(b_heads),
        jnp.stack([m_key, m_value, m_query])[:, None, :],
        cosine,
        sine,
    )
    heads = seq_exchange(blocks)

    codes = [x.reshape(rows, 1) for x in codes]
    w_out_next, w_down_next, w_gate_next, w_up_next = after(
        [w_out, w_down, w_gate, w_up], raw_heads
    )
    (
        square_out,
        cross_out,
        square_down,
        cross_down,
        wd_low,
        wgu_low,
        cross_gu,
        column_gu,
        scale_gu,
        m_gu,
        b_gu,
    ) = merge_others(
        (w_out_next, a_out.T, b_out),
        (w_down_next, a_down.T, b_down),
        (w_gate_next, a_gate.T, b_gate, m_gate[None, :]),
        (w_up_next, a_up.T, b_up, m_up[None, :]),
    )

    extra = []
    if groups > 1:
        members = [[g * peers + i for g in range(groups)] for i in range(peers)]
        gather = lambda x: lax.all_gather(
            x[None], "seq", axis=0, tiled=True, axis_index_groups=members
        )
        extra = [gather(jnp.stack([x[:2] for x in heads])), gather(jnp.stack(codes))]
    heads_next = after(heads, square_out)
    o_blocks, lse = attention_forward(
        scalars, heads_next, codes, extra, groups, n_mp, chunks
    )
    o_heads = seq_exchange(o_blocks)
    near_chunks = assemble(order, o_heads, square_out, square_down, a_out.T, chunks)

    def chunked(values):
        return values.reshape(n_mp, chunks, part, values.shape[-1])

    hid_view, cot_view = chunked(hidden_in), chunked(cotangent)
    b_out_low = b_out.astype(bf16)
    acts, hnorms, dz_gus, dh_chunks = [], [], [], []
    resid_own, raw_out_own, out_low_own, near_own = [], [], [], []
    g_gu = 0.0
    lines = ([near_chunks[0]], [near_chunks[0]])
    for step in range(1, n_mp):
        line_step(*lines, step)
    gathered_chunks = [line_blocks(*lines)]
    for c in range(1, chunks):
        (near_next,) = after([near_chunks[c]], *gathered_chunks[0])
        others = lax.all_gather(near_next, "mp", axis=0)
        gathered_chunks.append(
            [near_chunks[c]]
            + [
                lax.dynamic_index_in_dim(others, lax.rem(k + i, n_mp), 0, keepdims=False)
                for i in range(1, n_mp)
            ]
        )
    column_out, column_down, scale_out, scale_down, a_out_low = unpack(
        k_scalar, gathered_chunks[0], n_mp * part, m_out[None, :], m_down[None, :]
    )
    a_out_twice = SCALING * a_out_low
    for c in range(chunks):
        gathered = gathered_chunks[c]
        if c > 0:
            gathered = after(gathered, dh_chunks[-1])
        hnorm, resid, raw_out, out_low, own = out_project(
            k_scalar,
            c,
            gathered,
            wo_all,
            a_out_low,
            hid_view,
            (SCALING * b_out).astype(bf16),
            scale_out,
            gain_mlp[None, :],
        )
        act, dz_gu, g, dh = feed_forward(
            c, hnorm, cot_view, scale_down, scale_gu, wgu_low, wd_low
        )
        g_gu = g_gu + g
        dh_chunks.append(dh)
        acts.append(act)
        hnorms.append(hnorm)
        dz_gus.append(dz_gu)
        resid_own.append(resid)
        raw_out_own.append(raw_out)
        out_low_own.append(out_low)
        near_own.append(own)

    def scatter(parts):
        return lax.psum_scatter(parts, "mp", scatter_dimension=0, tiled=True)

    pieces = [scatter(x) for x in dh_chunks]

    arrived, dresid_own, dz_out = [], [], []
    out_sums = ()
    earlier = dh_chunks[-1]
    for c in range(chunks):
        (own_piece,) = after([pieces[c]], earlier)
        dattn, dresid, dz, *out_sums = back_out(
            k_scalar,
            c,
            own_piece,
            cot_view,
            resid_own[c],
            raw_out_own[c],
            gain_mlp[None, :],
            scale_out,
            b_out_low,
            near_own[c],
            out_low_own[c],
            wo_all,
            a_out_twice,
            out_sums,
        )
        arrived.append(dattn[0])
        for shift in range(1, n_mp):
            pairs = [(i, (i + shift) % n_mp) for i in range(n_mp)]
            arrived.append(lax.ppermute(dattn[shift], "mp", pairs))
        dresid_own.append(dresid)
        dz_out.append(dz)
        earlier = dz
        if c == 0:
            acts_next = after(acts, dz)
            raw_down, g_down, ap_down, pb_down = down_project(
                acts_next, wd_low, cot_view, scale_down, a_down.T, b_down
            )
            earlier = (g_down, *arrived[1:])
    arrived = jnp.concatenate(arrived, axis=0)
    by_head = [arrived[:, h * HD : (h + 1) * HD] for h in range(peers)]
    grad_blocks = seq_exchange([pick_blocks(by_head, me ^ d) for d in range(peers)])
    dresid_own = jnp.concatenate(dresid_own, axis=0)
    g_out, ap_out, pb_out = out_sums

    grads, dkv = attention_backward(
        scalars, heads_next, codes, extra, o_blocks, grad_blocks, lse, groups, n_mp, chunks
    )
    if groups > 1:
        members = [[g * peers + i for g in range(groups)] for i in range(peers)]
        dkv = lax.psum_scatter(
            dkv, "seq", scatter_dimension=0, tiled=True, axis_index_groups=members
        )
        grads = [jnp.concatenate([dkv[0, d], grads[d]], axis=0) for d in range(peers)]
    head_grads = seq_exchange(grads)

    hnorms_next, dz_gus_next = after([tuple(hnorms), tuple(dz_gus)], grads[0])
    share_a_gu, share_b_gu = layer_shares(
        hnorms_next,
        jnp.concatenate([a_gate.T, a_up.T], axis=0),
        dz_gus_next,
        b_gu,
        HD,
        wgu_low,
        cross_gu,
        g_gu,
        m_gu,
        column_gu,
    )
    (raw_down,) = after([raw_down], *grad_blocks)
    down_own = scatter(raw_down.reshape(rows, width))
    head_grads = after(head_grads, share_a_gu)

    dz_heads, g_heads, dnormed = unproject(
        order, cosine, sine, raw_heads, scale_heads, wh_low, head_grads
    )
    dnormed_own = scatter(dnormed)

    (down_own,) = after([down_own], dnormed)
    result = jnp.concatenate(resid_own, axis=0) + down_own.astype(f32) * scale_down
    hidden_own = lax.dynamic_slice_in_dim(hidden_in, k * share, share, 0).astype(f32)

    early_rows = pack(
        k_scalar,
        48,
        share_b_gu.shape[1],
        (share_b_gu, 1, False),
        (pb_down, 1, False),
        (g_gu, 1, False),
    )
    (early_rows,) = after([early_rows], dnormed)
    early_rows = doc_join(butterfly(doc_halve(early_rows), ["seq"])).astype(f32)

    share_a_heads, share_b_heads = layer_shares(
        [normed],
        a_heads.reshape(3 * RANK, width),
        [dz_heads],
        jnp.concatenate(b_heads, axis=1),
        near_width,
        wh_low,
        cross_heads,
        g_heads,
        m_heads,
        column_heads,
    )
    late = pack(
        k_scalar,
        256,
        width,
        (share_a_gu, 1, False),
        (ap_down, 1, False),
        (cross_out / copies, 1, False),
        (cross_down / copies, 1, False),
        (ap_out, 1, False),
        (jnp.concatenate([g_down, g_out], axis=1), 2, False),
        (pb_out, 1, False),
        (share_a_heads, 1, False),
        (share_b_heads, 3, True),
        (g_heads, 3, True),
    )
    late = spread_join(spread_sum(doc_halve(late), peers, ["mp"]), peers)
    (late,) = after([late], dnormed_own)
    late = doc_join(late).astype(f32)
    early, late = late[:128], late[128:]
    late_columns = late[3 * RANK : 7 * RANK]
    late_own = lax.dynamic_slice_in_dim(late_columns, k * near_width, near_width, 1)

    grad_input = dresid_own + rms_backward(
        hidden_own, gain_attn, dnormed_own.astype(f32)
    )

    def rank_rows(array, index):
        return array[index * RANK : (index + 1) * RANK]

    ff = w_gate.shape[1]
    total_g_down, total_g_out = early[96:97], early[97:98]
    shrink_out = total_g_out * m_out / (column_out * column_out * column_out)
    shrink_down = total_g_down * m_down / (column_down * column_down * column_down)
    turned_out = (b_out * shrink_out).astype(bf16)
    radial_out = dot_nt(turned_out, w_out) + SCALING * dot(
        dot_nt(turned_out, b_out.astype(bf16)), a_out.T
    )
    radial_down = dot_nt((b_down * shrink_down).astype(bf16), wd_low)
    pb_out = lax.dynamic_slice_in_dim(early[112:128], k * near_width, near_width, 1)
    grad_a_out = SCALING * (pb_out - radial_out)
    grad_a_down = SCALING * (early_rows[16:32, :ff] - radial_down)
    grad_b_out = SCALING * (rank_rows(early, 5) - rank_rows(early, 3) * shrink_out)
    grad_b_down = SCALING * (rank_rows(early, 2) - rank_rows(early, 4) * shrink_down)

    g_rows = late_own[3 * RANK : 3 * RANK + 3].reshape(1, -1) / column_heads
    g_rows = [g_rows[0, i * near_width : (i + 1) * near_width] for i in range(3)]
    grad_m_gate, grad_m_up = separate(early_rows[32:33] / column_gu)
    grad_b_gate, grad_b_up = separate(early_rows[:16])
    return (
        result,
        grad_input,
        rank_rows(late, 2).T,
        rank_rows(late_own, 2),
        g_rows[2],
        rank_rows(late, 0).T,
        rank_rows(late_own, 0),
        g_rows[0],
        rank_rows(late, 1).T,
        rank_rows(late_own, 1),
        g_rows[1],
        grad_a_out.T,
        grad_b_out,
        (total_g_out / column_out)[0],
        rank_rows(early, 0).T,
        grad_b_gate,
        grad_m_gate[0],
        rank_rows(early, 1).T,
        grad_b_up,
        grad_m_up[0],
        grad_a_down.T,
        grad_b_down,
        (total_g_down / column_down)[0],
    )


def solution(mesh):
    rows = P(("doc", "seq"))
    split_columns = (P(None, "mp"), P(None, "mp"))
    column_layer = (P(), P(None, "mp"), P("mp"))
    row_layer = (P("mp", None), P(), P())
    in_specs = (
        P(("doc", "seq"), None),
        P(("doc", "seq"), None),
        rows,
        rows,
        P(),
        P(),
        P(),
        P(None, "mp"),
        P(None, "mp"),
        P(None, "mp"),
        P("mp", None),
        *split_columns,
        P("mp", None),
        *column_layer,
        *column_layer,
        *column_layer,
        *row_layer,
        *column_layer,
        *column_layer,
        *row_layer,
    )
    out_specs = (
        P(("doc", "seq", "mp"), None),
        P(("doc", "seq", "mp"), None),
        *column_layer,
        *column_layer,
        *column_layer,
        *row_layer,
        *column_layer,
        *column_layer,
        *row_layer,
    )
    return jax.shard_map(
        per_device, mesh=mesh, in_specs=in_specs, out_specs=out_specs, check_vma=False
    )
```

```python
import functools
import math

import jax
import jax.numpy as jnp
import numpy as np
from jax import lax
from jax.experimental import pallas as pl
from jax.experimental.pallas import tpu as pltpu
from jax.sharding import PartitionSpec as P

HD = 128
RANK = 16
ALPHA = 32
HALF = HD // 2
SCALING = ALPHA / RANK
INV_ROOT = HD ** (-0.5)
EPS = 1e-05
ROPE_BASE = 10000.0
MASKED = -1e30
CHUNKS = 2
MIB = 1 << 20
VMEM_LIMIT = 56 * MIB

f32 = jnp.float32
bf16 = jnp.bfloat16


def dot(left, right):
    return jnp.dot(left, right, preferred_element_type=f32)


def dot_nt(left, right):
    return lax.dot_general(left, right, (((1,), (1,)), ((), ())), preferred_element_type=f32)


def dot_tn(left, right):
    return lax.dot_general(left, right, (((0,), (0,)), ((), ())), preferred_element_type=f32)


def whole_spec(array):
    rank = len(array.shape)
    return pl.BlockSpec(tuple(array.shape), lambda *_: (0,) * rank)


def cost(flops, moved):
    return pl.CostEstimate(flops=1, bytes_accessed=1, transcendentals=0)


def swap(value, axis, distance):
    size = lax.axis_size(axis)
    return lax.ppermute(value, axis, [(i, i ^ distance) for i in range(size)])


def butterfly(value, axes):
    for axis in axes:
        distance = 1
        while distance < lax.axis_size(axis):
            value = lax.optimization_barrier(value + swap(value, axis, distance))
            distance *= 2
    return value


def doc_halve(value):
    doc = lax.axis_index("doc")
    half = value.shape[0] // 2
    mine = lax.dynamic_slice_in_dim(value, doc * half, half, 0)
    other = lax.dynamic_slice_in_dim(value, (1 - doc) * half, half, 0)
    return lax.optimization_barrier(mine + swap(other, "doc", 1))


def doc_join(mine):
    doc = lax.axis_index("doc")
    other = swap(mine, "doc", 1)
    first = jnp.where(doc == 0, mine, other)
    second = jnp.where(doc == 0, other, mine)
    return jnp.concatenate([first, second], axis=0)


def spread_sum(value, peers, axes, leading):
    me = lax.rem(lax.axis_index("seq"), peers)
    parts = value.reshape(peers, -1, value.shape[-1])
    piece = lambda index: lax.dynamic_index_in_dim(parts, index, 0, keepdims=False)
    mine = piece(me).astype(f32)
    for d in range(1, peers):
        mine = mine + swap(piece(me ^ d), "seq", d).astype(f32)
    mine = lax.optimization_barrier(mine.astype(bf16))
    distance = peers
    while distance < lax.axis_size("seq"):
        mine = lax.optimization_barrier(mine + swap(mine, "seq", distance))
        distance *= 2
    return jnp.concatenate([butterfly(mine[:leading], axes), mine[leading:]], axis=0)


def spread_join(mine, peers):
    me = lax.rem(lax.axis_index("seq"), peers)
    found = [mine] + [swap(mine, "seq", d) for d in range(1, peers)]
    return jnp.concatenate([pick_blocks(found, me ^ i) for i in range(peers)], axis=0)


def after(values, *earlier):
    tied = lax.optimization_barrier((tuple(values), earlier))
    return tied[0]


def line_step(rights, lefts, step, *earlier):
    size = lax.axis_size("mp")
    right, left = rights[-1], lefts[-1]
    if earlier:
        right, left = after([right, left], *earlier)
    right_pairs = [(i, i + 1) for i in range(step - 1, size - 1)]
    left_pairs = [(i, i - 1) for i in range(1, size - step + 1)]
    rights.append(lax.ppermute(right, "mp", right_pairs))
    lefts.append(lax.ppermute(left, "mp", left_pairs))


def line_blocks(rights, lefts):
    size = lax.axis_size("mp")
    k = lax.axis_index("mp")
    return [rights[0]] + [
        jnp.where(k + c < size, lefts[c], rights[size - c]) for c in range(1, size)
    ]


def seq_exchange(blocks):
    return [blocks[0]] + [swap(blocks[d], "seq", d) for d in range(1, len(blocks))]


def key_marks(code):
    lane = lax.broadcasted_iota(jnp.int32, (code.shape[0], HD), 1)
    segment, real = code >> 1, code & 1
    wrong = (lane < 16) & (lane != segment)
    absent = (lane == 16) & (real == 0)
    return jnp.where(wrong | absent, MASKED, 0.0).astype(bf16)


def query_marks(code):
    lane = lax.broadcasted_iota(jnp.int32, (code.shape[0], HD), 1)
    segment = code >> 1
    return jnp.where((lane == segment) | (lane == 16), 1.0, 0.0).astype(bf16)


def diagonal_scores(keys, query):
    marked = dot_nt(keys, query)
    plain = dot_nt(keys[:, :HD], query[:, :HD])
    key_id = lax.broadcasted_iota(jnp.int32, marked.shape, 0)
    query_id = lax.broadcasted_iota(jnp.int32, marked.shape, 1)
    return jnp.where(
        key_id < query_id, marked, jnp.where(key_id == query_id, plain, MASKED)
    )


def block_readers(groups, heads, kv_refs, code_refs):
    if groups == 1:
        return (
            lambda g, d, rows: heads[d][0, rows, :],
            lambda g, d, rows: heads[d][1, rows, :],
            lambda g, d, rows: code_refs[d][rows, :],
        )
    return (
        lambda g, d, rows: kv_refs[0][g, d, 0, rows, :],
        lambda g, d, rows: kv_refs[0][g, d, 1, rows, :],
        lambda g, d, rows: kv_refs[1][g, d, rows, :],
    )


def taker(refs):
    refs = list(refs)

    def take(count):
        taken = refs[:count]
        del refs[:count]
        return taken

    return take


def forward_kernel(meta, scalars, *refs):
    peers, groups, span, pieces, chunks, n_extra = meta
    take = taker(refs)
    heads, code_refs, kv_refs = take(peers), take(peers), take(n_extra)
    o_refs, (lse_ref,) = take(peers), take(1)
    q_all, o_all, k_all, v_turned = take(4)
    key_of, value_of, key_code_of = block_readers(groups, heads, kv_refs, code_refs)
    n_query = 2 * peers

    for g in range(groups):
        for d in range(peers):
            for half in range(2):
                rows = pl.ds(half * span, span)
                place = scalars[n_query + (g * peers + d) * 2 + half]
                at = pl.ds(pl.multiple_of(place * span, HD), span)
                k_all[at, :HD] = key_of(g, d, rows)
                k_all[at, HD:] = key_marks(key_code_of(g, d, rows))
                v_turned[:, at] = value_of(g, d, rows).astype(f32).T.astype(bf16)
    for d in range(peers):
        for half in range(2):
            rows = pl.ds(half * span, span)
            q_all[2 * d + half, :, :HD] = heads[d][2, rows, :]
            q_all[2 * d + half, :, HD:] = query_marks(code_refs[d][rows, :])

    def one_span(i, carry):
        place = scalars[i]
        query = q_all[i]
        at = pl.ds(pl.multiple_of(place * span, HD), span)
        scores = diagonal_scores(k_all[at, :], query)
        peak = jnp.max(scores, axis=0, keepdims=True)
        weights = jnp.exp((scores - peak) * INV_ROOT)
        total = jnp.sum(weights, axis=0, keepdims=True)
        out = dot(v_turned[:, at], weights.astype(bf16))

        def key_span(j, state):
            peak, total, out = state
            at = pl.ds(pl.multiple_of(j * span, HD), span)
            scores = dot_nt(k_all[at, :], query)
            new_peak = jnp.maximum(peak, jnp.max(scores, axis=0, keepdims=True))
            fade = jnp.exp((peak - new_peak) * INV_ROOT)
            weights = jnp.exp((scores - new_peak) * INV_ROOT)
            total = total * fade + jnp.sum(weights, axis=0, keepdims=True)
            out = out * fade + dot(v_turned[:, at], weights.astype(bf16))
            return (new_peak, total, out)

        peak, total, out = lax.fori_loop(0, place, key_span, (peak, total, out))
        lse_ref[i] = peak * INV_ROOT + jnp.log(total)
        o_all[i] = (out / total).T.astype(bf16)
        return carry

    lax.fori_loop(0, n_query, one_span, 0)
    share = 2 * span // pieces
    part = share // chunks
    for d in range(peers):
        for piece in range(pieces):
            for c in range(chunks):
                row = piece * share + c * part
                to = (c * pieces + piece) * part
                o_refs[d][to : to + part, :] = o_all[
                    2 * d + row // span, row % span : row % span + part, :
                ]


def place_rows(scalars, peers, span):
    for d in range(peers):
        for half in range(2):
            place = scalars[2 * d + half]
            at = pl.ds(pl.multiple_of(place * span, HD), span)
            yield d, half, pl.ds(half * span, span), at


def piece_rows(peers, span, pieces, chunks):
    share = 2 * span // pieces
    part = share // chunks
    for d in range(peers):
        for piece in range(pieces):
            for c in range(chunks):
                row = piece * share + c * part
                yield d, piece, c, pl.ds((c * pieces + piece) * part, part), row, part


def forward_group_kernel(meta, scalars, *refs):
    peers, _, span, pieces, chunks, _ = meta
    take = taker(refs)
    heads, code_refs = take(peers), take(peers)
    o_refs, (lse_ref,) = take(peers), take(1)
    q_all, o_all, k_all, v_turned = take(4)
    tile = 2 * span

    for d, half, rows, at in place_rows(scalars, peers, span):
        code = code_refs[d][rows, :]
        k_all[at, :HD] = heads[d][0, rows, :]
        k_all[at, HD:] = key_marks(code)
        v_turned[:, at] = heads[d][1, rows, :].astype(f32).T.astype(bf16)
        q_all[at, :HD] = heads[d][2, rows, :]
        q_all[at, HD:] = query_marks(code)

    for m in range(peers):
        here = slice(m * tile, (m + 1) * tile)
        query = q_all[here, :]
        scores = diagonal_scores(k_all[here, :], query)
        peak = jnp.max(scores, axis=0, keepdims=True)
        weights = jnp.exp((scores - peak) * INV_ROOT)
        total = jnp.sum(weights, axis=0, keepdims=True)
        out = dot(v_turned[:, here], weights.astype(bf16))

        def key_tile(j, state):
            peak, total, out = state
            at = pl.ds(pl.multiple_of(j * tile, HD), tile)
            scores = dot_nt(k_all[at, :], query)
            new_peak = jnp.maximum(peak, jnp.max(scores, axis=0, keepdims=True))
            fade = jnp.exp((peak - new_peak) * INV_ROOT)
            weights = jnp.exp((scores - new_peak) * INV_ROOT)
            total = total * fade + jnp.sum(weights, axis=0, keepdims=True)
            out = out * fade + dot(v_turned[:, at], weights.astype(bf16))
            return (new_peak, total, out)

        if m:
            peak, total, out = lax.fori_loop(0, m, key_tile, (peak, total, out))
        lse_ref[m] = peak * INV_ROOT + jnp.log(total)
        o_all[here, :] = (out / total).T.astype(bf16)

    for d, piece, c, to, row, part in piece_rows(peers, span, pieces, chunks):
        place = scalars[2 * d + row // span] * span + row % span
        o_refs[d][to, :] = o_all[pl.ds(pl.multiple_of(place, 32), part), :]


def backward_group_kernel(meta, scalars, *refs):
    peers, groups, span, pieces, chunks, _ = meta
    take = taker(refs)
    heads, code_refs = take(peers), take(peers)
    o_refs, do_refs, (lse_ref,) = take(peers), take(peers), take(1)
    grad_refs = take(peers)
    q_all, o_all, do_all, k_all, k_turned, v_all, dk_all, dv_all = take(8)
    own_piece = scalars[4 * peers]
    tile = 2 * span
    share = 2 * span // pieces

    for d, half, rows, at in place_rows(scalars, peers, span):
        code = code_refs[d][rows, :]
        key = heads[d][0, rows, :]
        k_all[at, :HD] = key
        k_all[at, HD:] = key_marks(code)
        k_turned[:, at] = key.astype(f32).T.astype(bf16)
        v_all[at, :] = heads[d][1, rows, :]
        q_all[at, :HD] = heads[d][2, rows, :]
        q_all[at, HD:] = query_marks(code)
    for d, piece, c, source, row, part in piece_rows(peers, span, pieces, chunks):
        place = scalars[2 * d + row // span] * span + row % span
        o_all[pl.ds(pl.multiple_of(place, 32), part), :] = o_refs[d][source, :]
        row = lax.rem(own_piece + pieces - piece, pieces) * share + c * part
        late = row >= span
        place = scalars[2 * d + late.astype(jnp.int32)] * span + row - jnp.where(late, span, 0)
        do_all[pl.ds(pl.multiple_of(place, 32), part), :] = do_refs[d][source, :]

    for m in range(peers):
        here = slice(m * tile, (m + 1) * tile)
        query = q_all[here, :]
        grad = do_all[here, :]
        product = grad.astype(f32) * o_all[here, :].astype(f32)
        high, rest = split_low(product)
        ones = jnp.ones((16, HD), bf16)
        delta = (dot_nt(ones, high) + dot_nt(ones, rest))[:1, :]
        lse = lse_ref[m]

        def key_tile(at, scores, dq_turned, first):
            probs = jnp.exp(scores * INV_ROOT - lse)
            grad_score = (probs * (dot_nt(v_all[at, :], grad) - delta)).astype(bf16)
            dv = dot(probs.astype(bf16), grad)
            dk = dot(grad_score, query[:, :HD])
            if first:
                dv_all[at, :] = dv
                dk_all[at, :] = dk
            else:
                dv_all[at, :] += dv
                dk_all[at, :] += dk
            return dq_turned + dot(k_turned[:, at], grad_score)

        scores = diagonal_scores(k_all[here, :], query)
        dq_turned = key_tile(here, scores, jnp.zeros((HD, tile), f32), True)

        def step(j, dq_turned):
            at = pl.ds(pl.multiple_of(j * tile, HD), tile)
            return key_tile(at, dot_nt(k_all[at, :], query), dq_turned, False)

        if m:
            dq_turned = lax.fori_loop(0, m, step, dq_turned)
        o_all[here, :] = (dq_turned * INV_ROOT).T.astype(bf16)

    for d, half, rows, at in place_rows(scalars, peers, span):
        grad_refs[d][0, rows, :] = (dk_all[at, :] * INV_ROOT).astype(bf16)
        grad_refs[d][1, rows, :] = dv_all[at, :].astype(bf16)
        grad_refs[d][2, rows, :] = o_all[at, :]


def attention_forward(scalars, heads, codes, extra, groups, pieces, chunks):
    peers = len(heads)
    rows = heads[0].shape[1]
    span = rows // 2
    key_rows = groups * peers * rows
    meta = (peers, groups, span, pieces, chunks, len(extra))
    operands = [*heads, *codes, *extra]
    out_shape = [jax.ShapeDtypeStruct((rows, HD), bf16)] * peers
    n_query = 2 * peers if groups > 1 else peers
    out_shape.append(jax.ShapeDtypeStruct((n_query, 1, 2 * peers * span // n_query), f32))
    if groups == 1:
        body, q_shape, o_shape = forward_group_kernel, (key_rows, 2 * HD), (key_rows, HD)
    else:
        body, q_shape, o_shape = (
            forward_kernel,
            (2 * peers, span, 2 * HD),
            (2 * peers, span, HD),
        )
    outs = pl.pallas_call(
        functools.partial(body, meta),
        grid_spec=pltpu.PrefetchScalarGridSpec(
            num_scalar_prefetch=1,
            grid=(1,),
            in_specs=[whole_spec(x) for x in operands],
            out_specs=[whole_spec(x) for x in out_shape],
            scratch_shapes=[
                pltpu.VMEM(q_shape, bf16),
                pltpu.VMEM(o_shape, bf16),
                pltpu.VMEM((key_rows, 2 * HD), bf16),
                pltpu.VMEM((HD, key_rows), bf16),
            ],
        ),
        out_shape=out_shape,
        compiler_params=pltpu.CompilerParams(vmem_limit_bytes=VMEM_LIMIT),
        cost_estimate=cost(6 * peers * rows * key_rows // 2 * HD, 8 * key_rows * HD),
        name="attend",
    )(scalars, *operands)
    return outs[:-1], outs[-1]


def backward_kernel(meta, scalars, *refs):
    peers, groups, span, pieces, chunks, n_extra = meta
    take = taker(refs)
    heads, code_refs, kv_refs = take(peers), take(peers), take(n_extra)
    o_refs, do_refs, (lse_ref,) = take(peers), take(peers), take(1)
    grad_refs = take(peers)
    dkv_refs = take(1 if groups > 1 else 0)
    q_all, o_all, do_all, k_all, k_turned, v_all, dk_all, dv_all = take(8)
    key_of, value_of, key_code_of = block_readers(groups, heads, kv_refs, code_refs)
    n_query = 2 * peers
    own_piece = scalars[n_query + 2 * groups * peers]

    for g in range(groups):
        for d in range(peers):
            for half in range(2):
                rows = pl.ds(half * span, span)
                place = scalars[n_query + (g * peers + d) * 2 + half]
                at = pl.ds(pl.multiple_of(place * span, HD), span)
                key = key_of(g, d, rows)
                k_all[at, :HD] = key
                k_all[at, HD:] = key_marks(key_code_of(g, d, rows))
                k_turned[:, at] = key.astype(f32).T.astype(bf16)
                v_all[at, :] = value_of(g, d, rows)
    dk_all[...] = jnp.zeros_like(dk_all)
    dv_all[...] = jnp.zeros_like(dv_all)
    share = 2 * span // pieces
    part = share // chunks
    for d in range(peers):
        for half in range(2):
            rows = pl.ds(half * span, span)
            q_all[2 * d + half, :, :HD] = heads[d][2, rows, :]
            q_all[2 * d + half, :, HD:] = query_marks(code_refs[d][rows, :])
        for piece in range(pieces):
            origin = lax.rem(own_piece + pieces - piece, pieces)
            for c in range(chunks):
                source = pl.ds((c * pieces + piece) * part, part)
                row = (2 * d * span) + piece * share + c * part
                o_all[row : row + part, :] = o_refs[d][source, :]
                row = (2 * d * span) + origin * share + c * part
                do_all[pl.ds(pl.multiple_of(row, 16), part), :] = do_refs[d][source, :]

    def one_span(i, carry):
        place = scalars[i]
        query = q_all[i]
        rows = pl.ds(pl.multiple_of(i * span, HD), span)
        grad = do_all[rows, :]
        product = grad.astype(f32) * o_all[rows, :].astype(f32)
        high = product.astype(bf16)
        rest = (product - high.astype(f32)).astype(bf16)
        ones = jnp.ones((16, HD), bf16)
        delta = (dot_nt(ones, high) + dot_nt(ones, rest))[:1, :]
        lse = lse_ref[i]

        def key_span(at, scores, dq_turned):
            probs = jnp.exp(scores * INV_ROOT - lse)
            grad_prob = dot_nt(v_all[at, :], grad)
            grad_score = (probs * (grad_prob - delta)).astype(bf16)
            dv_all[at, :] += dot(probs.astype(bf16), grad)
            dk_all[at, :] += dot(grad_score, query[:, :HD])
            return dq_turned + dot(k_turned[:, at], grad_score)

        at = pl.ds(pl.multiple_of(place * span, HD), span)
        dq_turned = key_span(
            at, diagonal_scores(k_all[at, :], query), jnp.zeros((HD, span), f32)
        )

        def step(j, dq_turned):
            at = pl.ds(pl.multiple_of(j * span, HD), span)
            return key_span(at, dot_nt(k_all[at, :], query), dq_turned)

        dq_turned = lax.fori_loop(0, place, step, dq_turned)
        o_all[rows, :] = (dq_turned * INV_ROOT).T.astype(bf16)
        return carry

    lax.fori_loop(0, n_query, one_span, 0)
    at_query = 2 if groups == 1 else 0
    for d in range(peers):
        grad_refs[d][at_query] = o_all[2 * d * span : 2 * (d + 1) * span, :]
    for g in range(groups):
        for d in range(peers):
            for half in range(2):
                rows = pl.ds(half * span, span)
                place = scalars[n_query + (g * peers + d) * 2 + half]
                at = pl.ds(pl.multiple_of(place * span, HD), span)
                grad_key = (dk_all[at, :] * INV_ROOT).astype(bf16)
                grad_value = dv_all[at, :].astype(bf16)
                if groups == 1:
                    grad_refs[d][0, rows, :] = grad_key
                    grad_refs[d][1, rows, :] = grad_value
                else:
                    dkv_refs[0][g, d, 0, rows, :] = grad_key
                    dkv_refs[0][g, d, 1, rows, :] = grad_value


def attention_backward(scalars, heads, codes, extra, o, grads, lse, groups, pieces, chunks):
    peers = len(heads)
    rows = heads[0].shape[1]
    span = rows // 2
    key_rows = groups * peers * rows
    meta = (peers, groups, span, pieces, chunks, len(extra))
    operands = [*heads, *codes, *extra, *o, *grads, lse]
    parts = 3 if groups == 1 else 1
    out_shape = [jax.ShapeDtypeStruct((parts, rows, HD), bf16)] * peers
    if groups > 1:
        out_shape.append(jax.ShapeDtypeStruct(extra[0].shape, bf16))
    if groups == 1:
        body, q_shape = backward_group_kernel, (key_rows, 2 * HD)
    else:
        body, q_shape = backward_kernel, (2 * peers, span, 2 * HD)
    outs = pl.pallas_call(
        functools.partial(body, meta),
        grid_spec=pltpu.PrefetchScalarGridSpec(
            num_scalar_prefetch=1,
            grid=(1,),
            in_specs=[whole_spec(x) for x in operands],
            out_specs=[whole_spec(x) for x in out_shape],
            scratch_shapes=[
                pltpu.VMEM(q_shape, bf16),
                pltpu.VMEM((peers * rows, HD), bf16),
                pltpu.VMEM((peers * rows, HD), bf16),
                pltpu.VMEM((key_rows, 2 * HD), bf16),
                pltpu.VMEM((HD, key_rows), bf16),
                pltpu.VMEM((key_rows, HD), bf16),
                pltpu.VMEM((key_rows, HD), f32),
                pltpu.VMEM((key_rows, HD), f32),
            ],
        ),
        out_shape=out_shape,
        compiler_params=pltpu.CompilerParams(vmem_limit_bytes=VMEM_LIMIT),
        cost_estimate=cost(14 * peers * rows * key_rows // 2 * HD, 16 * key_rows * HD),
        name="attend_back",
    )(scalars, *operands)
    if groups == 1:
        return outs, None
    return outs[:peers], outs[peers]


def split_low(value):
    high = value.astype(bf16)
    return high, (value - high.astype(f32)).astype(bf16)


def low_rank(a_t, b):
    a_high, a_rest = split_low(a_t)
    b_high, b_rest = split_low(b * SCALING)
    a_cat = jnp.concatenate([a_high, a_rest, a_high], axis=0)
    b_cat = jnp.concatenate([b_high, b_high, b_rest], axis=0)
    return dot_tn(a_cat, b_cat)


def separate(both):
    rows, width = both.shape
    both = both.reshape(rows, -1, 2, HD)
    return both[:, :, 0].reshape(rows, width // 2), both[:, :, 1].reshape(rows, width // 2)


def merge_kernel(starts, out_w, out_a, out_b, down_w, down_a, down_b, gate_w, up_w, gate_a, up_a,
                 gate_b, up_b, gate_m, up_m, out_square, out_cross, down_square, down_cross,
                 down_low, pair_low, pair_cross, pair_column, pair_scale, mixed_m, mixed_b):
    step = pl.program_id(0)
    down_start, pair_start = starts

    def columns(w_ref, a_ref, b_ref, square_ref, cross_ref, low_ref):
        merged = w_ref[...].astype(f32) + low_rank(a_ref[...], b_ref[...])
        low = merged.astype(bf16)
        if low_ref is not None:
            low_ref[...] = low
        square_ref[...] = jnp.sum(merged * merged, axis=0, keepdims=True)
        cross_ref[...] = dot(a_ref[...].astype(bf16), low)

    @pl.when(step < down_start)
    def _():
        columns(out_w, out_a, out_b, out_square, out_cross, None)

    @pl.when((step >= down_start) & (step < pair_start))
    def _():
        columns(down_w, down_a, down_b, down_square, down_cross, down_low)

    sides = ((gate_w, gate_a, gate_b, gate_m), (up_w, up_a, up_b, up_m))
    blocks = [
        (side, slice(j * HD, (j + 1) * HD), pl.ds((2 * j + side) * HD, HD))
        for side in range(2)
        for j in range(gate_w.shape[1] // HD)
    ]

    @pl.when(step == pair_start)
    def _():
        pair_column[...] = jnp.zeros_like(pair_column)
        pair_cross[...] = jnp.zeros_like(pair_cross)
        for side, source, at in blocks:
            mixed_b[:, at] = sides[side][2][:, source]
            mixed_m[:, at] = sides[side][3][:, source]

    @pl.when(step >= pair_start)
    def _():
        results = []
        for w_ref, a_ref, b_ref, _ in sides:
            merged = w_ref[...].astype(f32) + low_rank(a_ref[...], b_ref[...])
            low = merged.astype(bf16)
            square = jnp.sum(merged * merged, axis=0, keepdims=True)
            results.append((low, square, dot(a_ref[...].astype(bf16), low)))
        for side, source, at in blocks:
            low, square, cross = results[side]
            pair_low[:, at] = low[:, source]
            pair_column[:, at] += square[:, source]
            pair_cross[:, at] += cross[:, source]

    @pl.when(step == pl.num_programs(0) - 1)
    def _():
        column = jnp.sqrt(pair_column[...])
        pair_column[...] = column
        pair_scale[...] = mixed_m[...] / column


def merge_others(out, down, gate, up):
    step = 8 * HD
    rows = 2 * HD
    near, wide = out[0].shape
    ff = down[0].shape[0]
    depth, width = gate[0].shape
    n_columns = wide // step
    starts = (n_columns, 2 * n_columns)
    n_pair = depth // rows
    at_out = lambda i: jnp.minimum(i, n_columns - 1)
    at_down = lambda i: jnp.clip(i - starts[0], 0, n_columns - 1)
    at_pair = lambda i: jnp.clip(i - starts[1], 0, n_pair - 1)
    cut = lambda height, at: pl.BlockSpec((height, step), lambda i: (0, at(i)))
    fixed = lambda *shape: pl.BlockSpec(shape, lambda i: (0,) * len(shape))
    pair_rows = lambda lanes: pl.BlockSpec((rows, lanes), lambda i: (at_pair(i), 0))
    turned = pl.BlockSpec((RANK, rows), lambda i: (0, at_pair(i)))
    shape = jax.ShapeDtypeStruct
    return pl.pallas_call(
        functools.partial(merge_kernel, starts),
        grid=(starts[1] + n_pair,),
        in_specs=[
            cut(near, at_out),
            fixed(RANK, near),
            cut(RANK, at_out),
            cut(ff, at_down),
            fixed(RANK, ff),
            cut(RANK, at_down),
            pair_rows(width),
            pair_rows(width),
            turned,
            turned,
            fixed(RANK, width),
            fixed(RANK, width),
            fixed(1, width),
            fixed(1, width),
        ],
        out_specs=[
            cut(1, at_out),
            cut(RANK, at_out),
            cut(1, at_down),
            cut(RANK, at_down),
            cut(ff, at_down),
            pair_rows(2 * width),
            fixed(RANK, 2 * width),
            fixed(1, 2 * width),
            fixed(1, 2 * width),
            fixed(1, 2 * width),
            fixed(RANK, 2 * width),
        ],
        out_shape=[
            shape((1, wide), f32),
            shape((RANK, wide), f32),
            shape((1, wide), f32),
            shape((RANK, wide), f32),
            shape((ff, wide), bf16),
            shape((depth, 2 * width), bf16),
            shape((RANK, 2 * width), f32),
            shape((1, 2 * width), f32),
            shape((1, 2 * width), f32),
            shape((1, 2 * width), f32),
            shape((RANK, 2 * width), f32),
        ],
        compiler_params=pltpu.CompilerParams(vmem_limit_bytes=VMEM_LIMIT),
        cost_estimate=cost(4 * depth * width * RANK, 8 * depth * width),
        name="merge_others",
    )(*out, *down, gate[0], up[0], gate[1], up[1], gate[2], up[2], gate[3], up[3])


def heads_kernel(scalars, x_ref, gain_ref, a_ref, b_ref, m_ref, cos_ref, sin_ref,
                 wk_hbm, wv_hbm, wq_hbm, *refs):
    take = taker(refs)
    peers = len(refs) - 12
    blocks = take(peers)
    normed_ref, low_ref, raw_ref, column_ref, scale_ref, cross_ref = take(6)
    x_all, w_all, merged_all, column_now, scale_now, sem = take(6)
    step = pl.program_id(0)
    rows = x_ref.shape[0]
    sources = (wk_hbm, wv_hbm, wq_hbm)

    def copy(number):
        return pltpu.make_async_copy(sources[number], w_all.at[number], sem.at[number])

    def merge(layer):
        slot = lax.rem(layer, 2)
        merged = w_all[layer].astype(f32) + low_rank(a_ref[layer], b_ref[layer])
        low = merged.astype(bf16)
        merged_all[slot] = low
        low_ref[...] = low
        column = jnp.sqrt(jnp.sum(merged * merged, axis=0, keepdims=True))
        scale = m_ref[layer] / column
        column_ref[...] = column
        scale_ref[...] = scale
        scale_now[slot] = scale

    @pl.when(step == 0)
    def _():
        for number in range(3):
            copy(number).start()
        part = rows // 4
        for i in range(4):
            at = pl.ds(i * part, part)
            x = x_ref[at, :].astype(f32)
            inverse = lax.rsqrt(jnp.mean(x * x, axis=-1, keepdims=True) + EPS)
            normed = (x * inverse * gain_ref[...]).astype(bf16)
            x_all[at, :] = normed
            normed_ref[at, :] = normed
        x_all[rows:, :] = a_ref[0].astype(bf16)
        copy(0).wait()
        merge(0)

    for number in (1, 2):

        @pl.when(step == number)
        def _(number=number):
            copy(number).wait()

    @pl.when(step > 0)
    def _():
        layer = step - 1
        slot = lax.rem(layer, 2)
        product = dot(x_all[...], merged_all[slot])
        scale = scale_now[slot]
        x_next = a_ref[jnp.minimum(step, 2)].astype(bf16)
        merge(jnp.minimum(step, 2))
        cross_ref[...] = product[rows:, :]
        raw = product[:rows, :]
        raw_ref[...] = raw.astype(bf16)
        value = raw * scale
        for t in range(peers):
            head = value[:, t * HD : (t + 1) * HD]
            rotated = head * cos_ref[...] + pltpu.roll(head, HALF, 1) * sin_ref[...]
            head = jnp.where(layer != 1, rotated, head).astype(bf16)
            place = t ^ scalars[0]
            for d, block in enumerate(blocks):

                @pl.when(place == d)
                def _(block=block, head=head):
                    block[layer] = head

        x_all[rows:, :] = x_next


def project_heads(order, x, gain, weights, a_t, b, m, cosine, sine):
    rows, depth = x.shape
    width = weights[0].shape[1]
    heads = width // HD
    merged_at = lambda i, s: (0, jnp.minimum(i, 2))
    done_at = lambda i, s: (0, jnp.maximum(i - 1, 0))
    fixed = lambda *shape: pl.BlockSpec(shape, lambda i, s: (0,) * len(shape))
    out_shape = [jax.ShapeDtypeStruct((3, rows, HD), bf16)] * heads
    out_shape += [
        jax.ShapeDtypeStruct((rows, depth), bf16),
        jax.ShapeDtypeStruct((depth, 3 * width), bf16),
        jax.ShapeDtypeStruct((rows, 3 * width), bf16),
        jax.ShapeDtypeStruct((1, 3 * width), f32),
        jax.ShapeDtypeStruct((1, 3 * width), f32),
        jax.ShapeDtypeStruct((RANK, 3 * width), f32),
    ]
    outs = pl.pallas_call(
        heads_kernel,
        grid_spec=pltpu.PrefetchScalarGridSpec(
            num_scalar_prefetch=1,
            grid=(4,),
            in_specs=[
                fixed(rows, depth),
                fixed(1, depth),
                fixed(3, RANK, depth),
                fixed(3, RANK, width),
                fixed(3, 1, width),
                fixed(rows, HD),
                fixed(rows, HD),
            ]
            + [pl.BlockSpec(memory_space=pl.ANY)] * 3,
            out_specs=[fixed(3, rows, HD)] * heads
            + [
                fixed(rows, depth),
                pl.BlockSpec((depth, width), merged_at),
                pl.BlockSpec((rows, width), done_at),
                pl.BlockSpec((1, width), merged_at),
                pl.BlockSpec((1, width), merged_at),
                pl.BlockSpec((RANK, width), done_at),
            ],
            scratch_shapes=[
                pltpu.VMEM((rows + RANK, depth), bf16),
                pltpu.VMEM((3, depth, width), bf16),
                pltpu.VMEM((2, depth, width), bf16),
                pltpu.VMEM((2, 1, width), f32),
                pltpu.VMEM((2, 1, width), f32),
                pltpu.SemaphoreType.DMA((3,)),
            ],
        ),
        out_shape=out_shape,
        compiler_params=pltpu.CompilerParams(vmem_limit_bytes=VMEM_LIMIT),
        cost_estimate=cost(6 * rows * depth * width, 16 * rows * depth),
        name="project_heads",
    )(order, x, gain, a_t, b, m, cosine, sine, *weights)
    return outs[:heads], *outs[heads:]


def assemble_kernel(peers, chunks, scalars, *refs):
    take = taker(refs)
    heads = take(peers)
    out_ref, down_ref, a_ref = take(3)
    near_refs = refs[peers + 3 :]
    width = a_ref.shape[1]
    parts = out_ref.shape[1] // width
    part = heads[0].shape[0] // chunks
    for d in range(peers):
        at = pl.ds(pl.multiple_of((scalars[0] ^ d) * HD, HD), HD)
        for c in range(chunks):
            near_refs[c][:part, at] = heads[d][c * part : (c + 1) * part, :]
    rows = []
    for ref in (out_ref, down_ref):
        high = ref[...].astype(bf16).astype(f32)
        for value in (high, ref[...] - high):
            rows += [value[:, j * width : (j + 1) * width] for j in range(parts)]
    near_refs[0][part : part + RANK, :] = jnp.concatenate(rows, axis=0).astype(bf16)
    near_refs[0][part + RANK :, :] = a_ref[...].astype(bf16)


def assemble(order, heads, square_out, square_down, a_t, chunks):
    peers = len(heads)
    part = heads[0].shape[0] // chunks
    width = peers * HD
    operands = [*heads, square_out, square_down, a_t]
    heights = [part + 2 * RANK] + [part] * (chunks - 1)
    out_shape = [jax.ShapeDtypeStruct((height, width), bf16) for height in heights]
    return pl.pallas_call(
        functools.partial(assemble_kernel, peers, chunks),
        grid_spec=pltpu.PrefetchScalarGridSpec(
            num_scalar_prefetch=1,
            grid=(1,),
            in_specs=[whole_spec(x) for x in operands],
            out_specs=[whole_spec(x) for x in out_shape],
        ),
        out_shape=out_shape,
        compiler_params=pltpu.CompilerParams(vmem_limit_bytes=VMEM_LIMIT),
        cost_estimate=cost(0, 0),
        name="assemble",
    )(order, *operands)


def unpack_kernel(size, scalars, *refs):
    take = taker(refs)
    blocks, m_refs = take(size), take(2)
    column_refs, scale_refs, (a_ref,) = take(2), take(2), take(1)
    width = blocks[0].shape[1]
    total = jnp.zeros((RANK, width), f32)
    for device in range(size):
        value = blocks[0][:RANK, :]
        for c in range(1, size):
            here = lax.rem(scalars[0] + c, size) == device
            value = jnp.where(here, blocks[c][:RANK, :], value)
        total = total + value.astype(f32)
    for side in range(2):
        for j in range(size):
            row = 2 * side * size + j
            square = total[row : row + 1, :] + total[row + size : row + size + 1, :]
            at = slice(j * width, (j + 1) * width)
            column = jnp.sqrt(square)
            column_refs[side][:, at] = column
            scale_refs[side][:, at] = m_refs[side][:, at] / column
    for c in range(size):
        device = lax.rem(scalars[0] + c, size)
        at = pl.ds(pl.multiple_of(device * width, HD), width)
        a_ref[:, at] = blocks[c][RANK:, :]


def unpack(k, blocks, rows, m_out, m_down):
    size = len(blocks)
    width = blocks[0].shape[1]
    wide = size * width
    row = jax.ShapeDtypeStruct((1, wide), f32)
    out_shape = [row] * 4 + [jax.ShapeDtypeStruct((RANK, wide), bf16)]
    tail = pl.BlockSpec((2 * RANK, width), lambda i, s: (rows // (2 * RANK), 0))
    return pl.pallas_call(
        functools.partial(unpack_kernel, size),
        grid_spec=pltpu.PrefetchScalarGridSpec(
            num_scalar_prefetch=1,
            grid=(1,),
            in_specs=[tail] * size + [whole_spec(m_out), whole_spec(m_down)],
            out_specs=[whole_spec(x) for x in out_shape],
        ),
        out_shape=out_shape,
        compiler_params=pltpu.CompilerParams(vmem_limit_bytes=VMEM_LIMIT),
        cost_estimate=cost(0, 0),
        name="unpack",
    )(k, *blocks, m_out, m_down)


def block_kernel(sizes, size, scalars, *refs):
    take = taker(refs)
    x_refs = take(size)
    a_ref, hid_ref, b_ref, out_scale_ref, gain_ref = take(5)
    cot_ref, down_scale_ref, scale_ref, wo_hbm, w_hbm, wd_hbm = take(6)
    hnorm_ref, resid_ref, raw_own_ref, low_ref, own_ref = take(5)
    act_ref, dz_ref, g_ref, dh_ref = take(4)
    total, through, dz_down, wo_all, w_all, wd_all, out_sem, sem, down_sem = take(9)
    k = scalars[0]
    rows, width = x_refs[0].shape
    part = rows // size
    starts = [sum(sizes[:j]) for j in range(len(sizes))]

    def out_copy(c):
        source = pl.ds(pl.multiple_of(lax.rem(k + c, size) * width, HD), width)
        return pltpu.make_async_copy(wo_hbm.at[source, :], wo_all.at[c], out_sem.at[c])

    def copies(j):
        both = pl.ds(2 * starts[j], 2 * sizes[j])
        one = pl.ds(starts[j], sizes[j])
        return (
            pltpu.make_async_copy(wd_hbm.at[one, :], wd_all.at[one, :], down_sem.at[j]),
            pltpu.make_async_copy(w_hbm.at[:, both], w_all.at[:, both], sem.at[j]),
        )

    for c in range(size):
        out_copy(c).start()
    for j in range(len(sizes)):
        for copy in copies(j):
            copy.start()
    for i in range(size):
        cot = cot_ref[i, 0].astype(f32)
        dz_down[i * part : (i + 1) * part, :] = (cot * down_scale_ref[...]).astype(bf16)

    mine = pl.ds(pl.multiple_of(k * part, 16), part)
    for c, x_ref in enumerate(x_refs):
        at = pl.ds(pl.multiple_of(lax.rem(k + c, size) * width, HD), width)
        own_ref[:, at] = x_ref[mine, :]
        out_copy(c).wait()
        x = x_ref[...]
        product = dot(x, wo_all[c])
        rank_part = dot_nt(x, a_ref[:, at])
        total[...] = total[...] + product if c else product
        through[...] = through[...] + rank_part if c else rank_part
    for piece in range(size):
        at = pl.ds(piece * part, part)
        low = through[at, :].astype(bf16)
        raw = total[at, :] + dot(low, b_ref[...])
        resid = hid_ref[piece, 0].astype(f32) + raw * out_scale_ref[...]
        inverse = lax.rsqrt(jnp.mean(resid * resid, axis=-1, keepdims=True) + EPS)
        hnorm_ref[at, :] = (resid * inverse * gain_ref[...]).astype(bf16)

        @pl.when(k == piece)
        def _(resid=resid, raw=raw, low=low):
            resid_ref[...] = resid
            raw_own_ref[...] = raw
            low_ref[...] = low

    def products(j):
        for copy in copies(j):
            copy.wait()
        both = slice(2 * starts[j], 2 * (starts[j] + sizes[j]))
        one = slice(starts[j], starts[j] + sizes[j])
        return dot(hnorm_ref[...], w_all[:, both]), dot_nt(dz_down[...], wd_all[one, :])

    ready = products(0)
    for j in range(len(sizes)):
        v, dact_all = ready
        if j + 1 < len(sizes):
            ready = products(j + 1)
        for i in range(sizes[j] // HD):
            hidden = starts[j] + i * HD
            gate_at = slice(2 * hidden, 2 * hidden + HD)
            up_at = slice(2 * hidden + HD, 2 * hidden + 2 * HD)
            raw_gate = v[:, 2 * i * HD : (2 * i + 1) * HD]
            raw_up = v[:, (2 * i + 1) * HD : (2 * i + 2) * HD]
            dact = dact_all[:, i * HD : (i + 1) * HD]
            scale_gate, scale_up = scale_ref[:, gate_at], scale_ref[:, up_at]
            gate = raw_gate * scale_gate
            up = raw_up * scale_up
            sigmoid = 1.0 / (1.0 + jnp.exp(-gate))
            silu = gate * sigmoid
            dgate = dact * up * (sigmoid + silu * (1.0 - sigmoid))
            dup = dact * silu
            act_ref[:, hidden : hidden + HD] = (silu * up).astype(bf16)
            g_ref[:, gate_at] = jnp.sum(dgate * raw_gate, axis=0, keepdims=True)
            g_ref[:, up_at] = jnp.sum(dup * raw_up, axis=0, keepdims=True)
            dz_ref[:, gate_at] = (dgate * scale_gate).astype(bf16)
            dz_ref[:, up_at] = (dup * scale_up).astype(bf16)
    dh_ref[...] = dot_nt(dz_ref[...], w_all[...]).astype(bf16)


def block(k, chunk, x, a_t, hidden, b2, out_scale, gain, cotangent, down_scale, scale, wo, w, wd):
    size, _, part, wide = hidden.shape
    rows, width = size * part, x[0].shape[1]
    ff = wd.shape[0]
    sizes = [ff]
    fixed = lambda *shape: pl.BlockSpec(shape, lambda i, s: (0,) * len(shape))
    view = pl.BlockSpec((size, 1, part, wide), lambda i, s: (0, chunk, 0, 0))
    shapes = [
        ((rows, wide), bf16),
        ((part, wide), f32),
        ((part, wide), f32),
        ((part, RANK), bf16),
        ((part, size * width), bf16),
        ((rows, ff), bf16),
        ((rows, 2 * ff), bf16),
        ((1, 2 * ff), f32),
        ((rows, wide), bf16),
    ]
    return pl.pallas_call(
        functools.partial(block_kernel, sizes, size),
        grid_spec=pltpu.PrefetchScalarGridSpec(
            num_scalar_prefetch=1,
            grid=(1,),
            in_specs=[fixed(rows, width)] * size
            + [
                fixed(RANK, size * width),
                view,
                fixed(RANK, wide),
                fixed(1, wide),
                fixed(1, wide),
                view,
                fixed(1, wide),
                fixed(1, 2 * ff),
            ]
            + [pl.BlockSpec(memory_space=pl.ANY)] * 3,
            out_specs=[fixed(*shape) for shape, _ in shapes],
            scratch_shapes=[
                pltpu.VMEM((rows, wide), f32),
                pltpu.VMEM((rows, RANK), f32),
                pltpu.VMEM((rows, wide), bf16),
                pltpu.VMEM((size, width, wide), bf16),
                pltpu.VMEM((wide, 2 * ff), bf16),
                pltpu.VMEM((ff, wide), bf16),
                pltpu.SemaphoreType.DMA((size,)),
                pltpu.SemaphoreType.DMA((len(sizes),)),
                pltpu.SemaphoreType.DMA((len(sizes),)),
            ],
        ),
        out_shape=[jax.ShapeDtypeStruct(shape, kind) for shape, kind in shapes],
        compiler_params=pltpu.CompilerParams(vmem_limit_bytes=60 * MIB),
        cost_estimate=cost(10 * rows * wide * ff, 6 * wide * ff),
        name="block",
    )(k, *x, a_t, hidden, b2, out_scale, gain, cotangent, down_scale, scale, wo, w, wd)


def back_out_kernel(scalars, *refs):
    take = taker(refs)
    earlier = take(len(refs) - 18)
    piece_ref, cot_ref, resid_ref, raw_ref, gain_ref, scale_ref = take(6)
    b_ref, own_ref, low_ref, w_ref, a_ref = take(5)
    dattn_ref, dresid_ref, dz_ref, g_ref, ap_ref, pb_ref = take(6)
    (through,) = take(1)

    @pl.when(pl.program_id(0) == 0)
    def _():
        grad = piece_ref[...].astype(f32)
        resid = resid_ref[...]
        inverse = lax.rsqrt(jnp.mean(resid * resid, axis=-1, keepdims=True) + EPS)
        scaled = grad * gain_ref[...]
        lean = jnp.mean(resid * scaled, axis=-1, keepdims=True)
        dresid = cot_ref[0, 0].astype(f32) + inverse * scaled
        dresid = dresid - resid * (inverse * inverse * inverse * lean)
        dresid_ref[...] = dresid
        dz = (dresid * scale_ref[...]).astype(bf16)
        dz_ref[...] = dz
        through[...] = dot_nt(dz, b_ref[...]).astype(bf16)
        sums = [
            jnp.sum(dresid * raw_ref[...], axis=0, keepdims=True),
            dot_tn(low_ref[...], dz),
            dot_tn(through[...], own_ref[...]),
        ]
        for i, ref in enumerate((g_ref, ap_ref, pb_ref)):
            ref[...] = sums[i] + earlier[i][...] if earlier else sums[i]

    dattn = dot_nt(dz_ref[...], w_ref[...]) + dot(through[...], a_ref[...])
    dattn_ref[0] = dattn.astype(bf16)


def back_out(k, chunk, piece, cotangent, resid, raw, gain, scale, b, own, low, w, a2_t, earlier):
    size = cotangent.shape[0]
    part, wide = resid.shape
    width = w.shape[0] // size
    fixed = lambda *shape: pl.BlockSpec(shape, lambda i, s: (0,) * len(shape))
    return pl.pallas_call(
        back_out_kernel,
        grid_spec=pltpu.PrefetchScalarGridSpec(
            num_scalar_prefetch=1,
            grid=(size,),
            in_specs=[fixed(*x.shape) for x in earlier]
            + [
                fixed(part, wide),
                pl.BlockSpec((1, 1, part, wide), lambda i, s: (s[0], chunk, 0, 0)),
                fixed(part, wide),
                fixed(part, wide),
                fixed(1, wide),
                fixed(1, wide),
                fixed(RANK, wide),
                fixed(*own.shape),
                fixed(part, RANK),
                pl.BlockSpec((width, wide), lambda i, s: (lax.rem(i + s[0], size), 0)),
                pl.BlockSpec((RANK, width), lambda i, s: (0, lax.rem(i + s[0], size))),
            ],
            out_specs=[
                pl.BlockSpec((1, part, width), lambda i, s: (i, 0, 0)),
                fixed(part, wide),
                fixed(part, wide),
                fixed(1, wide),
                fixed(RANK, wide),
                fixed(RANK, size * width),
            ],
            scratch_shapes=[pltpu.VMEM((part, RANK), bf16)],
        ),
        out_shape=[
            jax.ShapeDtypeStruct((size, part, width), bf16),
            jax.ShapeDtypeStruct((part, wide), f32),
            jax.ShapeDtypeStruct((part, wide), bf16),
            jax.ShapeDtypeStruct((1, wide), f32),
            jax.ShapeDtypeStruct((RANK, wide), f32),
            jax.ShapeDtypeStruct((RANK, size * width), f32),
        ],
        compiler_params=pltpu.CompilerParams(vmem_limit_bytes=VMEM_LIMIT),
        cost_estimate=cost(2 * part * width * size * wide, 2 * width * size * wide),
        name="back_out",
    )(k, *earlier, piece, cotangent, resid, raw, gain, scale, b, own, low, w, a2_t)


def unproject_kernel(heads, scalars, cos_ref, sin_ref, raw_ref, scale_ref, w_ref, *refs):
    take = taker(refs)
    grads = take(heads)
    dz_ref, g_ref, out_ref = refs[heads:]
    width = heads * HD

    @pl.when(pl.program_id(0) == 0)
    def _():
        for layer in range(3):
            for d in range(heads):
                at = pl.ds(pl.multiple_of(layer * width + (scalars[0] ^ d) * HD, HD), HD)
                grad = grads[d][layer].astype(f32)
                if layer != 1:
                    grad = grad * cos_ref[...] - pltpu.roll(grad, HALF, 1) * sin_ref[...]
                raw = raw_ref[:, at].astype(f32)
                g_ref[:, at] = jnp.sum(grad * raw, axis=0, keepdims=True)
                dz_ref[:, at] = (grad * scale_ref[:, at]).astype(bf16)

    out_ref[...] = dot_nt(dz_ref[...], w_ref[...]).astype(bf16)


def unproject(order, cosine, sine, raw, scale, w, grads):
    operands = [cosine, sine, raw, scale]
    rows, wide = raw.shape
    depth = w.shape[0]
    step = 8 * HD
    return pl.pallas_call(
        functools.partial(unproject_kernel, len(grads)),
        grid_spec=pltpu.PrefetchScalarGridSpec(
            num_scalar_prefetch=1,
            grid=(depth // step,),
            in_specs=[whole_spec(x) for x in operands]
            + [pl.BlockSpec((step, wide), lambda i, s: (i, 0))]
            + [whole_spec(x) for x in grads],
            out_specs=[
                whole_spec(raw),
                whole_spec(scale),
                pl.BlockSpec((rows, step), lambda i, s: (0, i)),
            ],
        ),
        out_shape=[
            jax.ShapeDtypeStruct(raw.shape, bf16),
            jax.ShapeDtypeStruct(scale.shape, f32),
            jax.ShapeDtypeStruct((rows, depth), bf16),
        ],
        compiler_params=pltpu.CompilerParams(vmem_limit_bytes=VMEM_LIMIT),
        cost_estimate=cost(2 * rows * wide * depth, 2 * wide * depth),
        name="unproject",
    )(order, *operands, w, *grads)


def shares_kernel(count, chunks, span, *refs):
    take = taker(refs)
    x_refs, dz_refs = take(chunks), take(chunks)
    a_ref, b_ref, w_ref, cross_ref, g_ref, m_ref, column_ref = take(7)
    share_a_ref, share_b_ref = take(2)
    low, up, radial = take(3)
    step = pl.program_id(0)
    wide = b_ref.shape[1]

    @pl.when(step == 0)
    def _():
        up[...] = jnp.zeros_like(up)
        radial[...] = jnp.zeros_like(radial)
        for c in range(chunks):
            low[c] = dot_nt(x_refs[c][...], a_ref[...]).astype(bf16)

    shrink = g_ref[...] * m_ref[...] / (column_ref[...] * column_ref[...] * column_ref[...])
    shape = (count * RANK, wide)
    column = lax.broadcasted_iota(jnp.int32, shape, 1) + step * wide
    layer_of = lax.rem(column // span, count)
    own = (lax.broadcasted_iota(jnp.int32, shape, 0) // RANK) == layer_of
    b_pad = jnp.where(own, jnp.concatenate([b_ref[...]] * count, axis=0), 0.0)
    b_low = b_pad.astype(bf16)
    ap = jnp.zeros(shape, f32)
    for c in range(chunks):
        dz = dz_refs[c][...]
        up[c] += dot_nt(dz, b_low)
        ap += dot_tn(low[c], dz)
    radial[...] += dot_nt((b_pad * shrink).astype(bf16), w_ref[...])
    ap = jnp.where(own, ap, 0.0)
    picked = ap[:RANK]
    for i in range(1, count):
        picked = picked + ap[i * RANK : (i + 1) * RANK]
    share_b_ref[...] = (SCALING * (picked - cross_ref[...] * shrink)).astype(bf16)

    @pl.when(step == pl.num_programs(0) - 1)
    def _():
        total = -radial[...]
        for c in range(chunks):
            total = total + dot_tn(up[c].astype(bf16), x_refs[c][...])
        share_a_ref[...] = (SCALING * total).astype(bf16)


def layer_shares(inputs, a_t, dz, b, span, merged, cross, g, magnitude, column):
    chunks = len(inputs)
    rows, depth = inputs[0].shape
    width = dz[0].shape[1]
    count = a_t.shape[0] // RANK
    step = width // count
    columns = lambda height: pl.BlockSpec((height, step), lambda i: (0, i))
    fixed = lambda x: pl.BlockSpec(x.shape, lambda i: (0, 0))
    return pl.pallas_call(
        functools.partial(shares_kernel, count, chunks, span),
        grid=(width // step,),
        in_specs=[fixed(x) for x in inputs]
        + [columns(rows)] * chunks
        + [fixed(a_t), columns(RANK), columns(depth), columns(RANK)]
        + [columns(1)] * 3,
        out_specs=[fixed(a_t), columns(RANK)],
        out_shape=[
            jax.ShapeDtypeStruct(a_t.shape, bf16),
            jax.ShapeDtypeStruct((RANK, width), bf16),
        ],
        scratch_shapes=[
            pltpu.VMEM((chunks, rows, count * RANK), bf16),
            pltpu.VMEM((chunks, rows, count * RANK), f32),
            pltpu.VMEM(a_t.shape, f32),
        ],
        compiler_params=pltpu.CompilerParams(vmem_limit_bytes=VMEM_LIMIT),
        cost_estimate=cost(rows * depth * 64, depth * width),
        name="shares",
    )(*inputs, *dz, a_t.astype(bf16), b, merged, cross, g, magnitude, column)


def down_kernel(chunks, *refs):
    take = taker(refs)
    act_refs = take(chunks)
    w_ref, cot_ref, scale_ref, a_ref, b_ref = take(5)
    raw_ref, g_ref, ap_ref, pb_ref = take(4)
    low, up = take(2)
    step = pl.program_id(0)
    rows = act_refs[0].shape[0]
    size, _, part, wide = cot_ref.shape

    @pl.when(step == 0)
    def _():
        up[...] = jnp.zeros_like(up)
        for c in range(chunks):
            low[c] = dot_nt(act_refs[c][...], a_ref[...]).astype(bf16)

    g = jnp.zeros((1, wide), f32)
    ap = jnp.zeros((RANK, wide), f32)
    b_low = b_ref[...].astype(bf16)
    for c in range(chunks):
        raw = dot(act_refs[c][...], w_ref[...])
        raw_ref[:, c] = raw.astype(bf16).reshape(size, part, wide)
        cot = cot_ref[:, c].reshape(rows, wide).astype(f32)
        g += jnp.sum(cot * raw, axis=0, keepdims=True)
        dz = (cot * scale_ref[...]).astype(bf16)
        up[c] += dot_nt(dz, b_low)
        ap += dot_tn(low[c], dz)
    g_ref[...] = g
    ap_ref[...] = ap.astype(bf16)

    @pl.when(step == pl.num_programs(0) - 1)
    def _():
        total = jnp.zeros(pb_ref.shape, f32)
        for c in range(chunks):
            total = total + dot_tn(up[c].astype(bf16), act_refs[c][...])
        pb_ref[...] = total.astype(bf16)


def down_project(acts, w, cotangent, scale, a_t, b):
    chunks = len(acts)
    rows, ff = acts[0].shape
    wide = w.shape[1]
    step = 2 * HD
    size, _, part, _ = cotangent.shape
    columns = lambda height: pl.BlockSpec((height, step), lambda i: (0, i))
    fixed = lambda *shape: pl.BlockSpec(shape, lambda i: (0,) * len(shape))
    view = pl.BlockSpec((size, chunks, part, step), lambda i: (0, 0, 0, i))
    return pl.pallas_call(
        functools.partial(down_kernel, chunks),
        grid=(wide // step,),
        in_specs=[fixed(rows, ff)] * chunks
        + [columns(ff), view, columns(1), fixed(RANK, ff), columns(RANK)],
        out_specs=[view, columns(1), columns(RANK), fixed(RANK, ff)],
        out_shape=[
            jax.ShapeDtypeStruct(cotangent.shape, bf16),
            jax.ShapeDtypeStruct((1, wide), f32),
            jax.ShapeDtypeStruct((RANK, wide), bf16),
            jax.ShapeDtypeStruct((RANK, ff), bf16),
        ],
        scratch_shapes=[
            pltpu.VMEM((chunks, rows, RANK), bf16),
            pltpu.VMEM((chunks, rows, RANK), f32),
        ],
        compiler_params=pltpu.CompilerParams(vmem_limit_bytes=VMEM_LIMIT),
        cost_estimate=cost(2 * chunks * rows * ff * wide, 2 * ff * wide),
        name="down_project",
    )(*acts, w, cotangent, scale, a_t.astype(bf16), b)


def pack_kernel(plan, scalars, *refs):
    out_ref = refs[-1]
    out_ref[...] = jnp.zeros_like(out_ref)
    for ref, (parts, placed, rows) in zip(refs[:-1], plan):
        height, width = ref.shape
        wide = width // parts
        lanes = slice(0, wide)
        if placed:
            lanes = pl.ds(pl.multiple_of(scalars[0] * wide, HD), wide)
        if height == 1:
            value = [ref[:, i * wide : (i + 1) * wide].astype(f32) for i in range(parts)]
            value.append(jnp.zeros((RANK - parts, wide), f32))
            value = jnp.concatenate(value, axis=0).astype(bf16)
            out_ref[rows[0] : rows[0] + RANK, lanes] = value
            continue
        for i in range(parts):
            for j in range(height // RANK):
                row = rows[i * (height // RANK) + j]
                value = ref[j * RANK : (j + 1) * RANK, i * wide : (i + 1) * wide].astype(bf16)
                out_ref[row : row + RANK, lanes] = value


def pack(k, height, width, *entries):
    arrays = [entry[0] for entry in entries]
    plan = [entry[1:] for entry in entries]
    return pl.pallas_call(
        functools.partial(pack_kernel, plan),
        grid_spec=pltpu.PrefetchScalarGridSpec(
            num_scalar_prefetch=1,
            grid=(1,),
            in_specs=[whole_spec(x) for x in arrays],
            out_specs=pl.BlockSpec((height, width), lambda i, s: (0, 0)),
        ),
        out_shape=jax.ShapeDtypeStruct((height, width), bf16),
        compiler_params=pltpu.CompilerParams(vmem_limit_bytes=VMEM_LIMIT),
        cost_estimate=cost(height * width, 4 * height * width),
        name="pack",
    )(k, *arrays)


def span_positions(row_ids, span_order, span_len):
    slot_ids = row_ids // span_len
    slot_table = jnp.arange(span_order.shape[0], dtype=jnp.int32)
    picked = jnp.sum(
        jnp.where(slot_ids[:, None] == slot_table[None, :], span_order[None, :], 0), axis=1
    )
    return picked * span_len + row_ids % span_len


def rotary_tables(positions):
    lane = np.arange(HD)
    frequency = (ROPE_BASE ** (-2.0 * (lane % HALF) / HD)).astype(np.float32)
    sign = np.where(lane < HALF, -1.0, 1.0).astype(np.float32)
    angles = positions.astype(f32)[:, None] * frequency[None, :]
    return jnp.cos(angles), jnp.sin(angles) * sign[None, :]


def pick_blocks(blocks, index):
    out = blocks[0]
    for i in range(1, len(blocks)):
        out = jnp.where(index == i, blocks[i], out)
    return out


def inverse_rms(values):
    return lax.rsqrt(jnp.mean(values * values, axis=-1, keepdims=True) + EPS)


def rms_backward(values, gain_vec, grad_in, inverse):
    scaled = grad_in * gain_vec
    return inverse * scaled - values * inverse * inverse * inverse * jnp.mean(
        values * scaled, axis=-1, keepdims=True
    )


def per_device(
    hidden_in,
    cotangent,
    segment_ids,
    padding,
    span_order,
    gain_attn,
    gain_mlp,
    w_query,
    w_key,
    w_value,
    w_out,
    w_gate,
    w_up,
    w_down,
    a_query,
    b_query,
    m_query,
    a_key,
    b_key,
    m_key,
    a_value,
    b_value,
    m_value,
    a_out,
    b_out,
    m_out,
    a_gate,
    b_gate,
    m_gate,
    a_up,
    b_up,
    m_up,
    a_down,
    b_down,
    m_down,
):
    rows, width = hidden_in.shape
    span_len = rows // 2
    near_width = w_query.shape[1]
    peers = near_width // HD
    n_mp = lax.axis_size("mp")
    n_seq = lax.axis_size("seq")
    n_doc = lax.axis_size("doc")
    groups = n_seq // peers
    copies = n_seq * n_doc
    share = rows // n_mp
    chunks = CHUNKS
    part = share // chunks
    k = lax.axis_index("mp")
    doc = lax.axis_index("doc")
    seq = lax.axis_index("seq")
    me = lax.rem(seq, peers)
    my_group = seq // peers
    order = jnp.reshape(me, (1,)).astype(jnp.int32)
    k_scalar = jnp.reshape(k, (1,)).astype(jnp.int32)

    slice_rows = near_width // n_doc
    wo_slice = lax.dynamic_slice_in_dim(w_out, doc * slice_rows, slice_rows, 0)
    wo_all = lax.all_gather(wo_slice, ("mp", "doc"), axis=0, tiled=True)

    slots = [
        2 * (my_group * peers + (me ^ d)) + half for d in range(peers) for half in range(2)
    ]
    slots += [
        2 * (g * peers + (me ^ d)) + half
        for g in range(groups)
        for d in range(peers)
        for half in range(2)
    ]
    slots = jnp.stack(slots)
    table = jnp.arange(span_order.shape[0], dtype=jnp.int32)
    places = jnp.sum(jnp.where(slots[:, None] == table[None, :], span_order[None, :], 0), axis=1)
    scalars = jnp.concatenate([places, k_scalar]).astype(jnp.int32)
    row_ids = jnp.arange(rows, dtype=jnp.int32) + seq * rows
    cosine, sine = rotary_tables(span_positions(row_ids, span_order, span_len))
    codes = seq_exchange([segment_ids * 2 + padding] * peers)
    (hidden_next,) = after([hidden_in], *codes)

    a_heads = jnp.stack([a_key.T, a_value.T, a_query.T])
    b_heads = [b_key, b_value, b_query]
    m_heads = jnp.concatenate([m_key, m_value, m_query])[None, :]
    blocks, normed, wh_low, raw_heads, column_heads, scale_heads, cross_heads = project_heads(
        order,
        hidden_next,
        gain_attn[None, :],
        (w_key, w_value, w_query),
        a_heads,
        jnp.stack(b_heads),
        jnp.stack([m_key, m_value, m_query])[:, None, :],
        cosine,
        sine,
    )
    heads = seq_exchange(blocks)

    codes = [x.reshape(rows, 1) for x in codes]
    w_out_next, w_down_next, w_gate_next, w_up_next = after(
        [w_out, w_down, w_gate, w_up], raw_heads
    )
    (
        square_out,
        cross_out,
        square_down,
        cross_down,
        wd_low,
        wgu_low,
        cross_gu,
        column_gu,
        scale_gu,
        m_gu,
        b_gu,
    ) = merge_others(
        (w_out_next, a_out.T, b_out),
        (w_down_next, a_down.T, b_down),
        (w_gate_next, a_gate.T, b_gate, m_gate[None, :]),
        (w_up_next, a_up.T, b_up, m_up[None, :]),
    )

    extra = []
    if groups > 1:
        members = [[g * peers + i for g in range(groups)] for i in range(peers)]
        gather = lambda x: lax.all_gather(
            x[None], "seq", axis=0, tiled=True, axis_index_groups=members
        )
        extra = [gather(jnp.stack([x[:2] for x in heads])), gather(jnp.stack(codes))]
    heads_next = after(heads, square_out)
    o_blocks, lse = attention_forward(
        scalars, heads_next, codes, extra, groups, n_mp, chunks
    )
    o_heads = seq_exchange(o_blocks)
    near_chunks = assemble(order, o_heads, square_out, square_down, a_out.T, chunks)

    def chunked(values):
        return values.reshape(n_mp, chunks, part, values.shape[-1])

    hid_view, cot_view = chunked(hidden_in), chunked(cotangent)
    b_out_low = b_out.astype(bf16)
    acts, hnorms, dz_gus, dh_chunks = [], [], [], []
    resid_own, raw_out_own, out_low_own, near_own = [], [], [], []
    g_gu = 0.0
    lines = ([near_chunks[0]], [near_chunks[0]])
    for step in range(1, n_mp):
        line_step(*lines, step)
    gathered_chunks = [line_blocks(*lines)]
    for c in range(1, chunks):
        (near_next,) = after([near_chunks[c]], wo_all, *gathered_chunks[0])
        others = lax.all_gather(near_next, "mp", axis=0)
        gathered_chunks.append(
            [near_chunks[c]]
            + [
                lax.dynamic_index_in_dim(others, lax.rem(k + i, n_mp), 0, keepdims=False)
                for i in range(1, n_mp)
            ]
        )
    column_out, column_down, scale_out, scale_down, a_out_low = unpack(
        k_scalar, gathered_chunks[0], n_mp * part, m_out[None, :], m_down[None, :]
    )
    a_out_twice = SCALING * a_out_low
    for c in range(chunks):
        gathered = gathered_chunks[c]
        if c > 0:
            gathered = after(gathered, dh_chunks[-1])
        hnorm, resid, raw_out, out_low, own, act, dz_gu, g, dh = block(
            k_scalar,
            c,
            gathered,
            a_out_low,
            hid_view,
            (SCALING * b_out).astype(bf16),
            scale_out,
            gain_mlp[None, :],
            cot_view,
            scale_down,
            scale_gu,
            wo_all,
            wgu_low,
            wd_low,
        )
        g_gu = g_gu + g
        dh_chunks.append(dh)
        acts.append(act)
        hnorms.append(hnorm)
        dz_gus.append(dz_gu)
        resid_own.append(resid)
        raw_out_own.append(raw_out)
        out_low_own.append(out_low)
        near_own.append(own)

    def scatter(parts):
        return lax.psum_scatter(parts, "mp", scatter_dimension=0, tiled=True)

    pieces = [scatter(x) for x in dh_chunks]

    arrived, dresid_own, dz_out = [], [], []
    out_sums = ()
    earlier = dh_chunks[-1]
    for c in range(chunks):
        (own_piece,) = after([pieces[c]], earlier)
        dattn, dresid, dz, *out_sums = back_out(
            k_scalar,
            c,
            own_piece,
            cot_view,
            resid_own[c],
            raw_out_own[c],
            gain_mlp[None, :],
            scale_out,
            b_out_low,
            near_own[c],
            out_low_own[c],
            wo_all,
            a_out_twice,
            out_sums,
        )
        arrived.append(dattn[0])
        for shift in range(1, n_mp):
            pairs = [(i, (i + shift) % n_mp) for i in range(n_mp)]
            arrived.append(lax.ppermute(dattn[shift], "mp", pairs))
        dresid_own.append(dresid)
        dz_out.append(dz)
        earlier = dz
        if c == 0:
            acts_next = after(acts, dz)
            raw_down, g_down, ap_down, pb_down = down_project(
                acts_next, wd_low, cot_view, scale_down, a_down.T, b_down
            )
            earlier = (g_down, *arrived[1:])
    arrived = jnp.concatenate(arrived, axis=0)
    by_head = [arrived[:, h * HD : (h + 1) * HD] for h in range(peers)]
    grad_blocks = seq_exchange([pick_blocks(by_head, me ^ d) for d in range(peers)])
    dresid_own = jnp.concatenate(dresid_own, axis=0)
    g_out, ap_out, pb_out = out_sums

    grads, dkv = attention_backward(
        scalars, heads_next, codes, extra, o_blocks, grad_blocks, lse, groups, n_mp, chunks
    )
    if groups > 1:
        members = [[g * peers + i for g in range(groups)] for i in range(peers)]
        dkv = lax.psum_scatter(
            dkv, "seq", scatter_dimension=0, tiled=True, axis_index_groups=members
        )
        grads = [jnp.concatenate([dkv[0, d], grads[d]], axis=0) for d in range(peers)]
    head_grads = seq_exchange(grads)

    hnorms_next, dz_gus_next = after([tuple(hnorms), tuple(dz_gus)], grads[0])
    share_a_gu, share_b_gu = layer_shares(
        hnorms_next,
        jnp.concatenate([a_gate.T, a_up.T], axis=0),
        dz_gus_next,
        b_gu,
        HD,
        wgu_low,
        cross_gu,
        g_gu,
        m_gu,
        column_gu,
    )
    (raw_down,) = after([raw_down], *grad_blocks)
    down_own = scatter(raw_down.reshape(rows, width))
    head_grads = after(head_grads, share_a_gu)

    dz_heads, g_heads, dnormed = unproject(
        order, cosine, sine, raw_heads, scale_heads, wh_low, head_grads
    )
    dnormed_own = scatter(dnormed)

    (down_own,) = after([down_own], dnormed)
    result = jnp.concatenate(resid_own, axis=0) + down_own.astype(f32) * scale_down
    hidden_own = lax.dynamic_slice_in_dim(hidden_in, k * share, share, 0).astype(f32)


    share_a_heads, share_b_heads = layer_shares(
        [normed],
        a_heads.reshape(3 * RANK, width),
        [dz_heads],
        jnp.concatenate(b_heads, axis=1),
        near_width,
        wh_low,
        cross_heads,
        g_heads,
        m_heads,
        column_heads,
    )
    parts = n_doc * peers
    part_rows = 3 * RANK
    summed = [(u // 2) * part_rows + (u % 2) * RANK for u in range(2 * parts)]
    apart = [u * part_rows + 2 * RANK for u in range(parts)]
    totals = pack(
        k_scalar,
        parts * part_rows,
        width,
        (share_a_gu, 1, False, summed[0:2]),
        (ap_down, 1, False, summed[2:3]),
        (cross_out / copies, 1, False, summed[3:4]),
        (cross_down / copies, 1, False, summed[4:5]),
        (ap_out, 1, False, summed[5:6]),
        (jnp.concatenate([g_down, g_out], axis=1), 2, False, summed[6:7]),
        (pb_out, 1, False, summed[7:8]),
        (share_a_heads, 1, False, summed[8:11]),
        (share_b_heads, 3, True, summed[11:14]),
        (g_heads, 3, True, summed[14:15]),
        (share_b_gu, 2, False, apart[0:2]),
        (pb_down, 1, False, apart[2:3]),
        (g_gu, 2, False, apart[3:4]),
    )
    totals = spread_join(spread_sum(doc_halve(totals), peers, ["mp"], 2 * RANK), peers)
    hidden_inverse = inverse_rms(hidden_own)
    (totals,) = after([totals], dnormed_own, result, hidden_inverse)
    totals = doc_join(totals).astype(f32)

    def unit(index, rows=RANK):
        return totals[summed[index] : summed[index] + rows]

    def own_columns(values):
        return lax.dynamic_slice_in_dim(values, k * near_width, near_width, 1)

    def unit_apart(index, rows=RANK):
        return totals[apart[index] : apart[index] + rows, : w_gate.shape[1]]

    grad_input = dresid_own + rms_backward(
        hidden_own, gain_attn, dnormed_own.astype(f32), hidden_inverse
    )

    total_g_down, total_g_out = unit(6, 2)[:1], unit(6, 2)[1:]
    shrink_out = total_g_out * m_out / (column_out * column_out * column_out)
    shrink_down = total_g_down * m_down / (column_down * column_down * column_down)
    turned_out = (b_out * shrink_out).astype(bf16)
    radial_out = dot_nt(turned_out, w_out) + SCALING * dot(
        dot_nt(turned_out, b_out.astype(bf16)), a_out.T
    )
    radial_down = dot_nt((b_down * shrink_down).astype(bf16), wd_low)
    grad_a_out = SCALING * (own_columns(unit(7)) - radial_out)
    grad_a_down = SCALING * (unit_apart(2) - radial_down)
    grad_b_out = SCALING * (unit(5) - unit(3) * shrink_out)
    grad_b_down = SCALING * (unit(2) - unit(4) * shrink_down)
    g_rows = own_columns(unit(14, 3))
    g_rows = [
        g_rows[i] / column_heads[0, i * near_width : (i + 1) * near_width] for i in range(3)
    ]
    both = jnp.concatenate([unit_apart(0), unit_apart(1)], axis=1)
    g_both = jnp.concatenate([unit_apart(3, 2)[:1], unit_apart(3, 2)[1:]], axis=1)
    grad_m_gate, grad_m_up = separate(g_both / column_gu)
    grad_b_gate, grad_b_up = separate(both)
    return (
        result,
        grad_input,
        unit(10).T,
        own_columns(unit(13)),
        g_rows[2],
        unit(8).T,
        own_columns(unit(11)),
        g_rows[0],
        unit(9).T,
        own_columns(unit(12)),
        g_rows[1],
        grad_a_out.T,
        grad_b_out,
        (total_g_out / column_out)[0],
        unit(0).T,
        grad_b_gate,
        grad_m_gate[0],
        unit(1).T,
        grad_b_up,
        grad_m_up[0],
        grad_a_down.T,
        grad_b_down,
        (total_g_down / column_down)[0],
    )


def solution(mesh):
    rows = P(("doc", "seq"))
    split_columns = (P(None, "mp"), P(None, "mp"))
    column_layer = (P(), P(None, "mp"), P("mp"))
    row_layer = (P("mp", None), P(), P())
    in_specs = (
        P(("doc", "seq"), None),
        P(("doc", "seq"), None),
        rows,
        rows,
        P(),
        P(),
        P(),
        P(None, "mp"),
        P(None, "mp"),
        P(None, "mp"),
        P("mp", None),
        *split_columns,
        P("mp", None),
        *column_layer,
        *column_layer,
        *column_layer,
        *row_layer,
        *column_layer,
        *column_layer,
        *row_layer,
    )
    out_specs = (
        P(("doc", "seq", "mp"), None),
        P(("doc", "seq", "mp"), None),
        *column_layer,
        *column_layer,
        *column_layer,
        *row_layer,
        *column_layer,
        *column_layer,
        *row_layer,
    )
    return jax.shard_map(
        per_device, mesh=mesh, in_specs=in_specs, out_specs=out_specs, check_vma=False
    )
```

```python
import functools
import math

import jax
import jax.numpy as jnp
import numpy as np
from jax import lax
from jax.experimental import pallas as pl
from jax.experimental.pallas import tpu as pltpu
from jax.sharding import PartitionSpec as P

HD = 128
RANK = 16
ALPHA = 32
HALF = HD // 2
SCALING = ALPHA / RANK
INV_ROOT = HD ** (-0.5)
EPS = 1e-05
ROPE_BASE = 10000.0
MASKED = -1e30
CHUNKS = 2
MIB = 1 << 20
VMEM_LIMIT = 56 * MIB

f32 = jnp.float32
bf16 = jnp.bfloat16


def dot(left, right):
    return jnp.dot(left, right, preferred_element_type=f32)


def dot_nt(left, right):
    return lax.dot_general(left, right, (((1,), (1,)), ((), ())), preferred_element_type=f32)


def dot_tn(left, right):
    return lax.dot_general(left, right, (((0,), (0,)), ((), ())), preferred_element_type=f32)


def whole_spec(array):
    rank = len(array.shape)
    return pl.BlockSpec(tuple(array.shape), lambda *_: (0,) * rank)


def cost(flops, moved):
    return pl.CostEstimate(flops=1, bytes_accessed=1, transcendentals=0)


def swap(value, axis, distance):
    size = lax.axis_size(axis)
    return lax.ppermute(value, axis, [(i, i ^ distance) for i in range(size)])


def butterfly(value, axes):
    for axis in axes:
        distance = 1
        while distance < lax.axis_size(axis):
            value = lax.optimization_barrier(value + swap(value, axis, distance))
            distance *= 2
    return value


def doc_halve(value):
    doc = lax.axis_index("doc")
    half = value.shape[0] // 2
    mine = lax.dynamic_slice_in_dim(value, doc * half, half, 0)
    other = lax.dynamic_slice_in_dim(value, (1 - doc) * half, half, 0)
    return lax.optimization_barrier(mine + swap(other, "doc", 1))


def doc_join(mine):
    doc = lax.axis_index("doc")
    other = swap(mine, "doc", 1)
    first = jnp.where(doc == 0, mine, other)
    second = jnp.where(doc == 0, other, mine)
    return jnp.concatenate([first, second], axis=0)


def spread_sum(value, peers, axes, leading):
    me = lax.rem(lax.axis_index("seq"), peers)
    parts = value.reshape(peers, -1, value.shape[-1])
    piece = lambda index: lax.dynamic_index_in_dim(parts, index, 0, keepdims=False)
    mine = piece(me).astype(f32)
    for d in range(1, peers):
        mine = mine + swap(piece(me ^ d), "seq", d).astype(f32)
    mine = lax.optimization_barrier(mine.astype(bf16))
    distance = peers
    while distance < lax.axis_size("seq"):
        mine = lax.optimization_barrier(mine + swap(mine, "seq", distance))
        distance *= 2
    return jnp.concatenate([butterfly(mine[:leading], axes), mine[leading:]], axis=0)


def spread_join(mine, peers):
    me = lax.rem(lax.axis_index("seq"), peers)
    found = [mine] + [swap(mine, "seq", d) for d in range(1, peers)]
    return jnp.concatenate([pick_blocks(found, me ^ i) for i in range(peers)], axis=0)


def after(values, *earlier):
    tied = lax.optimization_barrier((tuple(values), earlier))
    return tied[0]


def line_step(rights, lefts, step, *earlier):
    size = lax.axis_size("mp")
    right, left = rights[-1], lefts[-1]
    if earlier:
        right, left = after([right, left], *earlier)
    right_pairs = [(i, i + 1) for i in range(step - 1, size - 1)]
    left_pairs = [(i, i - 1) for i in range(1, size - step + 1)]
    rights.append(lax.ppermute(right, "mp", right_pairs))
    lefts.append(lax.ppermute(left, "mp", left_pairs))


def line_blocks(rights, lefts):
    size = lax.axis_size("mp")
    k = lax.axis_index("mp")
    return [rights[0]] + [
        jnp.where(k + c < size, lefts[c], rights[size - c]) for c in range(1, size)
    ]


def seq_exchange(blocks):
    return [blocks[0]] + [swap(blocks[d], "seq", d) for d in range(1, len(blocks))]


def key_marks(code):
    lane = lax.broadcasted_iota(jnp.int32, (code.shape[0], HD), 1)
    segment, real = code >> 1, code & 1
    wrong = (lane < 16) & (lane != segment)
    absent = (lane == 16) & (real == 0)
    return jnp.where(wrong | absent, MASKED, 0.0).astype(bf16)


def query_marks(code):
    lane = lax.broadcasted_iota(jnp.int32, (code.shape[0], HD), 1)
    segment = code >> 1
    return jnp.where((lane == segment) | (lane == 16), 1.0, 0.0).astype(bf16)


def diagonal_scores(keys, query):
    marked = dot_nt(keys, query)
    plain = dot_nt(keys[:, :HD], query[:, :HD])
    key_id = lax.broadcasted_iota(jnp.int32, marked.shape, 0)
    query_id = lax.broadcasted_iota(jnp.int32, marked.shape, 1)
    return jnp.where(
        key_id < query_id, marked, jnp.where(key_id == query_id, plain, MASKED)
    )


def block_readers(groups, heads, kv_refs, code_refs):
    if groups == 1:
        return (
            lambda g, d, rows: heads[d][0, rows, :],
            lambda g, d, rows: heads[d][1, rows, :],
            lambda g, d, rows: code_refs[d][rows, :],
        )
    return (
        lambda g, d, rows: kv_refs[0][g, d, 0, rows, :],
        lambda g, d, rows: kv_refs[0][g, d, 1, rows, :],
        lambda g, d, rows: kv_refs[1][g, d, rows, :],
    )


def taker(refs):
    refs = list(refs)

    def take(count):
        taken = refs[:count]
        del refs[:count]
        return taken

    return take


def forward_kernel(meta, scalars, *refs):
    peers, groups, span, pieces, chunks, n_extra = meta
    take = taker(refs)
    heads, code_refs, kv_refs = take(peers), take(peers), take(n_extra)
    o_refs, (lse_ref,) = take(peers), take(1)
    q_all, o_all, k_all, v_turned = take(4)
    key_of, value_of, key_code_of = block_readers(groups, heads, kv_refs, code_refs)
    n_query = 2 * peers

    for g in range(groups):
        for d in range(peers):
            for half in range(2):
                rows = pl.ds(half * span, span)
                place = scalars[n_query + (g * peers + d) * 2 + half]
                at = pl.ds(pl.multiple_of(place * span, HD), span)
                k_all[at, :HD] = key_of(g, d, rows)
                k_all[at, HD:] = key_marks(key_code_of(g, d, rows))
                v_turned[:, at] = value_of(g, d, rows).astype(f32).T.astype(bf16)
    for d in range(peers):
        for half in range(2):
            rows = pl.ds(half * span, span)
            q_all[2 * d + half, :, :HD] = heads[d][2, rows, :]
            q_all[2 * d + half, :, HD:] = query_marks(code_refs[d][rows, :])

    def one_span(i, carry):
        place = scalars[i]
        query = q_all[i]
        at = pl.ds(pl.multiple_of(place * span, HD), span)
        scores = diagonal_scores(k_all[at, :], query)
        peak = jnp.max(scores, axis=0, keepdims=True)
        weights = jnp.exp((scores - peak) * INV_ROOT)
        total = jnp.sum(weights, axis=0, keepdims=True)
        out = dot(v_turned[:, at], weights.astype(bf16))

        def key_span(j, state):
            peak, total, out = state
            at = pl.ds(pl.multiple_of(j * span, HD), span)
            scores = dot_nt(k_all[at, :], query)
            new_peak = jnp.maximum(peak, jnp.max(scores, axis=0, keepdims=True))
            fade = jnp.exp((peak - new_peak) * INV_ROOT)
            weights = jnp.exp((scores - new_peak) * INV_ROOT)
            total = total * fade + jnp.sum(weights, axis=0, keepdims=True)
            out = out * fade + dot(v_turned[:, at], weights.astype(bf16))
            return (new_peak, total, out)

        peak, total, out = lax.fori_loop(0, place, key_span, (peak, total, out))
        lse_ref[i] = peak * INV_ROOT + jnp.log(total)
        o_all[i] = (out / total).T.astype(bf16)
        return carry

    lax.fori_loop(0, n_query, one_span, 0)
    share = 2 * span // pieces
    part = share // chunks
    for d in range(peers):
        for piece in range(pieces):
            for c in range(chunks):
                row = piece * share + c * part
                to = (c * pieces + piece) * part
                o_refs[d][to : to + part, :] = o_all[
                    2 * d + row // span, row % span : row % span + part, :
                ]


def place_rows(scalars, peers, span):
    for d in range(peers):
        for half in range(2):
            place = scalars[2 * d + half]
            at = pl.ds(pl.multiple_of(place * span, HD), span)
            yield d, half, pl.ds(half * span, span), at


def piece_rows(peers, span, pieces, chunks):
    share = 2 * span // pieces
    part = share // chunks
    for d in range(peers):
        for piece in range(pieces):
            for c in range(chunks):
                row = piece * share + c * part
                yield d, piece, c, pl.ds((c * pieces + piece) * part, part), row, part


def forward_group_kernel(meta, scalars, *refs):
    peers, _, span, pieces, chunks, _ = meta
    take = taker(refs)
    heads, code_refs = take(peers), take(peers)
    o_refs, (lse_ref,) = take(peers), take(1)
    q_all, o_all, k_all, v_turned = take(4)
    tile = 2 * span

    for d, half, rows, at in place_rows(scalars, peers, span):
        code = code_refs[d][rows, :]
        k_all[at, :HD] = heads[d][0, rows, :]
        k_all[at, HD:] = key_marks(code)
        v_turned[:, at] = heads[d][1, rows, :].astype(f32).T.astype(bf16)
        q_all[at, :HD] = heads[d][2, rows, :]
        q_all[at, HD:] = query_marks(code)

    for m in range(peers):
        here = slice(m * tile, (m + 1) * tile)
        query = q_all[here, :]
        scores = diagonal_scores(k_all[here, :], query)
        peak = jnp.max(scores, axis=0, keepdims=True)
        weights = jnp.exp((scores - peak) * INV_ROOT)
        total = jnp.sum(weights, axis=0, keepdims=True)
        out = dot(v_turned[:, here], weights.astype(bf16))

        def key_tile(j, state):
            peak, total, out = state
            at = pl.ds(pl.multiple_of(j * tile, HD), tile)
            scores = dot_nt(k_all[at, :], query)
            new_peak = jnp.maximum(peak, jnp.max(scores, axis=0, keepdims=True))
            fade = jnp.exp((peak - new_peak) * INV_ROOT)
            weights = jnp.exp((scores - new_peak) * INV_ROOT)
            total = total * fade + jnp.sum(weights, axis=0, keepdims=True)
            out = out * fade + dot(v_turned[:, at], weights.astype(bf16))
            return (new_peak, total, out)

        if m:
            peak, total, out = lax.fori_loop(0, m, key_tile, (peak, total, out))
        lse_ref[m] = peak * INV_ROOT + jnp.log(total)
        o_all[here, :] = (out / total).T.astype(bf16)

    for d, piece, c, to, row, part in piece_rows(peers, span, pieces, chunks):
        place = scalars[2 * d + row // span] * span + row % span
        o_refs[d][to, :] = o_all[pl.ds(pl.multiple_of(place, 32), part), :]


def backward_group_kernel(meta, scalars, *refs):
    peers, groups, span, pieces, chunks, _ = meta
    take = taker(refs)
    heads, code_refs = take(peers), take(peers)
    o_refs, do_refs, (lse_ref,) = take(peers), take(peers), take(1)
    grad_refs = take(peers)
    q_all, o_all, do_all, k_all, k_turned, v_all, dk_all, dv_all = take(8)
    own_piece = scalars[4 * peers]
    tile = 2 * span
    share = 2 * span // pieces

    for d, half, rows, at in place_rows(scalars, peers, span):
        code = code_refs[d][rows, :]
        key = heads[d][0, rows, :]
        k_all[at, :HD] = key
        k_all[at, HD:] = key_marks(code)
        k_turned[:, at] = key.astype(f32).T.astype(bf16)
        v_all[at, :] = heads[d][1, rows, :]
        q_all[at, :HD] = heads[d][2, rows, :]
        q_all[at, HD:] = query_marks(code)
    for d, piece, c, source, row, part in piece_rows(peers, span, pieces, chunks):
        place = scalars[2 * d + row // span] * span + row % span
        o_all[pl.ds(pl.multiple_of(place, 32), part), :] = o_refs[d][source, :]
        row = lax.rem(own_piece + pieces - piece, pieces) * share + c * part
        late = row >= span
        place = scalars[2 * d + late.astype(jnp.int32)] * span + row - jnp.where(late, span, 0)
        do_all[pl.ds(pl.multiple_of(place, 32), part), :] = do_refs[d][source, :]

    for m in range(peers):
        here = slice(m * tile, (m + 1) * tile)
        query = q_all[here, :]
        grad = do_all[here, :]
        product = grad.astype(f32) * o_all[here, :].astype(f32)
        high, rest = split_low(product)
        ones = jnp.ones((16, HD), bf16)
        delta = (dot_nt(ones, high) + dot_nt(ones, rest))[:1, :]
        lse = lse_ref[m]

        def key_tile(at, scores, dq_turned, first):
            probs = jnp.exp(scores * INV_ROOT - lse)
            grad_score = (probs * (dot_nt(v_all[at, :], grad) - delta)).astype(bf16)
            dv = dot(probs.astype(bf16), grad)
            dk = dot(grad_score, query[:, :HD])
            if first:
                dv_all[at, :] = dv
                dk_all[at, :] = dk
            else:
                dv_all[at, :] += dv
                dk_all[at, :] += dk
            return dq_turned + dot(k_turned[:, at], grad_score)

        scores = diagonal_scores(k_all[here, :], query)
        dq_turned = key_tile(here, scores, jnp.zeros((HD, tile), f32), True)

        def step(j, dq_turned):
            at = pl.ds(pl.multiple_of(j * tile, HD), tile)
            return key_tile(at, dot_nt(k_all[at, :], query), dq_turned, False)

        if m:
            dq_turned = lax.fori_loop(0, m, step, dq_turned)
        o_all[here, :] = (dq_turned * INV_ROOT).T.astype(bf16)

    for d, half, rows, at in place_rows(scalars, peers, span):
        grad_refs[d][0, rows, :] = (dk_all[at, :] * INV_ROOT).astype(bf16)
        grad_refs[d][1, rows, :] = dv_all[at, :].astype(bf16)
        grad_refs[d][2, rows, :] = o_all[at, :]


def attention_forward(scalars, heads, codes, extra, groups, pieces, chunks):
    peers = len(heads)
    rows = heads[0].shape[1]
    span = rows // 2
    key_rows = groups * peers * rows
    meta = (peers, groups, span, pieces, chunks, len(extra))
    operands = [*heads, *codes, *extra]
    out_shape = [jax.ShapeDtypeStruct((rows, HD), bf16)] * peers
    n_query = 2 * peers if groups > 1 else peers
    out_shape.append(jax.ShapeDtypeStruct((n_query, 1, 2 * peers * span // n_query), f32))
    if groups == 1:
        body, q_shape, o_shape = forward_group_kernel, (key_rows, 2 * HD), (key_rows, HD)
    else:
        body, q_shape, o_shape = (
            forward_kernel,
            (2 * peers, span, 2 * HD),
            (2 * peers, span, HD),
        )
    outs = pl.pallas_call(
        functools.partial(body, meta),
        grid_spec=pltpu.PrefetchScalarGridSpec(
            num_scalar_prefetch=1,
            grid=(1,),
            in_specs=[whole_spec(x) for x in operands],
            out_specs=[whole_spec(x) for x in out_shape],
            scratch_shapes=[
                pltpu.VMEM(q_shape, bf16),
                pltpu.VMEM(o_shape, bf16),
                pltpu.VMEM((key_rows, 2 * HD), bf16),
                pltpu.VMEM((HD, key_rows), bf16),
            ],
        ),
        out_shape=out_shape,
        compiler_params=pltpu.CompilerParams(vmem_limit_bytes=VMEM_LIMIT),
        cost_estimate=cost(6 * peers * rows * key_rows // 2 * HD, 8 * key_rows * HD),
        name="attend",
    )(scalars, *operands)
    return outs[:-1], outs[-1]


def backward_kernel(meta, scalars, *refs):
    peers, groups, span, pieces, chunks, n_extra = meta
    take = taker(refs)
    heads, code_refs, kv_refs = take(peers), take(peers), take(n_extra)
    o_refs, do_refs, (lse_ref,) = take(peers), take(peers), take(1)
    grad_refs = take(peers)
    dkv_refs = take(1 if groups > 1 else 0)
    q_all, o_all, do_all, k_all, k_turned, v_all, dk_all, dv_all = take(8)
    key_of, value_of, key_code_of = block_readers(groups, heads, kv_refs, code_refs)
    n_query = 2 * peers
    own_piece = scalars[n_query + 2 * groups * peers]

    for g in range(groups):
        for d in range(peers):
            for half in range(2):
                rows = pl.ds(half * span, span)
                place = scalars[n_query + (g * peers + d) * 2 + half]
                at = pl.ds(pl.multiple_of(place * span, HD), span)
                key = key_of(g, d, rows)
                k_all[at, :HD] = key
                k_all[at, HD:] = key_marks(key_code_of(g, d, rows))
                k_turned[:, at] = key.astype(f32).T.astype(bf16)
                v_all[at, :] = value_of(g, d, rows)
    dk_all[...] = jnp.zeros_like(dk_all)
    dv_all[...] = jnp.zeros_like(dv_all)
    share = 2 * span // pieces
    part = share // chunks
    for d in range(peers):
        for half in range(2):
            rows = pl.ds(half * span, span)
            q_all[2 * d + half, :, :HD] = heads[d][2, rows, :]
            q_all[2 * d + half, :, HD:] = query_marks(code_refs[d][rows, :])
        for piece in range(pieces):
            origin = lax.rem(own_piece + pieces - piece, pieces)
            for c in range(chunks):
                source = pl.ds((c * pieces + piece) * part, part)
                row = (2 * d * span) + piece * share + c * part
                o_all[row : row + part, :] = o_refs[d][source, :]
                row = (2 * d * span) + origin * share + c * part
                do_all[pl.ds(pl.multiple_of(row, 16), part), :] = do_refs[d][source, :]

    def one_span(i, carry):
        place = scalars[i]
        query = q_all[i]
        rows = pl.ds(pl.multiple_of(i * span, HD), span)
        grad = do_all[rows, :]
        product = grad.astype(f32) * o_all[rows, :].astype(f32)
        high = product.astype(bf16)
        rest = (product - high.astype(f32)).astype(bf16)
        ones = jnp.ones((16, HD), bf16)
        delta = (dot_nt(ones, high) + dot_nt(ones, rest))[:1, :]
        lse = lse_ref[i]

        def key_span(at, scores, dq_turned):
            probs = jnp.exp(scores * INV_ROOT - lse)
            grad_prob = dot_nt(v_all[at, :], grad)
            grad_score = (probs * (grad_prob - delta)).astype(bf16)
            dv_all[at, :] += dot(probs.astype(bf16), grad)
            dk_all[at, :] += dot(grad_score, query[:, :HD])
            return dq_turned + dot(k_turned[:, at], grad_score)

        at = pl.ds(pl.multiple_of(place * span, HD), span)
        dq_turned = key_span(
            at, diagonal_scores(k_all[at, :], query), jnp.zeros((HD, span), f32)
        )

        def step(j, dq_turned):
            at = pl.ds(pl.multiple_of(j * span, HD), span)
            return key_span(at, dot_nt(k_all[at, :], query), dq_turned)

        dq_turned = lax.fori_loop(0, place, step, dq_turned)
        o_all[rows, :] = (dq_turned * INV_ROOT).T.astype(bf16)
        return carry

    lax.fori_loop(0, n_query, one_span, 0)
    at_query = 2 if groups == 1 else 0
    for d in range(peers):
        grad_refs[d][at_query] = o_all[2 * d * span : 2 * (d + 1) * span, :]
    for g in range(groups):
        for d in range(peers):
            for half in range(2):
                rows = pl.ds(half * span, span)
                place = scalars[n_query + (g * peers + d) * 2 + half]
                at = pl.ds(pl.multiple_of(place * span, HD), span)
                grad_key = (dk_all[at, :] * INV_ROOT).astype(bf16)
                grad_value = dv_all[at, :].astype(bf16)
                if groups == 1:
                    grad_refs[d][0, rows, :] = grad_key
                    grad_refs[d][1, rows, :] = grad_value
                else:
                    dkv_refs[0][g, d, 0, rows, :] = grad_key
                    dkv_refs[0][g, d, 1, rows, :] = grad_value


def attention_backward(scalars, heads, codes, extra, o, grads, lse, groups, pieces, chunks):
    peers = len(heads)
    rows = heads[0].shape[1]
    span = rows // 2
    key_rows = groups * peers * rows
    meta = (peers, groups, span, pieces, chunks, len(extra))
    operands = [*heads, *codes, *extra, *o, *grads, lse]
    parts = 3 if groups == 1 else 1
    out_shape = [jax.ShapeDtypeStruct((parts, rows, HD), bf16)] * peers
    if groups > 1:
        out_shape.append(jax.ShapeDtypeStruct(extra[0].shape, bf16))
    if groups == 1:
        body, q_shape = backward_group_kernel, (key_rows, 2 * HD)
    else:
        body, q_shape = backward_kernel, (2 * peers, span, 2 * HD)
    outs = pl.pallas_call(
        functools.partial(body, meta),
        grid_spec=pltpu.PrefetchScalarGridSpec(
            num_scalar_prefetch=1,
            grid=(1,),
            in_specs=[whole_spec(x) for x in operands],
            out_specs=[whole_spec(x) for x in out_shape],
            scratch_shapes=[
                pltpu.VMEM(q_shape, bf16),
                pltpu.VMEM((peers * rows, HD), bf16),
                pltpu.VMEM((peers * rows, HD), bf16),
                pltpu.VMEM((key_rows, 2 * HD), bf16),
                pltpu.VMEM((HD, key_rows), bf16),
                pltpu.VMEM((key_rows, HD), bf16),
                pltpu.VMEM((key_rows, HD), f32),
                pltpu.VMEM((key_rows, HD), f32),
            ],
        ),
        out_shape=out_shape,
        compiler_params=pltpu.CompilerParams(vmem_limit_bytes=VMEM_LIMIT),
        cost_estimate=cost(14 * peers * rows * key_rows // 2 * HD, 16 * key_rows * HD),
        name="attend_back",
    )(scalars, *operands)
    if groups == 1:
        return outs, None
    return outs[:peers], outs[peers]


def split_low(value):
    high = value.astype(bf16)
    return high, (value - high.astype(f32)).astype(bf16)


def low_rank(a_t, b):
    a_high, a_rest = split_low(a_t)
    b_high, b_rest = split_low(b * SCALING)
    a_cat = jnp.concatenate([a_high, a_rest, a_high], axis=0)
    b_cat = jnp.concatenate([b_high, b_high, b_rest], axis=0)
    return dot_tn(a_cat, b_cat)


def separate(both):
    rows, width = both.shape
    both = both.reshape(rows, -1, 2, HD)
    return both[:, :, 0].reshape(rows, width // 2), both[:, :, 1].reshape(rows, width // 2)


def merge_kernel(starts, out_w, out_a, out_b, down_w, down_a, down_b, gate_w, up_w, gate_a, up_a,
                 gate_b, up_b, gate_m, up_m, out_square, out_cross, down_square, down_cross,
                 down_low, pair_low, pair_cross, pair_column, pair_scale, mixed_m, mixed_b):
    step = pl.program_id(0)
    down_start, pair_start = starts

    def columns(w_ref, a_ref, b_ref, square_ref, cross_ref, low_ref):
        merged = w_ref[...].astype(f32) + low_rank(a_ref[...], b_ref[...])
        low = merged.astype(bf16)
        if low_ref is not None:
            low_ref[...] = low
        square_ref[...] = jnp.sum(merged * merged, axis=0, keepdims=True)
        cross_ref[...] = dot(a_ref[...].astype(bf16), low)

    @pl.when(step < down_start)
    def _():
        columns(out_w, out_a, out_b, out_square, out_cross, None)

    @pl.when((step >= down_start) & (step < pair_start))
    def _():
        columns(down_w, down_a, down_b, down_square, down_cross, down_low)

    sides = ((gate_w, gate_a, gate_b, gate_m), (up_w, up_a, up_b, up_m))
    blocks = [
        (side, slice(j * HD, (j + 1) * HD), pl.ds((2 * j + side) * HD, HD))
        for side in range(2)
        for j in range(gate_w.shape[1] // HD)
    ]

    @pl.when(step == pair_start)
    def _():
        pair_column[...] = jnp.zeros_like(pair_column)
        pair_cross[...] = jnp.zeros_like(pair_cross)
        for side, source, at in blocks:
            mixed_b[:, at] = sides[side][2][:, source]
            mixed_m[:, at] = sides[side][3][:, source]

    @pl.when(step >= pair_start)
    def _():
        results = []
        for w_ref, a_ref, b_ref, _ in sides:
            merged = w_ref[...].astype(f32) + low_rank(a_ref[...], b_ref[...])
            low = merged.astype(bf16)
            square = jnp.sum(merged * merged, axis=0, keepdims=True)
            results.append((low, square, dot(a_ref[...].astype(bf16), low)))
        for side, source, at in blocks:
            low, square, cross = results[side]
            pair_low[:, at] = low[:, source]
            pair_column[:, at] += square[:, source]
            pair_cross[:, at] += cross[:, source]

    @pl.when(step == pl.num_programs(0) - 1)
    def _():
        column = jnp.sqrt(pair_column[...])
        pair_column[...] = column
        pair_scale[...] = mixed_m[...] / column


def merge_others(out, down, gate, up):
    step = 8 * HD
    rows = 2 * HD
    near, wide = out[0].shape
    ff = down[0].shape[0]
    depth, width = gate[0].shape
    n_columns = wide // step
    starts = (n_columns, 2 * n_columns)
    n_pair = depth // rows
    at_out = lambda i: jnp.minimum(i, n_columns - 1)
    at_down = lambda i: jnp.clip(i - starts[0], 0, n_columns - 1)
    at_pair = lambda i: jnp.clip(i - starts[1], 0, n_pair - 1)
    cut = lambda height, at: pl.BlockSpec((height, step), lambda i: (0, at(i)))
    fixed = lambda *shape: pl.BlockSpec(shape, lambda i: (0,) * len(shape))
    pair_rows = lambda lanes: pl.BlockSpec((rows, lanes), lambda i: (at_pair(i), 0))
    turned = pl.BlockSpec((RANK, rows), lambda i: (0, at_pair(i)))
    shape = jax.ShapeDtypeStruct
    return pl.pallas_call(
        functools.partial(merge_kernel, starts),
        grid=(starts[1] + n_pair,),
        in_specs=[
            cut(near, at_out),
            fixed(RANK, near),
            cut(RANK, at_out),
            cut(ff, at_down),
            fixed(RANK, ff),
            cut(RANK, at_down),
            pair_rows(width),
            pair_rows(width),
            turned,
            turned,
            fixed(RANK, width),
            fixed(RANK, width),
            fixed(1, width),
            fixed(1, width),
        ],
        out_specs=[
            cut(1, at_out),
            cut(RANK, at_out),
            cut(1, at_down),
            cut(RANK, at_down),
            cut(ff, at_down),
            pair_rows(2 * width),
            fixed(RANK, 2 * width),
            fixed(1, 2 * width),
            fixed(1, 2 * width),
            fixed(1, 2 * width),
            fixed(RANK, 2 * width),
        ],
        out_shape=[
            shape((1, wide), f32),
            shape((RANK, wide), f32),
            shape((1, wide), f32),
            shape((RANK, wide), f32),
            shape((ff, wide), bf16),
            shape((depth, 2 * width), bf16),
            shape((RANK, 2 * width), f32),
            shape((1, 2 * width), f32),
            shape((1, 2 * width), f32),
            shape((1, 2 * width), f32),
            shape((RANK, 2 * width), f32),
        ],
        compiler_params=pltpu.CompilerParams(vmem_limit_bytes=VMEM_LIMIT),
        cost_estimate=cost(4 * depth * width * RANK, 8 * depth * width),
        name="merge_others",
    )(*out, *down, gate[0], up[0], gate[1], up[1], gate[2], up[2], gate[3], up[3])


def heads_kernel(scalars, x_ref, gain_ref, a_ref, b_ref, m_ref, cos_ref, sin_ref,
                 wk_hbm, wv_hbm, wq_hbm, *refs):
    take = taker(refs)
    peers = len(refs) - 12
    blocks = take(peers)
    normed_ref, low_ref, raw_ref, column_ref, scale_ref, cross_ref = take(6)
    x_all, w_all, merged_all, column_now, scale_now, sem = take(6)
    step = pl.program_id(0)
    rows = x_ref.shape[0]
    sources = (wk_hbm, wv_hbm, wq_hbm)

    def copy(number):
        return pltpu.make_async_copy(sources[number], w_all.at[number], sem.at[number])

    def merge(layer):
        slot = lax.rem(layer, 2)
        merged = w_all[layer].astype(f32) + low_rank(a_ref[layer], b_ref[layer])
        low = merged.astype(bf16)
        merged_all[slot] = low
        low_ref[...] = low
        column = jnp.sqrt(jnp.sum(merged * merged, axis=0, keepdims=True))
        scale = m_ref[layer] / column
        column_ref[...] = column
        scale_ref[...] = scale
        scale_now[slot] = scale

    @pl.when(step == 0)
    def _():
        for number in range(3):
            copy(number).start()
        part = rows // 4
        for i in range(4):
            at = pl.ds(i * part, part)
            x = x_ref[at, :].astype(f32)
            inverse = lax.rsqrt(jnp.mean(x * x, axis=-1, keepdims=True) + EPS)
            normed = (x * inverse * gain_ref[...]).astype(bf16)
            x_all[at, :] = normed
            normed_ref[at, :] = normed
        x_all[rows:, :] = a_ref[0].astype(bf16)
        copy(0).wait()
        merge(0)

    for number in (1, 2):

        @pl.when(step == number)
        def _(number=number):
            copy(number).wait()

    @pl.when(step > 0)
    def _():
        layer = step - 1
        slot = lax.rem(layer, 2)
        product = dot(x_all[...], merged_all[slot])
        scale = scale_now[slot]
        x_next = a_ref[jnp.minimum(step, 2)].astype(bf16)
        merge(jnp.minimum(step, 2))
        cross_ref[...] = product[rows:, :]
        raw = product[:rows, :]
        raw_ref[...] = raw.astype(bf16)
        value = raw * scale
        for t in range(peers):
            head = value[:, t * HD : (t + 1) * HD]
            rotated = head * cos_ref[...] + pltpu.roll(head, HALF, 1) * sin_ref[...]
            head = jnp.where(layer != 1, rotated, head).astype(bf16)
            place = t ^ scalars[0]
            for d, block in enumerate(blocks):

                @pl.when(place == d)
                def _(block=block, head=head):
                    block[layer] = head

        x_all[rows:, :] = x_next


def project_heads(order, x, gain, weights, a_t, b, m, cosine, sine):
    rows, depth = x.shape
    width = weights[0].shape[1]
    heads = width // HD
    merged_at = lambda i, s: (0, jnp.minimum(i, 2))
    done_at = lambda i, s: (0, jnp.maximum(i - 1, 0))
    fixed = lambda *shape: pl.BlockSpec(shape, lambda i, s: (0,) * len(shape))
    out_shape = [jax.ShapeDtypeStruct((3, rows, HD), bf16)] * heads
    out_shape += [
        jax.ShapeDtypeStruct((rows, depth), bf16),
        jax.ShapeDtypeStruct((depth, 3 * width), bf16),
        jax.ShapeDtypeStruct((rows, 3 * width), bf16),
        jax.ShapeDtypeStruct((1, 3 * width), f32),
        jax.ShapeDtypeStruct((1, 3 * width), f32),
        jax.ShapeDtypeStruct((RANK, 3 * width), f32),
    ]
    outs = pl.pallas_call(
        heads_kernel,
        grid_spec=pltpu.PrefetchScalarGridSpec(
            num_scalar_prefetch=1,
            grid=(4,),
            in_specs=[
                fixed(rows, depth),
                fixed(1, depth),
                fixed(3, RANK, depth),
                fixed(3, RANK, width),
                fixed(3, 1, width),
                fixed(rows, HD),
                fixed(rows, HD),
            ]
            + [pl.BlockSpec(memory_space=pl.ANY)] * 3,
            out_specs=[fixed(3, rows, HD)] * heads
            + [
                fixed(rows, depth),
                pl.BlockSpec((depth, width), merged_at),
                pl.BlockSpec((rows, width), done_at),
                pl.BlockSpec((1, width), merged_at),
                pl.BlockSpec((1, width), merged_at),
                pl.BlockSpec((RANK, width), done_at),
            ],
            scratch_shapes=[
                pltpu.VMEM((rows + RANK, depth), bf16),
                pltpu.VMEM((3, depth, width), bf16),
                pltpu.VMEM((2, depth, width), bf16),
                pltpu.VMEM((2, 1, width), f32),
                pltpu.VMEM((2, 1, width), f32),
                pltpu.SemaphoreType.DMA((3,)),
            ],
        ),
        out_shape=out_shape,
        compiler_params=pltpu.CompilerParams(vmem_limit_bytes=VMEM_LIMIT),
        cost_estimate=cost(6 * rows * depth * width, 16 * rows * depth),
        name="project_heads",
    )(order, x, gain, a_t, b, m, cosine, sine, *weights)
    return outs[:heads], *outs[heads:]


def assemble_kernel(peers, chunks, scalars, *refs):
    take = taker(refs)
    heads = take(peers)
    out_ref, down_ref, a_ref = take(3)
    near_refs = refs[peers + 3 :]
    width = a_ref.shape[1]
    parts = out_ref.shape[1] // width
    part = heads[0].shape[0] // chunks
    for d in range(peers):
        at = pl.ds(pl.multiple_of((scalars[0] ^ d) * HD, HD), HD)
        for c in range(chunks):
            near_refs[c][:part, at] = heads[d][c * part : (c + 1) * part, :]
    rows = []
    for ref in (out_ref, down_ref):
        high = ref[...].astype(bf16).astype(f32)
        for value in (high, ref[...] - high):
            rows += [value[:, j * width : (j + 1) * width] for j in range(parts)]
    near_refs[0][part : part + RANK, :] = jnp.concatenate(rows, axis=0).astype(bf16)
    near_refs[0][part + RANK :, :] = a_ref[...].astype(bf16)


def assemble(order, heads, square_out, square_down, a_t, chunks):
    peers = len(heads)
    part = heads[0].shape[0] // chunks
    width = peers * HD
    operands = [*heads, square_out, square_down, a_t]
    heights = [part + 2 * RANK] + [part] * (chunks - 1)
    out_shape = [jax.ShapeDtypeStruct((height, width), bf16) for height in heights]
    return pl.pallas_call(
        functools.partial(assemble_kernel, peers, chunks),
        grid_spec=pltpu.PrefetchScalarGridSpec(
            num_scalar_prefetch=1,
            grid=(1,),
            in_specs=[whole_spec(x) for x in operands],
            out_specs=[whole_spec(x) for x in out_shape],
        ),
        out_shape=out_shape,
        compiler_params=pltpu.CompilerParams(vmem_limit_bytes=VMEM_LIMIT),
        cost_estimate=cost(0, 0),
        name="assemble",
    )(order, *operands)


def unpack_kernel(size, scalars, *refs):
    take = taker(refs)
    blocks, m_refs = take(size), take(2)
    column_refs, scale_refs, (a_ref,) = take(2), take(2), take(1)
    width = blocks[0].shape[1]
    total = jnp.zeros((RANK, width), f32)
    for device in range(size):
        value = blocks[0][:RANK, :]
        for c in range(1, size):
            here = lax.rem(scalars[0] + c, size) == device
            value = jnp.where(here, blocks[c][:RANK, :], value)
        total = total + value.astype(f32)
    for side in range(2):
        for j in range(size):
            row = 2 * side * size + j
            square = total[row : row + 1, :] + total[row + size : row + size + 1, :]
            at = slice(j * width, (j + 1) * width)
            column = jnp.sqrt(square)
            column_refs[side][:, at] = column
            scale_refs[side][:, at] = m_refs[side][:, at] / column
    for c in range(size):
        device = lax.rem(scalars[0] + c, size)
        at = pl.ds(pl.multiple_of(device * width, HD), width)
        a_ref[:, at] = blocks[c][RANK:, :]


def unpack(k, blocks, rows, m_out, m_down):
    size = len(blocks)
    width = blocks[0].shape[1]
    wide = size * width
    row = jax.ShapeDtypeStruct((1, wide), f32)
    out_shape = [row] * 4 + [jax.ShapeDtypeStruct((RANK, wide), bf16)]
    tail = pl.BlockSpec((2 * RANK, width), lambda i, s: (rows // (2 * RANK), 0))
    return pl.pallas_call(
        functools.partial(unpack_kernel, size),
        grid_spec=pltpu.PrefetchScalarGridSpec(
            num_scalar_prefetch=1,
            grid=(1,),
            in_specs=[tail] * size + [whole_spec(m_out), whole_spec(m_down)],
            out_specs=[whole_spec(x) for x in out_shape],
        ),
        out_shape=out_shape,
        compiler_params=pltpu.CompilerParams(vmem_limit_bytes=VMEM_LIMIT),
        cost_estimate=cost(0, 0),
        name="unpack",
    )(k, *blocks, m_out, m_down)


def block_kernel(sizes, size, scalars, *refs):
    take = taker(refs)
    x_refs = take(size)
    a_ref, hid_ref, b_ref, out_scale_ref, gain_ref = take(5)
    cot_ref, down_scale_ref, scale_ref, wo_hbm, w_hbm, wd_hbm = take(6)
    hnorm_ref, resid_ref, raw_own_ref, low_ref, own_ref = take(5)
    act_ref, dz_ref, g_ref, dh_ref = take(4)
    total, through, dz_down, wo_all, w_all, wd_all, out_sem, sem, down_sem = take(9)
    k = scalars[0]
    rows, width = x_refs[0].shape
    part = rows // size
    starts = [sum(sizes[:j]) for j in range(len(sizes))]

    def out_copy(c):
        source = pl.ds(pl.multiple_of(lax.rem(k + c, size) * width, HD), width)
        return pltpu.make_async_copy(wo_hbm.at[source, :], wo_all.at[c], out_sem.at[c])

    def copies(j):
        both = pl.ds(2 * starts[j], 2 * sizes[j])
        one = pl.ds(starts[j], sizes[j])
        return (
            pltpu.make_async_copy(wd_hbm.at[one, :], wd_all.at[one, :], down_sem.at[j]),
            pltpu.make_async_copy(w_hbm.at[:, both], w_all.at[:, both], sem.at[j]),
        )

    for c in range(size):
        out_copy(c).start()
    for j in range(len(sizes)):
        for copy in copies(j):
            copy.start()
    for i in range(size):
        cot = cot_ref[i, 0].astype(f32)
        dz_down[i * part : (i + 1) * part, :] = (cot * down_scale_ref[...]).astype(bf16)

    mine = pl.ds(pl.multiple_of(k * part, 16), part)
    for c, x_ref in enumerate(x_refs):
        at = pl.ds(pl.multiple_of(lax.rem(k + c, size) * width, HD), width)
        own_ref[:, at] = x_ref[mine, :]
        out_copy(c).wait()
        x = x_ref[...]
        product = dot(x, wo_all[c])
        rank_part = dot_nt(x, a_ref[:, at])
        total[...] = total[...] + product if c else product
        through[...] = through[...] + rank_part if c else rank_part
    for piece in range(size):
        at = pl.ds(piece * part, part)
        low = through[at, :].astype(bf16)
        raw = total[at, :] + dot(low, b_ref[...])
        resid = hid_ref[piece, 0].astype(f32) + raw * out_scale_ref[...]
        inverse = lax.rsqrt(jnp.mean(resid * resid, axis=-1, keepdims=True) + EPS)
        hnorm_ref[at, :] = (resid * inverse * gain_ref[...]).astype(bf16)

        @pl.when(k == piece)
        def _(resid=resid, raw=raw, low=low):
            resid_ref[...] = resid
            raw_own_ref[...] = raw
            low_ref[...] = low

    def products(j):
        for copy in copies(j):
            copy.wait()
        both = slice(2 * starts[j], 2 * (starts[j] + sizes[j]))
        one = slice(starts[j], starts[j] + sizes[j])
        return dot(hnorm_ref[...], w_all[:, both]), dot_nt(dz_down[...], wd_all[one, :])

    ready = products(0)
    for j in range(len(sizes)):
        v, dact_all = ready
        if j + 1 < len(sizes):
            ready = products(j + 1)
        for i in range(sizes[j] // HD):
            hidden = starts[j] + i * HD
            gate_at = slice(2 * hidden, 2 * hidden + HD)
            up_at = slice(2 * hidden + HD, 2 * hidden + 2 * HD)
            raw_gate = v[:, 2 * i * HD : (2 * i + 1) * HD]
            raw_up = v[:, (2 * i + 1) * HD : (2 * i + 2) * HD]
            dact = dact_all[:, i * HD : (i + 1) * HD]
            scale_gate, scale_up = scale_ref[:, gate_at], scale_ref[:, up_at]
            gate = raw_gate * scale_gate
            up = raw_up * scale_up
            sigmoid = 1.0 / (1.0 + jnp.exp(-gate))
            silu = gate * sigmoid
            dgate = dact * up * (sigmoid + silu * (1.0 - sigmoid))
            dup = dact * silu
            act_ref[:, hidden : hidden + HD] = (silu * up).astype(bf16)
            g_ref[:, gate_at] = jnp.sum(dgate * raw_gate, axis=0, keepdims=True)
            g_ref[:, up_at] = jnp.sum(dup * raw_up, axis=0, keepdims=True)
            dz_ref[:, gate_at] = (dgate * scale_gate).astype(bf16)
            dz_ref[:, up_at] = (dup * scale_up).astype(bf16)
    dh_ref[...] = dot_nt(dz_ref[...], w_all[...]).astype(bf16)


def block(k, chunk, x, a_t, hidden, b2, out_scale, gain, cotangent, down_scale, scale, wo, w, wd):
    size, _, part, wide = hidden.shape
    rows, width = size * part, x[0].shape[1]
    ff = wd.shape[0]
    sizes = [ff]
    fixed = lambda *shape: pl.BlockSpec(shape, lambda i, s: (0,) * len(shape))
    view = pl.BlockSpec((size, 1, part, wide), lambda i, s: (0, chunk, 0, 0))
    shapes = [
        ((rows, wide), bf16),
        ((part, wide), f32),
        ((part, wide), f32),
        ((part, RANK), bf16),
        ((part, size * width), bf16),
        ((rows, ff), bf16),
        ((rows, 2 * ff), bf16),
        ((1, 2 * ff), f32),
        ((rows, wide), bf16),
    ]
    return pl.pallas_call(
        functools.partial(block_kernel, sizes, size),
        grid_spec=pltpu.PrefetchScalarGridSpec(
            num_scalar_prefetch=1,
            grid=(1,),
            in_specs=[fixed(rows, width)] * size
            + [
                fixed(RANK, size * width),
                view,
                fixed(RANK, wide),
                fixed(1, wide),
                fixed(1, wide),
                view,
                fixed(1, wide),
                fixed(1, 2 * ff),
            ]
            + [pl.BlockSpec(memory_space=pl.ANY)] * 3,
            out_specs=[fixed(*shape) for shape, _ in shapes],
            scratch_shapes=[
                pltpu.VMEM((rows, wide), f32),
                pltpu.VMEM((rows, RANK), f32),
                pltpu.VMEM((rows, wide), bf16),
                pltpu.VMEM((size, width, wide), bf16),
                pltpu.VMEM((wide, 2 * ff), bf16),
                pltpu.VMEM((ff, wide), bf16),
                pltpu.SemaphoreType.DMA((size,)),
                pltpu.SemaphoreType.DMA((len(sizes),)),
                pltpu.SemaphoreType.DMA((len(sizes),)),
            ],
        ),
        out_shape=[jax.ShapeDtypeStruct(shape, kind) for shape, kind in shapes],
        compiler_params=pltpu.CompilerParams(vmem_limit_bytes=60 * MIB),
        cost_estimate=cost(10 * rows * wide * ff, 6 * wide * ff),
        name="block",
    )(k, *x, a_t, hidden, b2, out_scale, gain, cotangent, down_scale, scale, wo, w, wd)


def back_out_kernel(scalars, *refs):
    take = taker(refs)
    earlier = take(len(refs) - 18)
    piece_ref, cot_ref, resid_ref, raw_ref, gain_ref, scale_ref = take(6)
    b_ref, own_ref, low_ref, w_ref, a_ref = take(5)
    dattn_ref, dresid_ref, dz_ref, g_ref, ap_ref, pb_ref = take(6)
    (through,) = take(1)

    @pl.when(pl.program_id(0) == 0)
    def _():
        grad = piece_ref[...].astype(f32)
        resid = resid_ref[...]
        inverse = lax.rsqrt(jnp.mean(resid * resid, axis=-1, keepdims=True) + EPS)
        scaled = grad * gain_ref[...]
        lean = jnp.mean(resid * scaled, axis=-1, keepdims=True)
        dresid = cot_ref[0, 0].astype(f32) + inverse * scaled
        dresid = dresid - resid * (inverse * inverse * inverse * lean)
        dresid_ref[...] = dresid
        dz = (dresid * scale_ref[...]).astype(bf16)
        dz_ref[...] = dz
        through[...] = dot_nt(dz, b_ref[...]).astype(bf16)
        sums = [
            jnp.sum(dresid * raw_ref[...], axis=0, keepdims=True),
            dot_tn(low_ref[...], dz),
            dot_tn(through[...], own_ref[...]),
        ]
        for i, ref in enumerate((g_ref, ap_ref, pb_ref)):
            ref[...] = sums[i] + earlier[i][...] if earlier else sums[i]

    dattn = dot_nt(dz_ref[...], w_ref[...]) + dot(through[...], a_ref[...])
    dattn_ref[0] = dattn.astype(bf16)


def back_out(k, chunk, piece, cotangent, resid, raw, gain, scale, b, own, low, w, a2_t, earlier):
    size = cotangent.shape[0]
    part, wide = resid.shape
    width = w.shape[0] // size
    fixed = lambda *shape: pl.BlockSpec(shape, lambda i, s: (0,) * len(shape))
    return pl.pallas_call(
        back_out_kernel,
        grid_spec=pltpu.PrefetchScalarGridSpec(
            num_scalar_prefetch=1,
            grid=(size,),
            in_specs=[fixed(*x.shape) for x in earlier]
            + [
                fixed(part, wide),
                pl.BlockSpec((1, 1, part, wide), lambda i, s: (s[0], chunk, 0, 0)),
                fixed(part, wide),
                fixed(part, wide),
                fixed(1, wide),
                fixed(1, wide),
                fixed(RANK, wide),
                fixed(*own.shape),
                fixed(part, RANK),
                pl.BlockSpec((width, wide), lambda i, s: (lax.rem(i + s[0], size), 0)),
                pl.BlockSpec((RANK, width), lambda i, s: (0, lax.rem(i + s[0], size))),
            ],
            out_specs=[
                pl.BlockSpec((1, part, width), lambda i, s: (i, 0, 0)),
                fixed(part, wide),
                fixed(part, wide),
                fixed(1, wide),
                fixed(RANK, wide),
                fixed(RANK, size * width),
            ],
            scratch_shapes=[pltpu.VMEM((part, RANK), bf16)],
        ),
        out_shape=[
            jax.ShapeDtypeStruct((size, part, width), bf16),
            jax.ShapeDtypeStruct((part, wide), f32),
            jax.ShapeDtypeStruct((part, wide), bf16),
            jax.ShapeDtypeStruct((1, wide), f32),
            jax.ShapeDtypeStruct((RANK, wide), f32),
            jax.ShapeDtypeStruct((RANK, size * width), f32),
        ],
        compiler_params=pltpu.CompilerParams(vmem_limit_bytes=VMEM_LIMIT),
        cost_estimate=cost(2 * part * width * size * wide, 2 * width * size * wide),
        name="back_out",
    )(k, *earlier, piece, cotangent, resid, raw, gain, scale, b, own, low, w, a2_t)


def unproject_kernel(heads, scalars, cos_ref, sin_ref, raw_ref, scale_ref, w_ref, *refs):
    take = taker(refs)
    grads = take(heads)
    dz_ref, g_ref, out_ref = refs[heads:]
    width = heads * HD

    @pl.when(pl.program_id(0) == 0)
    def _():
        for layer in range(3):
            for d in range(heads):
                at = pl.ds(pl.multiple_of(layer * width + (scalars[0] ^ d) * HD, HD), HD)
                grad = grads[d][layer].astype(f32)
                if layer != 1:
                    grad = grad * cos_ref[...] - pltpu.roll(grad, HALF, 1) * sin_ref[...]
                raw = raw_ref[:, at].astype(f32)
                g_ref[:, at] = jnp.sum(grad * raw, axis=0, keepdims=True)
                dz_ref[:, at] = (grad * scale_ref[:, at]).astype(bf16)

    out_ref[...] = dot_nt(dz_ref[...], w_ref[...]).astype(bf16)


def unproject(order, cosine, sine, raw, scale, w, grads):
    operands = [cosine, sine, raw, scale]
    rows, wide = raw.shape
    depth = w.shape[0]
    step = 8 * HD
    return pl.pallas_call(
        functools.partial(unproject_kernel, len(grads)),
        grid_spec=pltpu.PrefetchScalarGridSpec(
            num_scalar_prefetch=1,
            grid=(depth // step,),
            in_specs=[whole_spec(x) for x in operands]
            + [pl.BlockSpec((step, wide), lambda i, s: (i, 0))]
            + [whole_spec(x) for x in grads],
            out_specs=[
                whole_spec(raw),
                whole_spec(scale),
                pl.BlockSpec((rows, step), lambda i, s: (0, i)),
            ],
        ),
        out_shape=[
            jax.ShapeDtypeStruct(raw.shape, bf16),
            jax.ShapeDtypeStruct(scale.shape, f32),
            jax.ShapeDtypeStruct((rows, depth), bf16),
        ],
        compiler_params=pltpu.CompilerParams(vmem_limit_bytes=VMEM_LIMIT),
        cost_estimate=cost(2 * rows * wide * depth, 2 * wide * depth),
        name="unproject",
    )(order, *operands, w, *grads)


def shares_kernel(count, chunks, span, *refs):
    take = taker(refs)
    x_refs, dz_refs = take(chunks), take(chunks)
    a_ref, b_ref, w_ref, cross_ref, g_ref, m_ref, column_ref = take(7)
    share_a_ref, share_b_ref = take(2)
    low, up, radial = take(3)
    step = pl.program_id(0)
    wide = b_ref.shape[1]

    @pl.when(step == 0)
    def _():
        up[...] = jnp.zeros_like(up)
        radial[...] = jnp.zeros_like(radial)
        for c in range(chunks):
            low[c] = dot_nt(x_refs[c][...], a_ref[...]).astype(bf16)

    shrink = g_ref[...] * m_ref[...] / (column_ref[...] * column_ref[...] * column_ref[...])
    shape = (count * RANK, wide)
    column = lax.broadcasted_iota(jnp.int32, shape, 1) + step * wide
    layer_of = lax.rem(column // span, count)
    own = (lax.broadcasted_iota(jnp.int32, shape, 0) // RANK) == layer_of
    b_pad = jnp.where(own, jnp.concatenate([b_ref[...]] * count, axis=0), 0.0)
    b_low = b_pad.astype(bf16)
    ap = jnp.zeros(shape, f32)
    for c in range(chunks):
        dz = dz_refs[c][...]
        up[c] += dot_nt(dz, b_low)
        ap += dot_tn(low[c], dz)
    radial[...] += dot_nt((b_pad * shrink).astype(bf16), w_ref[...])
    ap = jnp.where(own, ap, 0.0)
    picked = ap[:RANK]
    for i in range(1, count):
        picked = picked + ap[i * RANK : (i + 1) * RANK]
    share_b_ref[...] = (SCALING * (picked - cross_ref[...] * shrink)).astype(bf16)

    @pl.when(step == pl.num_programs(0) - 1)
    def _():
        total = -radial[...]
        for c in range(chunks):
            total = total + dot_tn(up[c].astype(bf16), x_refs[c][...])
        share_a_ref[...] = (SCALING * total).astype(bf16)


def layer_shares(inputs, a_t, dz, b, span, merged, cross, g, magnitude, column):
    chunks = len(inputs)
    rows, depth = inputs[0].shape
    width = dz[0].shape[1]
    count = a_t.shape[0] // RANK
    step = width // count
    columns = lambda height: pl.BlockSpec((height, step), lambda i: (0, i))
    fixed = lambda x: pl.BlockSpec(x.shape, lambda i: (0, 0))
    return pl.pallas_call(
        functools.partial(shares_kernel, count, chunks, span),
        grid=(width // step,),
        in_specs=[fixed(x) for x in inputs]
        + [columns(rows)] * chunks
        + [fixed(a_t), columns(RANK), columns(depth), columns(RANK)]
        + [columns(1)] * 3,
        out_specs=[fixed(a_t), columns(RANK)],
        out_shape=[
            jax.ShapeDtypeStruct(a_t.shape, bf16),
            jax.ShapeDtypeStruct((RANK, width), bf16),
        ],
        scratch_shapes=[
            pltpu.VMEM((chunks, rows, count * RANK), bf16),
            pltpu.VMEM((chunks, rows, count * RANK), f32),
            pltpu.VMEM(a_t.shape, f32),
        ],
        compiler_params=pltpu.CompilerParams(vmem_limit_bytes=VMEM_LIMIT),
        cost_estimate=cost(rows * depth * 64, depth * width),
        name="shares",
    )(*inputs, *dz, a_t.astype(bf16), b, merged, cross, g, magnitude, column)


def down_kernel(chunks, *refs):
    take = taker(refs)
    act_refs = take(chunks)
    w_ref, cot_ref, scale_ref, a_ref, b_ref = take(5)
    raw_ref, g_ref, ap_ref, pb_ref = take(4)
    low, up = take(2)
    step = pl.program_id(0)
    rows = act_refs[0].shape[0]
    size, _, part, wide = cot_ref.shape

    @pl.when(step == 0)
    def _():
        up[...] = jnp.zeros_like(up)
        for c in range(chunks):
            low[c] = dot_nt(act_refs[c][...], a_ref[...]).astype(bf16)

    g = jnp.zeros((1, wide), f32)
    ap = jnp.zeros((RANK, wide), f32)
    b_low = b_ref[...].astype(bf16)
    for c in range(chunks):
        raw = dot(act_refs[c][...], w_ref[...])
        raw_ref[:, c] = raw.astype(bf16).reshape(size, part, wide)
        cot = cot_ref[:, c].reshape(rows, wide).astype(f32)
        g += jnp.sum(cot * raw, axis=0, keepdims=True)
        dz = (cot * scale_ref[...]).astype(bf16)
        up[c] += dot_nt(dz, b_low)
        ap += dot_tn(low[c], dz)
    g_ref[...] = g
    ap_ref[...] = ap.astype(bf16)

    @pl.when(step == pl.num_programs(0) - 1)
    def _():
        total = jnp.zeros(pb_ref.shape, f32)
        for c in range(chunks):
            total = total + dot_tn(up[c].astype(bf16), act_refs[c][...])
        pb_ref[...] = total.astype(bf16)


def down_project(acts, w, cotangent, scale, a_t, b):
    chunks = len(acts)
    rows, ff = acts[0].shape
    wide = w.shape[1]
    step = 2 * HD
    size, _, part, _ = cotangent.shape
    columns = lambda height: pl.BlockSpec((height, step), lambda i: (0, i))
    fixed = lambda *shape: pl.BlockSpec(shape, lambda i: (0,) * len(shape))
    view = pl.BlockSpec((size, chunks, part, step), lambda i: (0, 0, 0, i))
    return pl.pallas_call(
        functools.partial(down_kernel, chunks),
        grid=(wide // step,),
        in_specs=[fixed(rows, ff)] * chunks
        + [columns(ff), view, columns(1), fixed(RANK, ff), columns(RANK)],
        out_specs=[view, columns(1), columns(RANK), fixed(RANK, ff)],
        out_shape=[
            jax.ShapeDtypeStruct(cotangent.shape, bf16),
            jax.ShapeDtypeStruct((1, wide), f32),
            jax.ShapeDtypeStruct((RANK, wide), bf16),
            jax.ShapeDtypeStruct((RANK, ff), bf16),
        ],
        scratch_shapes=[
            pltpu.VMEM((chunks, rows, RANK), bf16),
            pltpu.VMEM((chunks, rows, RANK), f32),
        ],
        compiler_params=pltpu.CompilerParams(vmem_limit_bytes=VMEM_LIMIT),
        cost_estimate=cost(2 * chunks * rows * ff * wide, 2 * ff * wide),
        name="down_project",
    )(*acts, w, cotangent, scale, a_t.astype(bf16), b)


def pack_kernel(plan, scalars, *refs):
    out_ref = refs[-1]
    out_ref[...] = jnp.zeros_like(out_ref)
    for ref, (parts, placed, rows) in zip(refs[:-1], plan):
        height, width = ref.shape
        wide = width // parts
        lanes = slice(0, wide)
        if placed:
            lanes = pl.ds(pl.multiple_of(scalars[0] * wide, HD), wide)
        if height == 1:
            value = [ref[:, i * wide : (i + 1) * wide].astype(f32) for i in range(parts)]
            value.append(jnp.zeros((RANK - parts, wide), f32))
            value = jnp.concatenate(value, axis=0).astype(bf16)
            out_ref[rows[0] : rows[0] + RANK, lanes] = value
            continue
        for i in range(parts):
            for j in range(height // RANK):
                row = rows[i * (height // RANK) + j]
                value = ref[j * RANK : (j + 1) * RANK, i * wide : (i + 1) * wide].astype(bf16)
                out_ref[row : row + RANK, lanes] = value


def pack(k, height, width, *entries):
    arrays = [entry[0] for entry in entries]
    plan = [entry[1:] for entry in entries]
    return pl.pallas_call(
        functools.partial(pack_kernel, plan),
        grid_spec=pltpu.PrefetchScalarGridSpec(
            num_scalar_prefetch=1,
            grid=(1,),
            in_specs=[whole_spec(x) for x in arrays],
            out_specs=pl.BlockSpec((height, width), lambda i, s: (0, 0)),
        ),
        out_shape=jax.ShapeDtypeStruct((height, width), bf16),
        compiler_params=pltpu.CompilerParams(vmem_limit_bytes=VMEM_LIMIT),
        cost_estimate=cost(height * width, 4 * height * width),
        name="pack",
    )(k, *arrays)


def span_positions(row_ids, span_order, span_len):
    slot_ids = row_ids // span_len
    slot_table = jnp.arange(span_order.shape[0], dtype=jnp.int32)
    picked = jnp.sum(
        jnp.where(slot_ids[:, None] == slot_table[None, :], span_order[None, :], 0), axis=1
    )
    return picked * span_len + row_ids % span_len


def rotary_tables(positions):
    lane = np.arange(HD)
    frequency = (ROPE_BASE ** (-2.0 * (lane % HALF) / HD)).astype(np.float32)
    sign = np.where(lane < HALF, -1.0, 1.0).astype(np.float32)
    angles = positions.astype(f32)[:, None] * frequency[None, :]
    return jnp.cos(angles), jnp.sin(angles) * sign[None, :]


def pick_blocks(blocks, index):
    out = blocks[0]
    for i in range(1, len(blocks)):
        out = jnp.where(index == i, blocks[i], out)
    return out


def inverse_rms(values):
    return lax.rsqrt(jnp.mean(values * values, axis=-1, keepdims=True) + EPS)


def rms_backward(values, gain_vec, grad_in, inverse):
    scaled = grad_in * gain_vec
    return inverse * scaled - values * inverse * inverse * inverse * jnp.mean(
        values * scaled, axis=-1, keepdims=True
    )


def per_device(
    hidden_in,
    cotangent,
    segment_ids,
    padding,
    span_order,
    gain_attn,
    gain_mlp,
    w_query,
    w_key,
    w_value,
    w_out,
    w_gate,
    w_up,
    w_down,
    a_query,
    b_query,
    m_query,
    a_key,
    b_key,
    m_key,
    a_value,
    b_value,
    m_value,
    a_out,
    b_out,
    m_out,
    a_gate,
    b_gate,
    m_gate,
    a_up,
    b_up,
    m_up,
    a_down,
    b_down,
    m_down,
):
    rows, width = hidden_in.shape
    span_len = rows // 2
    near_width = w_query.shape[1]
    peers = near_width // HD
    n_mp = lax.axis_size("mp")
    n_seq = lax.axis_size("seq")
    n_doc = lax.axis_size("doc")
    groups = n_seq // peers
    copies = n_seq * n_doc
    share = rows // n_mp
    chunks = CHUNKS
    part = share // chunks
    k = lax.axis_index("mp")
    doc = lax.axis_index("doc")
    seq = lax.axis_index("seq")
    me = lax.rem(seq, peers)
    my_group = seq // peers
    order = jnp.reshape(me, (1,)).astype(jnp.int32)
    k_scalar = jnp.reshape(k, (1,)).astype(jnp.int32)

    slice_rows = near_width // n_doc
    wo_slice = lax.dynamic_slice_in_dim(w_out, doc * slice_rows, slice_rows, 0)
    wo_all = lax.all_gather(wo_slice, ("mp", "doc"), axis=0, tiled=True)

    slots = [
        2 * (my_group * peers + (me ^ d)) + half for d in range(peers) for half in range(2)
    ]
    slots += [
        2 * (g * peers + (me ^ d)) + half
        for g in range(groups)
        for d in range(peers)
        for half in range(2)
    ]
    slots = jnp.stack(slots)
    table = jnp.arange(span_order.shape[0], dtype=jnp.int32)
    places = jnp.sum(jnp.where(slots[:, None] == table[None, :], span_order[None, :], 0), axis=1)
    scalars = jnp.concatenate([places, k_scalar]).astype(jnp.int32)
    row_ids = jnp.arange(rows, dtype=jnp.int32) + seq * rows
    cosine, sine = rotary_tables(span_positions(row_ids, span_order, span_len))
    codes = seq_exchange([segment_ids * 2 + padding] * peers)
    (hidden_next,) = after([hidden_in], *codes)

    a_heads = jnp.stack([a_key.T, a_value.T, a_query.T])
    b_heads = [b_key, b_value, b_query]
    m_heads = jnp.concatenate([m_key, m_value, m_query])[None, :]
    blocks, normed, wh_low, raw_heads, column_heads, scale_heads, cross_heads = project_heads(
        order,
        hidden_next,
        gain_attn[None, :],
        (w_key, w_value, w_query),
        a_heads,
        jnp.stack(b_heads),
        jnp.stack([m_key, m_value, m_query])[:, None, :],
        cosine,
        sine,
    )
    heads = seq_exchange(blocks)

    codes = [x.reshape(rows, 1) for x in codes]
    w_out_next, w_down_next, w_gate_next, w_up_next = after(
        [w_out, w_down, w_gate, w_up], raw_heads
    )
    (
        square_out,
        cross_out,
        square_down,
        cross_down,
        wd_low,
        wgu_low,
        cross_gu,
        column_gu,
        scale_gu,
        m_gu,
        b_gu,
    ) = merge_others(
        (w_out_next, a_out.T, b_out),
        (w_down_next, a_down.T, b_down),
        (w_gate_next, a_gate.T, b_gate, m_gate[None, :]),
        (w_up_next, a_up.T, b_up, m_up[None, :]),
    )

    extra = []
    if groups > 1:
        members = [[g * peers + i for g in range(groups)] for i in range(peers)]
        gather = lambda x: lax.all_gather(
            x[None], "seq", axis=0, tiled=True, axis_index_groups=members
        )
        extra = [gather(jnp.stack([x[:2] for x in heads])), gather(jnp.stack(codes))]
    heads_next = after(heads, square_out)
    o_blocks, lse = attention_forward(
        scalars, heads_next, codes, extra, groups, n_mp, chunks
    )
    o_heads = seq_exchange(o_blocks)
    near_chunks = assemble(order, o_heads, square_out, square_down, a_out.T, chunks)

    def chunked(values):
        return values.reshape(n_mp, chunks, part, values.shape[-1])

    hid_view, cot_view = chunked(hidden_in), chunked(cotangent)
    b_out_low = b_out.astype(bf16)
    acts, hnorms, dz_gus, dh_chunks = [], [], [], []
    resid_own, raw_out_own, out_low_own, near_own = [], [], [], []
    g_gu = 0.0
    lines = ([near_chunks[0]], [near_chunks[0]])
    for step in range(1, n_mp):
        line_step(*lines, step)
    gathered_chunks = [line_blocks(*lines)]
    for c in range(1, chunks):
        (near_next,) = after([near_chunks[c]], wo_all, *gathered_chunks[0])
        others = lax.all_gather(near_next, "mp", axis=0)
        gathered_chunks.append(
            [near_chunks[c]]
            + [
                lax.dynamic_index_in_dim(others, lax.rem(k + i, n_mp), 0, keepdims=False)
                for i in range(1, n_mp)
            ]
        )
    column_out, column_down, scale_out, scale_down, a_out_low = unpack(
        k_scalar, gathered_chunks[0], n_mp * part, m_out[None, :], m_down[None, :]
    )
    a_out_twice = SCALING * a_out_low
    for c in range(chunks):
        gathered = gathered_chunks[c]
        if c > 0:
            gathered = after(gathered, dh_chunks[-1])
        hnorm, resid, raw_out, out_low, own, act, dz_gu, g, dh = block(
            k_scalar,
            c,
            gathered,
            a_out_low,
            hid_view,
            (SCALING * b_out).astype(bf16),
            scale_out,
            gain_mlp[None, :],
            cot_view,
            scale_down,
            scale_gu,
            wo_all,
            wgu_low,
            wd_low,
        )
        g_gu = g_gu + g
        dh_chunks.append(dh)
        acts.append(act)
        hnorms.append(hnorm)
        dz_gus.append(dz_gu)
        resid_own.append(resid)
        raw_out_own.append(raw_out)
        out_low_own.append(out_low)
        near_own.append(own)

    def scatter(parts):
        return lax.psum_scatter(parts, "mp", scatter_dimension=0, tiled=True)

    pieces = [scatter(x) for x in dh_chunks]

    arrived, dresid_own, dz_out = [], [], []
    out_sums = ()
    earlier = dh_chunks[-1]
    for c in range(chunks):
        (own_piece,) = after([pieces[c]], earlier)
        dattn, dresid, dz, *out_sums = back_out(
            k_scalar,
            c,
            own_piece,
            cot_view,
            resid_own[c],
            raw_out_own[c],
            gain_mlp[None, :],
            scale_out,
            b_out_low,
            near_own[c],
            out_low_own[c],
            wo_all,
            a_out_twice,
            out_sums,
        )
        arrived.append(dattn[0])
        (dattn,) = after([dattn], *pieces)
        for shift in range(1, n_mp):
            pairs = [(i, (i + shift) % n_mp) for i in range(n_mp)]
            arrived.append(lax.ppermute(dattn[shift], "mp", pairs))
        dresid_own.append(dresid)
        dz_out.append(dz)
        earlier = dz
        if c == 0:
            acts_next = after(acts, dz)
            raw_down, g_down, ap_down, pb_down = down_project(
                acts_next, wd_low, cot_view, scale_down, a_down.T, b_down
            )
            earlier = g_down
    arrived = jnp.concatenate(arrived, axis=0)
    by_head = [arrived[:, h * HD : (h + 1) * HD] for h in range(peers)]
    grad_blocks = seq_exchange([pick_blocks(by_head, me ^ d) for d in range(peers)])
    dresid_own = jnp.concatenate(dresid_own, axis=0)
    g_out, ap_out, pb_out = out_sums

    grads, dkv = attention_backward(
        scalars, heads_next, codes, extra, o_blocks, grad_blocks, lse, groups, n_mp, chunks
    )
    if groups > 1:
        members = [[g * peers + i for g in range(groups)] for i in range(peers)]
        dkv = lax.psum_scatter(
            dkv, "seq", scatter_dimension=0, tiled=True, axis_index_groups=members
        )
        grads = [jnp.concatenate([dkv[0, d], grads[d]], axis=0) for d in range(peers)]
    head_grads = seq_exchange(grads)

    hnorms_next, dz_gus_next = after([tuple(hnorms), tuple(dz_gus)], grads[0])
    share_a_gu, share_b_gu = layer_shares(
        hnorms_next,
        jnp.concatenate([a_gate.T, a_up.T], axis=0),
        dz_gus_next,
        b_gu,
        HD,
        wgu_low,
        cross_gu,
        g_gu,
        m_gu,
        column_gu,
    )
    (raw_down,) = after([raw_down], *grad_blocks)
    down_own = scatter(raw_down.reshape(rows, width))
    head_grads = after(head_grads, share_a_gu)

    dz_heads, g_heads, dnormed = unproject(
        order, cosine, sine, raw_heads, scale_heads, wh_low, head_grads
    )
    dnormed_own = scatter(dnormed)

    (down_own,) = after([down_own], dnormed)
    result = jnp.concatenate(resid_own, axis=0) + down_own.astype(f32) * scale_down
    hidden_own = lax.dynamic_slice_in_dim(hidden_in, k * share, share, 0).astype(f32)


    share_a_heads, share_b_heads = layer_shares(
        [normed],
        a_heads.reshape(3 * RANK, width),
        [dz_heads],
        jnp.concatenate(b_heads, axis=1),
        near_width,
        wh_low,
        cross_heads,
        g_heads,
        m_heads,
        column_heads,
    )
    parts = n_doc * peers
    part_rows = 3 * RANK
    summed = [(u // 2) * part_rows + (u % 2) * RANK for u in range(2 * parts)]
    apart = [u * part_rows + 2 * RANK for u in range(parts)]
    totals = pack(
        k_scalar,
        parts * part_rows,
        width,
        (share_a_gu, 1, False, summed[0:2]),
        (ap_down, 1, False, summed[2:3]),
        (cross_out / copies, 1, False, summed[3:4]),
        (cross_down / copies, 1, False, summed[4:5]),
        (ap_out, 1, False, summed[5:6]),
        (jnp.concatenate([g_down, g_out], axis=1), 2, False, summed[6:7]),
        (pb_out, 1, False, summed[7:8]),
        (share_a_heads, 1, False, summed[8:11]),
        (share_b_heads, 3, True, summed[11:14]),
        (g_heads, 3, True, summed[14:15]),
        (share_b_gu, 2, False, apart[0:2]),
        (pb_down, 1, False, apart[2:3]),
        (g_gu, 2, False, apart[3:4]),
    )
    totals = spread_join(spread_sum(doc_halve(totals), peers, ["mp"], 2 * RANK), peers)
    hidden_inverse = inverse_rms(hidden_own)
    (totals,) = after([totals], dnormed_own, result, hidden_inverse)
    totals = doc_join(totals).astype(f32)

    def unit(index, rows=RANK):
        return totals[summed[index] : summed[index] + rows]

    def own_columns(values):
        return lax.dynamic_slice_in_dim(values, k * near_width, near_width, 1)

    def unit_apart(index, rows=RANK):
        return totals[apart[index] : apart[index] + rows, : w_gate.shape[1]]

    grad_input = dresid_own + rms_backward(
        hidden_own, gain_attn, dnormed_own.astype(f32), hidden_inverse
    )

    total_g_down, total_g_out = unit(6, 2)[:1], unit(6, 2)[1:]
    shrink_out = total_g_out * m_out / (column_out * column_out * column_out)
    shrink_down = total_g_down * m_down / (column_down * column_down * column_down)
    turned_out = (b_out * shrink_out).astype(bf16)
    radial_out = dot_nt(turned_out, w_out) + SCALING * dot(
        dot_nt(turned_out, b_out.astype(bf16)), a_out.T
    )
    radial_down = dot_nt((b_down * shrink_down).astype(bf16), wd_low)
    grad_a_out = SCALING * (own_columns(unit(7)) - radial_out)
    grad_a_down = SCALING * (unit_apart(2) - radial_down)
    grad_b_out = SCALING * (unit(5) - unit(3) * shrink_out)
    grad_b_down = SCALING * (unit(2) - unit(4) * shrink_down)
    g_rows = own_columns(unit(14, 3))
    g_rows = [
        g_rows[i] / column_heads[0, i * near_width : (i + 1) * near_width] for i in range(3)
    ]
    both = jnp.concatenate([unit_apart(0), unit_apart(1)], axis=1)
    g_both = jnp.concatenate([unit_apart(3, 2)[:1], unit_apart(3, 2)[1:]], axis=1)
    grad_m_gate, grad_m_up = separate(g_both / column_gu)
    grad_b_gate, grad_b_up = separate(both)
    return (
        result,
        grad_input,
        unit(10).T,
        own_columns(unit(13)),
        g_rows[2],
        unit(8).T,
        own_columns(unit(11)),
        g_rows[0],
        unit(9).T,
        own_columns(unit(12)),
        g_rows[1],
        grad_a_out.T,
        grad_b_out,
        (total_g_out / column_out)[0],
        unit(0).T,
        grad_b_gate,
        grad_m_gate[0],
        unit(1).T,
        grad_b_up,
        grad_m_up[0],
        grad_a_down.T,
        grad_b_down,
        (total_g_down / column_down)[0],
    )


def solution(mesh):
    rows = P(("doc", "seq"))
    split_columns = (P(None, "mp"), P(None, "mp"))
    column_layer = (P(), P(None, "mp"), P("mp"))
    row_layer = (P("mp", None), P(), P())
    in_specs = (
        P(("doc", "seq"), None),
        P(("doc", "seq"), None),
        rows,
        rows,
        P(),
        P(),
        P(),
        P(None, "mp"),
        P(None, "mp"),
        P(None, "mp"),
        P("mp", None),
        *split_columns,
        P("mp", None),
        *column_layer,
        *column_layer,
        *column_layer,
        *row_layer,
        *column_layer,
        *column_layer,
        *row_layer,
    )
    out_specs = (
        P(("doc", "seq", "mp"), None),
        P(("doc", "seq", "mp"), None),
        *column_layer,
        *column_layer,
        *column_layer,
        *row_layer,
        *column_layer,
        *column_layer,
        *row_layer,
    )
    return jax.shard_map(
        per_device, mesh=mesh, in_specs=in_specs, out_specs=out_specs, check_vma=False
    )
```

```python
import functools
import math

import jax
import jax.numpy as jnp
import numpy as np
from jax import lax
from jax.experimental import pallas as pl
from jax.experimental.pallas import tpu as pltpu
from jax.sharding import PartitionSpec as P

HD = 128
RANK = 16
ALPHA = 32
HALF = HD // 2
SCALING = ALPHA / RANK
INV_ROOT = HD ** (-0.5)
EPS = 1e-05
ROPE_BASE = 10000.0
MASKED = -1e30
CHUNKS = 2
MIB = 1 << 20
VMEM_LIMIT = 56 * MIB

f32 = jnp.float32
bf16 = jnp.bfloat16


def dot(left, right):
    return jnp.dot(left, right, preferred_element_type=f32)


def dot_nt(left, right):
    return lax.dot_general(left, right, (((1,), (1,)), ((), ())), preferred_element_type=f32)


def dot_tn(left, right):
    return lax.dot_general(left, right, (((0,), (0,)), ((), ())), preferred_element_type=f32)


def whole_spec(array):
    rank = len(array.shape)
    return pl.BlockSpec(tuple(array.shape), lambda *_: (0,) * rank)


def cost(flops, moved):
    return pl.CostEstimate(flops=1, bytes_accessed=1, transcendentals=0)


def swap(value, axis, distance):
    size = lax.axis_size(axis)
    return lax.ppermute(value, axis, [(i, i ^ distance) for i in range(size)])


def butterfly(value, axes):
    for axis in axes:
        distance = 1
        while distance < lax.axis_size(axis):
            value = lax.optimization_barrier(value + swap(value, axis, distance))
            distance *= 2
    return value


def doc_halve(value):
    doc = lax.axis_index("doc")
    half = value.shape[0] // 2
    mine = lax.dynamic_slice_in_dim(value, doc * half, half, 0)
    other = lax.dynamic_slice_in_dim(value, (1 - doc) * half, half, 0)
    return lax.optimization_barrier(mine + swap(other, "doc", 1))


def doc_join(mine):
    doc = lax.axis_index("doc")
    other = swap(mine, "doc", 1)
    first = jnp.where(doc == 0, mine, other)
    second = jnp.where(doc == 0, other, mine)
    return jnp.concatenate([first, second], axis=0)


def spread_sum(value, peers, axes, leading):
    me = lax.rem(lax.axis_index("seq"), peers)
    parts = value.reshape(peers, -1, value.shape[-1])
    piece = lambda index: lax.dynamic_index_in_dim(parts, index, 0, keepdims=False)
    mine = piece(me).astype(f32)
    for d in range(1, peers):
        mine = mine + swap(piece(me ^ d), "seq", d).astype(f32)
    mine = lax.optimization_barrier(mine.astype(bf16))
    distance = peers
    while distance < lax.axis_size("seq"):
        mine = lax.optimization_barrier(mine + swap(mine, "seq", distance))
        distance *= 2
    return jnp.concatenate([butterfly(mine[:leading], axes), mine[leading:]], axis=0)


def spread_join(mine, peers):
    me = lax.rem(lax.axis_index("seq"), peers)
    found = [mine] + [swap(mine, "seq", d) for d in range(1, peers)]
    return jnp.concatenate([pick_blocks(found, me ^ i) for i in range(peers)], axis=0)


def after(values, *earlier):
    tied = lax.optimization_barrier((tuple(values), earlier))
    return tied[0]


def line_step(rights, lefts, step, *earlier):
    size = lax.axis_size("mp")
    right, left = rights[-1], lefts[-1]
    if earlier:
        right, left = after([right, left], *earlier)
    right_pairs = [(i, i + 1) for i in range(step - 1, size - 1)]
    left_pairs = [(i, i - 1) for i in range(1, size - step + 1)]
    rights.append(lax.ppermute(right, "mp", right_pairs))
    lefts.append(lax.ppermute(left, "mp", left_pairs))


def line_blocks(rights, lefts):
    size = lax.axis_size("mp")
    k = lax.axis_index("mp")
    return [rights[0]] + [
        jnp.where(k + c < size, lefts[c], rights[size - c]) for c in range(1, size)
    ]


def seq_exchange(blocks):
    return [blocks[0]] + [swap(blocks[d], "seq", d) for d in range(1, len(blocks))]


def key_marks(code):
    lane = lax.broadcasted_iota(jnp.int32, (code.shape[0], HD), 1)
    segment, real = code >> 1, code & 1
    wrong = (lane < 16) & (lane != segment)
    absent = (lane == 16) & (real == 0)
    return jnp.where(wrong | absent, MASKED, 0.0).astype(bf16)


def query_marks(code):
    lane = lax.broadcasted_iota(jnp.int32, (code.shape[0], HD), 1)
    segment = code >> 1
    return jnp.where((lane == segment) | (lane == 16), 1.0, 0.0).astype(bf16)


def diagonal_scores(keys, query):
    marked = dot_nt(keys, query)
    plain = dot_nt(keys[:, :HD], query[:, :HD])
    key_id = lax.broadcasted_iota(jnp.int32, marked.shape, 0)
    query_id = lax.broadcasted_iota(jnp.int32, marked.shape, 1)
    return jnp.where(
        key_id < query_id, marked, jnp.where(key_id == query_id, plain, MASKED)
    )


def block_readers(groups, heads, kv_refs, code_refs):
    if groups == 1:
        return (
            lambda g, d, rows: heads[d][0, rows, :],
            lambda g, d, rows: heads[d][1, rows, :],
            lambda g, d, rows: code_refs[d][rows, :],
        )
    return (
        lambda g, d, rows: kv_refs[0][g, d, 0, rows, :],
        lambda g, d, rows: kv_refs[0][g, d, 1, rows, :],
        lambda g, d, rows: kv_refs[1][g, d, rows, :],
    )


def taker(refs):
    refs = list(refs)

    def take(count):
        taken = refs[:count]
        del refs[:count]
        return taken

    return take


def forward_kernel(meta, scalars, *refs):
    peers, groups, span, pieces, chunks, n_extra = meta
    take = taker(refs)
    heads, code_refs, kv_refs = take(peers), take(peers), take(n_extra)
    o_refs, (lse_ref,) = take(peers), take(1)
    q_all, o_all, k_all, v_turned = take(4)
    key_of, value_of, key_code_of = block_readers(groups, heads, kv_refs, code_refs)
    n_query = 2 * peers

    for g in range(groups):
        for d in range(peers):
            for half in range(2):
                rows = pl.ds(half * span, span)
                place = scalars[n_query + (g * peers + d) * 2 + half]
                at = pl.ds(pl.multiple_of(place * span, HD), span)
                k_all[at, :HD] = key_of(g, d, rows)
                k_all[at, HD:] = key_marks(key_code_of(g, d, rows))
                v_turned[:, at] = value_of(g, d, rows).astype(f32).T.astype(bf16)
    for d in range(peers):
        for half in range(2):
            rows = pl.ds(half * span, span)
            q_all[2 * d + half, :, :HD] = heads[d][2, rows, :]
            q_all[2 * d + half, :, HD:] = query_marks(code_refs[d][rows, :])

    def one_span(i, carry):
        place = scalars[i]
        query = q_all[i]
        at = pl.ds(pl.multiple_of(place * span, HD), span)
        scores = diagonal_scores(k_all[at, :], query)
        peak = jnp.max(scores, axis=0, keepdims=True)
        weights = jnp.exp((scores - peak) * INV_ROOT)
        total = jnp.sum(weights, axis=0, keepdims=True)
        out = dot(v_turned[:, at], weights.astype(bf16))

        def key_span(j, state):
            peak, total, out = state
            at = pl.ds(pl.multiple_of(j * span, HD), span)
            scores = dot_nt(k_all[at, :], query)
            new_peak = jnp.maximum(peak, jnp.max(scores, axis=0, keepdims=True))
            fade = jnp.exp((peak - new_peak) * INV_ROOT)
            weights = jnp.exp((scores - new_peak) * INV_ROOT)
            total = total * fade + jnp.sum(weights, axis=0, keepdims=True)
            out = out * fade + dot(v_turned[:, at], weights.astype(bf16))
            return (new_peak, total, out)

        peak, total, out = lax.fori_loop(0, place, key_span, (peak, total, out))
        lse_ref[i] = peak * INV_ROOT + jnp.log(total)
        o_all[i] = (out / total).T.astype(bf16)
        return carry

    lax.fori_loop(0, n_query, one_span, 0)
    share = 2 * span // pieces
    part = share // chunks
    for d in range(peers):
        for piece in range(pieces):
            for c in range(chunks):
                row = piece * share + c * part
                to = (c * pieces + piece) * part
                o_refs[d][to : to + part, :] = o_all[
                    2 * d + row // span, row % span : row % span + part, :
                ]


def place_rows(scalars, peers, span):
    for d in range(peers):
        for half in range(2):
            place = scalars[2 * d + half]
            at = pl.ds(pl.multiple_of(place * span, HD), span)
            yield d, half, pl.ds(half * span, span), at


def piece_rows(peers, span, pieces, chunks):
    share = 2 * span // pieces
    part = share // chunks
    for d in range(peers):
        for piece in range(pieces):
            for c in range(chunks):
                row = piece * share + c * part
                yield d, piece, c, pl.ds((c * pieces + piece) * part, part), row, part


def forward_group_kernel(meta, scalars, *refs):
    peers, _, span, pieces, chunks, _ = meta
    take = taker(refs)
    heads, code_refs = take(peers), take(peers)
    o_refs, (lse_ref,) = take(peers), take(1)
    q_all, o_all, k_all, v_turned = take(4)
    tile = 2 * span

    for d, half, rows, at in place_rows(scalars, peers, span):
        code = code_refs[d][rows, :]
        k_all[at, :HD] = heads[d][0, rows, :]
        k_all[at, HD:] = key_marks(code)
        v_turned[:, at] = heads[d][1, rows, :].astype(f32).T.astype(bf16)
        q_all[at, :HD] = heads[d][2, rows, :]
        q_all[at, HD:] = query_marks(code)

    for m in range(peers):
        here = slice(m * tile, (m + 1) * tile)
        query = q_all[here, :]
        scores = diagonal_scores(k_all[here, :], query)
        peak = jnp.max(scores, axis=0, keepdims=True)
        weights = jnp.exp((scores - peak) * INV_ROOT)
        total = jnp.sum(weights, axis=0, keepdims=True)
        out = dot(v_turned[:, here], weights.astype(bf16))

        def key_tile(j, state):
            peak, total, out = state
            at = pl.ds(pl.multiple_of(j * tile, HD), tile)
            scores = dot_nt(k_all[at, :], query)
            new_peak = jnp.maximum(peak, jnp.max(scores, axis=0, keepdims=True))
            fade = jnp.exp((peak - new_peak) * INV_ROOT)
            weights = jnp.exp((scores - new_peak) * INV_ROOT)
            total = total * fade + jnp.sum(weights, axis=0, keepdims=True)
            out = out * fade + dot(v_turned[:, at], weights.astype(bf16))
            return (new_peak, total, out)

        if m:
            peak, total, out = lax.fori_loop(0, m, key_tile, (peak, total, out))
        lse_ref[m] = peak * INV_ROOT + jnp.log(total)
        o_all[here, :] = (out / total).T.astype(bf16)

    for d, piece, c, to, row, part in piece_rows(peers, span, pieces, chunks):
        place = scalars[2 * d + row // span] * span + row % span
        o_refs[d][to, :] = o_all[pl.ds(pl.multiple_of(place, 32), part), :]


def backward_group_kernel(meta, scalars, *refs):
    peers, groups, span, pieces, chunks, _ = meta
    take = taker(refs)
    heads, code_refs = take(peers), take(peers)
    o_refs, do_refs, (lse_ref,) = take(peers), take(peers), take(1)
    grad_refs = take(peers)
    q_all, o_all, do_all, k_all, k_turned, v_all, dk_all, dv_all = take(8)
    own_piece = scalars[4 * peers]
    tile = 2 * span
    share = 2 * span // pieces

    for d, half, rows, at in place_rows(scalars, peers, span):
        code = code_refs[d][rows, :]
        key = heads[d][0, rows, :]
        k_all[at, :HD] = key
        k_all[at, HD:] = key_marks(code)
        k_turned[:, at] = key.astype(f32).T.astype(bf16)
        v_all[at, :] = heads[d][1, rows, :]
        q_all[at, :HD] = heads[d][2, rows, :]
        q_all[at, HD:] = query_marks(code)
    for d, piece, c, source, row, part in piece_rows(peers, span, pieces, chunks):
        place = scalars[2 * d + row // span] * span + row % span
        o_all[pl.ds(pl.multiple_of(place, 32), part), :] = o_refs[d][source, :]
        row = lax.rem(own_piece + pieces - piece, pieces) * share + c * part
        late = row >= span
        place = scalars[2 * d + late.astype(jnp.int32)] * span + row - jnp.where(late, span, 0)
        do_all[pl.ds(pl.multiple_of(place, 32), part), :] = do_refs[d][source, :]

    for m in range(peers):
        here = slice(m * tile, (m + 1) * tile)
        query = q_all[here, :]
        grad = do_all[here, :]
        product = grad.astype(f32) * o_all[here, :].astype(f32)
        high, rest = split_low(product)
        ones = jnp.ones((16, HD), bf16)
        delta = (dot_nt(ones, high) + dot_nt(ones, rest))[:1, :]
        lse = lse_ref[m]

        def key_tile(at, scores, dq_turned, first):
            probs = jnp.exp(scores * INV_ROOT - lse)
            grad_score = (probs * (dot_nt(v_all[at, :], grad) - delta)).astype(bf16)
            dv = dot(probs.astype(bf16), grad)
            dk = dot(grad_score, query[:, :HD])
            if first:
                dv_all[at, :] = dv
                dk_all[at, :] = dk
            else:
                dv_all[at, :] += dv
                dk_all[at, :] += dk
            return dq_turned + dot(k_turned[:, at], grad_score)

        scores = diagonal_scores(k_all[here, :], query)
        dq_turned = key_tile(here, scores, jnp.zeros((HD, tile), f32), True)

        def step(j, dq_turned):
            at = pl.ds(pl.multiple_of(j * tile, HD), tile)
            return key_tile(at, dot_nt(k_all[at, :], query), dq_turned, False)

        if m:
            dq_turned = lax.fori_loop(0, m, step, dq_turned)
        o_all[here, :] = (dq_turned * INV_ROOT).T.astype(bf16)

    for d, half, rows, at in place_rows(scalars, peers, span):
        grad_refs[d][0, rows, :] = (dk_all[at, :] * INV_ROOT).astype(bf16)
        grad_refs[d][1, rows, :] = dv_all[at, :].astype(bf16)
        grad_refs[d][2, rows, :] = o_all[at, :]


def attention_forward(scalars, heads, codes, extra, groups, pieces, chunks):
    peers = len(heads)
    rows = heads[0].shape[1]
    span = rows // 2
    key_rows = groups * peers * rows
    meta = (peers, groups, span, pieces, chunks, len(extra))
    operands = [*heads, *codes, *extra]
    out_shape = [jax.ShapeDtypeStruct((rows, HD), bf16)] * peers
    n_query = 2 * peers if groups > 1 else peers
    out_shape.append(jax.ShapeDtypeStruct((n_query, 1, 2 * peers * span // n_query), f32))
    if groups == 1:
        body, q_shape, o_shape = forward_group_kernel, (key_rows, 2 * HD), (key_rows, HD)
    else:
        body, q_shape, o_shape = (
            forward_kernel,
            (2 * peers, span, 2 * HD),
            (2 * peers, span, HD),
        )
    outs = pl.pallas_call(
        functools.partial(body, meta),
        grid_spec=pltpu.PrefetchScalarGridSpec(
            num_scalar_prefetch=1,
            grid=(1,),
            in_specs=[whole_spec(x) for x in operands],
            out_specs=[whole_spec(x) for x in out_shape],
            scratch_shapes=[
                pltpu.VMEM(q_shape, bf16),
                pltpu.VMEM(o_shape, bf16),
                pltpu.VMEM((key_rows, 2 * HD), bf16),
                pltpu.VMEM((HD, key_rows), bf16),
            ],
        ),
        out_shape=out_shape,
        compiler_params=pltpu.CompilerParams(vmem_limit_bytes=VMEM_LIMIT),
        cost_estimate=cost(6 * peers * rows * key_rows // 2 * HD, 8 * key_rows * HD),
        name="attend",
    )(scalars, *operands)
    return outs[:-1], outs[-1]


def backward_kernel(meta, scalars, *refs):
    peers, groups, span, pieces, chunks, n_extra = meta
    take = taker(refs)
    heads, code_refs, kv_refs = take(peers), take(peers), take(n_extra)
    o_refs, do_refs, (lse_ref,) = take(peers), take(peers), take(1)
    grad_refs = take(peers)
    dkv_refs = take(1 if groups > 1 else 0)
    q_all, o_all, do_all, k_all, k_turned, v_all, dk_all, dv_all = take(8)
    key_of, value_of, key_code_of = block_readers(groups, heads, kv_refs, code_refs)
    n_query = 2 * peers
    own_piece = scalars[n_query + 2 * groups * peers]

    for g in range(groups):
        for d in range(peers):
            for half in range(2):
                rows = pl.ds(half * span, span)
                place = scalars[n_query + (g * peers + d) * 2 + half]
                at = pl.ds(pl.multiple_of(place * span, HD), span)
                key = key_of(g, d, rows)
                k_all[at, :HD] = key
                k_all[at, HD:] = key_marks(key_code_of(g, d, rows))
                k_turned[:, at] = key.astype(f32).T.astype(bf16)
                v_all[at, :] = value_of(g, d, rows)
    dk_all[...] = jnp.zeros_like(dk_all)
    dv_all[...] = jnp.zeros_like(dv_all)
    share = 2 * span // pieces
    part = share // chunks
    for d in range(peers):
        for half in range(2):
            rows = pl.ds(half * span, span)
            q_all[2 * d + half, :, :HD] = heads[d][2, rows, :]
            q_all[2 * d + half, :, HD:] = query_marks(code_refs[d][rows, :])
        for piece in range(pieces):
            origin = lax.rem(own_piece + pieces - piece, pieces)
            for c in range(chunks):
                source = pl.ds((c * pieces + piece) * part, part)
                row = (2 * d * span) + piece * share + c * part
                o_all[row : row + part, :] = o_refs[d][source, :]
                row = (2 * d * span) + origin * share + c * part
                do_all[pl.ds(pl.multiple_of(row, 16), part), :] = do_refs[d][source, :]

    def one_span(i, carry):
        place = scalars[i]
        query = q_all[i]
        rows = pl.ds(pl.multiple_of(i * span, HD), span)
        grad = do_all[rows, :]
        product = grad.astype(f32) * o_all[rows, :].astype(f32)
        high = product.astype(bf16)
        rest = (product - high.astype(f32)).astype(bf16)
        ones = jnp.ones((16, HD), bf16)
        delta = (dot_nt(ones, high) + dot_nt(ones, rest))[:1, :]
        lse = lse_ref[i]

        def key_span(at, scores, dq_turned):
            probs = jnp.exp(scores * INV_ROOT - lse)
            grad_prob = dot_nt(v_all[at, :], grad)
            grad_score = (probs * (grad_prob - delta)).astype(bf16)
            dv_all[at, :] += dot(probs.astype(bf16), grad)
            dk_all[at, :] += dot(grad_score, query[:, :HD])
            return dq_turned + dot(k_turned[:, at], grad_score)

        at = pl.ds(pl.multiple_of(place * span, HD), span)
        dq_turned = key_span(
            at, diagonal_scores(k_all[at, :], query), jnp.zeros((HD, span), f32)
        )

        def step(j, dq_turned):
            at = pl.ds(pl.multiple_of(j * span, HD), span)
            return key_span(at, dot_nt(k_all[at, :], query), dq_turned)

        dq_turned = lax.fori_loop(0, place, step, dq_turned)
        o_all[rows, :] = (dq_turned * INV_ROOT).T.astype(bf16)
        return carry

    lax.fori_loop(0, n_query, one_span, 0)
    at_query = 2 if groups == 1 else 0
    for d in range(peers):
        grad_refs[d][at_query] = o_all[2 * d * span : 2 * (d + 1) * span, :]
    for g in range(groups):
        for d in range(peers):
            for half in range(2):
                rows = pl.ds(half * span, span)
                place = scalars[n_query + (g * peers + d) * 2 + half]
                at = pl.ds(pl.multiple_of(place * span, HD), span)
                grad_key = (dk_all[at, :] * INV_ROOT).astype(bf16)
                grad_value = dv_all[at, :].astype(bf16)
                if groups == 1:
                    grad_refs[d][0, rows, :] = grad_key
                    grad_refs[d][1, rows, :] = grad_value
                else:
                    dkv_refs[0][g, d, 0, rows, :] = grad_key
                    dkv_refs[0][g, d, 1, rows, :] = grad_value


def attention_backward(scalars, heads, codes, extra, o, grads, lse, groups, pieces, chunks):
    peers = len(heads)
    rows = heads[0].shape[1]
    span = rows // 2
    key_rows = groups * peers * rows
    meta = (peers, groups, span, pieces, chunks, len(extra))
    operands = [*heads, *codes, *extra, *o, *grads, lse]
    parts = 3 if groups == 1 else 1
    out_shape = [jax.ShapeDtypeStruct((parts, rows, HD), bf16)] * peers
    if groups > 1:
        out_shape.append(jax.ShapeDtypeStruct(extra[0].shape, bf16))
    if groups == 1:
        body, q_shape = backward_group_kernel, (key_rows, 2 * HD)
    else:
        body, q_shape = backward_kernel, (2 * peers, span, 2 * HD)
    outs = pl.pallas_call(
        functools.partial(body, meta),
        grid_spec=pltpu.PrefetchScalarGridSpec(
            num_scalar_prefetch=1,
            grid=(1,),
            in_specs=[whole_spec(x) for x in operands],
            out_specs=[whole_spec(x) for x in out_shape],
            scratch_shapes=[
                pltpu.VMEM(q_shape, bf16),
                pltpu.VMEM((peers * rows, HD), bf16),
                pltpu.VMEM((peers * rows, HD), bf16),
                pltpu.VMEM((key_rows, 2 * HD), bf16),
                pltpu.VMEM((HD, key_rows), bf16),
                pltpu.VMEM((key_rows, HD), bf16),
                pltpu.VMEM((key_rows, HD), f32),
                pltpu.VMEM((key_rows, HD), f32),
            ],
        ),
        out_shape=out_shape,
        compiler_params=pltpu.CompilerParams(vmem_limit_bytes=VMEM_LIMIT),
        cost_estimate=cost(14 * peers * rows * key_rows // 2 * HD, 16 * key_rows * HD),
        name="attend_back",
    )(scalars, *operands)
    if groups == 1:
        return outs, None
    return outs[:peers], outs[peers]


def split_low(value):
    high = value.astype(bf16)
    return high, (value - high.astype(f32)).astype(bf16)


def low_rank(a_t, b):
    a_high, a_rest = split_low(a_t)
    b_high, b_rest = split_low(b * SCALING)
    a_cat = jnp.concatenate([a_high, a_rest, a_high], axis=0)
    b_cat = jnp.concatenate([b_high, b_high, b_rest], axis=0)
    return dot_tn(a_cat, b_cat)


def separate(both):
    rows, width = both.shape
    both = both.reshape(rows, -1, 2, HD)
    return both[:, :, 0].reshape(rows, width // 2), both[:, :, 1].reshape(rows, width // 2)


def merge_kernel(starts, out_w, out_a, out_b, down_w, down_a, down_b, gate_w, up_w, gate_a, up_a,
                 gate_b, up_b, gate_m, up_m, out_square, out_cross, down_square, down_cross,
                 down_low, pair_low, pair_cross, pair_column, pair_scale, mixed_m, mixed_b):
    step = pl.program_id(0)
    down_start, pair_start = starts

    def columns(w_ref, a_ref, b_ref, square_ref, cross_ref, low_ref):
        merged = w_ref[...].astype(f32) + low_rank(a_ref[...], b_ref[...])
        low = merged.astype(bf16)
        if low_ref is not None:
            low_ref[...] = low
        square_ref[...] = jnp.sum(merged * merged, axis=0, keepdims=True)
        cross_ref[...] = dot(a_ref[...].astype(bf16), low)

    @pl.when(step < down_start)
    def _():
        columns(out_w, out_a, out_b, out_square, out_cross, None)

    @pl.when((step >= down_start) & (step < pair_start))
    def _():
        columns(down_w, down_a, down_b, down_square, down_cross, down_low)

    sides = ((gate_w, gate_a, gate_b, gate_m), (up_w, up_a, up_b, up_m))
    blocks = [
        (side, slice(j * HD, (j + 1) * HD), pl.ds((2 * j + side) * HD, HD))
        for side in range(2)
        for j in range(gate_w.shape[1] // HD)
    ]

    @pl.when(step == pair_start)
    def _():
        pair_column[...] = jnp.zeros_like(pair_column)
        pair_cross[...] = jnp.zeros_like(pair_cross)
        for side, source, at in blocks:
            mixed_b[:, at] = sides[side][2][:, source]
            mixed_m[:, at] = sides[side][3][:, source]

    @pl.when(step >= pair_start)
    def _():
        results = []
        for w_ref, a_ref, b_ref, _ in sides:
            merged = w_ref[...].astype(f32) + low_rank(a_ref[...], b_ref[...])
            low = merged.astype(bf16)
            square = jnp.sum(merged * merged, axis=0, keepdims=True)
            results.append((low, square, dot(a_ref[...].astype(bf16), low)))
        for side, source, at in blocks:
            low, square, cross = results[side]
            pair_low[:, at] = low[:, source]
            pair_column[:, at] += square[:, source]
            pair_cross[:, at] += cross[:, source]

    @pl.when(step == pl.num_programs(0) - 1)
    def _():
        column = jnp.sqrt(pair_column[...])
        pair_column[...] = column
        pair_scale[...] = mixed_m[...] / column


def merge_others(out, down, gate, up):
    step = 8 * HD
    rows = 2 * HD
    near, wide = out[0].shape
    ff = down[0].shape[0]
    depth, width = gate[0].shape
    n_columns = wide // step
    starts = (n_columns, 2 * n_columns)
    n_pair = depth // rows
    at_out = lambda i: jnp.minimum(i, n_columns - 1)
    at_down = lambda i: jnp.clip(i - starts[0], 0, n_columns - 1)
    at_pair = lambda i: jnp.clip(i - starts[1], 0, n_pair - 1)
    cut = lambda height, at: pl.BlockSpec((height, step), lambda i: (0, at(i)))
    fixed = lambda *shape: pl.BlockSpec(shape, lambda i: (0,) * len(shape))
    pair_rows = lambda lanes: pl.BlockSpec((rows, lanes), lambda i: (at_pair(i), 0))
    turned = pl.BlockSpec((RANK, rows), lambda i: (0, at_pair(i)))
    shape = jax.ShapeDtypeStruct
    return pl.pallas_call(
        functools.partial(merge_kernel, starts),
        grid=(starts[1] + n_pair,),
        in_specs=[
            cut(near, at_out),
            fixed(RANK, near),
            cut(RANK, at_out),
            cut(ff, at_down),
            fixed(RANK, ff),
            cut(RANK, at_down),
            pair_rows(width),
            pair_rows(width),
            turned,
            turned,
            fixed(RANK, width),
            fixed(RANK, width),
            fixed(1, width),
            fixed(1, width),
        ],
        out_specs=[
            cut(1, at_out),
            cut(RANK, at_out),
            cut(1, at_down),
            cut(RANK, at_down),
            cut(ff, at_down),
            pair_rows(2 * width),
            fixed(RANK, 2 * width),
            fixed(1, 2 * width),
            fixed(1, 2 * width),
            fixed(1, 2 * width),
            fixed(RANK, 2 * width),
        ],
        out_shape=[
            shape((1, wide), f32),
            shape((RANK, wide), f32),
            shape((1, wide), f32),
            shape((RANK, wide), f32),
            shape((ff, wide), bf16),
            shape((depth, 2 * width), bf16),
            shape((RANK, 2 * width), f32),
            shape((1, 2 * width), f32),
            shape((1, 2 * width), f32),
            shape((1, 2 * width), f32),
            shape((RANK, 2 * width), f32),
        ],
        compiler_params=pltpu.CompilerParams(vmem_limit_bytes=VMEM_LIMIT),
        cost_estimate=cost(4 * depth * width * RANK, 8 * depth * width),
        name="merge_others",
    )(*out, *down, gate[0], up[0], gate[1], up[1], gate[2], up[2], gate[3], up[3])


def heads_kernel(scalars, x_ref, gain_ref, a_ref, b_ref, m_ref, cos_ref, sin_ref,
                 wk_hbm, wv_hbm, wq_hbm, *refs):
    take = taker(refs)
    peers = len(refs) - 12
    blocks = take(peers)
    normed_ref, low_ref, raw_ref, column_ref, scale_ref, cross_ref = take(6)
    x_all, w_all, merged_all, column_now, scale_now, sem = take(6)
    step = pl.program_id(0)
    rows = x_ref.shape[0]
    sources = (wk_hbm, wv_hbm, wq_hbm)

    def copy(number):
        return pltpu.make_async_copy(sources[number], w_all.at[number], sem.at[number])

    def merge(layer):
        slot = lax.rem(layer, 2)
        merged = w_all[layer].astype(f32) + low_rank(a_ref[layer], b_ref[layer])
        low = merged.astype(bf16)
        merged_all[slot] = low
        low_ref[...] = low
        column = jnp.sqrt(jnp.sum(merged * merged, axis=0, keepdims=True))
        scale = m_ref[layer] / column
        column_ref[...] = column
        scale_ref[...] = scale
        scale_now[slot] = scale

    @pl.when(step == 0)
    def _():
        for number in range(3):
            copy(number).start()
        part = rows // 4
        for i in range(4):
            at = pl.ds(i * part, part)
            x = x_ref[at, :].astype(f32)
            inverse = lax.rsqrt(jnp.mean(x * x, axis=-1, keepdims=True) + EPS)
            normed = (x * inverse * gain_ref[...]).astype(bf16)
            x_all[at, :] = normed
            normed_ref[at, :] = normed
        x_all[rows:, :] = a_ref[0].astype(bf16)
        copy(0).wait()
        merge(0)

    for number in (1, 2):

        @pl.when(step == number)
        def _(number=number):
            copy(number).wait()

    @pl.when(step > 0)
    def _():
        layer = step - 1
        slot = lax.rem(layer, 2)
        product = dot(x_all[...], merged_all[slot])
        scale = scale_now[slot]
        x_next = a_ref[jnp.minimum(step, 2)].astype(bf16)
        merge(jnp.minimum(step, 2))
        cross_ref[...] = product[rows:, :]
        raw = product[:rows, :]
        raw_ref[...] = raw.astype(bf16)
        value = raw * scale
        for t in range(peers):
            head = value[:, t * HD : (t + 1) * HD]
            rotated = head * cos_ref[...] + pltpu.roll(head, HALF, 1) * sin_ref[...]
            head = jnp.where(layer != 1, rotated, head).astype(bf16)
            place = t ^ scalars[0]
            for d, block in enumerate(blocks):

                @pl.when(place == d)
                def _(block=block, head=head):
                    block[layer] = head

        x_all[rows:, :] = x_next


def project_heads(order, x, gain, weights, a_t, b, m, cosine, sine):
    rows, depth = x.shape
    width = weights[0].shape[1]
    heads = width // HD
    merged_at = lambda i, s: (0, jnp.minimum(i, 2))
    done_at = lambda i, s: (0, jnp.maximum(i - 1, 0))
    fixed = lambda *shape: pl.BlockSpec(shape, lambda i, s: (0,) * len(shape))
    out_shape = [jax.ShapeDtypeStruct((3, rows, HD), bf16)] * heads
    out_shape += [
        jax.ShapeDtypeStruct((rows, depth), bf16),
        jax.ShapeDtypeStruct((depth, 3 * width), bf16),
        jax.ShapeDtypeStruct((rows, 3 * width), bf16),
        jax.ShapeDtypeStruct((1, 3 * width), f32),
        jax.ShapeDtypeStruct((1, 3 * width), f32),
        jax.ShapeDtypeStruct((RANK, 3 * width), f32),
    ]
    outs = pl.pallas_call(
        heads_kernel,
        grid_spec=pltpu.PrefetchScalarGridSpec(
            num_scalar_prefetch=1,
            grid=(4,),
            in_specs=[
                fixed(rows, depth),
                fixed(1, depth),
                fixed(3, RANK, depth),
                fixed(3, RANK, width),
                fixed(3, 1, width),
                fixed(rows, HD),
                fixed(rows, HD),
            ]
            + [pl.BlockSpec(memory_space=pl.ANY)] * 3,
            out_specs=[fixed(3, rows, HD)] * heads
            + [
                fixed(rows, depth),
                pl.BlockSpec((depth, width), merged_at),
                pl.BlockSpec((rows, width), done_at),
                pl.BlockSpec((1, width), merged_at),
                pl.BlockSpec((1, width), merged_at),
                pl.BlockSpec((RANK, width), done_at),
            ],
            scratch_shapes=[
                pltpu.VMEM((rows + RANK, depth), bf16),
                pltpu.VMEM((3, depth, width), bf16),
                pltpu.VMEM((2, depth, width), bf16),
                pltpu.VMEM((2, 1, width), f32),
                pltpu.VMEM((2, 1, width), f32),
                pltpu.SemaphoreType.DMA((3,)),
            ],
        ),
        out_shape=out_shape,
        compiler_params=pltpu.CompilerParams(vmem_limit_bytes=VMEM_LIMIT),
        cost_estimate=cost(6 * rows * depth * width, 16 * rows * depth),
        name="project_heads",
    )(order, x, gain, a_t, b, m, cosine, sine, *weights)
    return outs[:heads], *outs[heads:]


def assemble_kernel(peers, chunks, scalars, *refs):
    take = taker(refs)
    heads = take(peers)
    out_ref, down_ref, a_ref = take(3)
    near_refs = refs[peers + 3 :]
    width = a_ref.shape[1]
    parts = out_ref.shape[1] // width
    part = heads[0].shape[0] // chunks
    for d in range(peers):
        at = pl.ds(pl.multiple_of((scalars[0] ^ d) * HD, HD), HD)
        for c in range(chunks):
            near_refs[c][:part, at] = heads[d][c * part : (c + 1) * part, :]
    rows = []
    for ref in (out_ref, down_ref):
        high = ref[...].astype(bf16).astype(f32)
        for value in (high, ref[...] - high):
            rows += [value[:, j * width : (j + 1) * width] for j in range(parts)]
    near_refs[0][part : part + RANK, :] = jnp.concatenate(rows, axis=0).astype(bf16)
    near_refs[0][part + RANK :, :] = a_ref[...].astype(bf16)


def assemble(order, heads, square_out, square_down, a_t, chunks):
    peers = len(heads)
    part = heads[0].shape[0] // chunks
    width = peers * HD
    operands = [*heads, square_out, square_down, a_t]
    heights = [part + 2 * RANK] + [part] * (chunks - 1)
    out_shape = [jax.ShapeDtypeStruct((height, width), bf16) for height in heights]
    return pl.pallas_call(
        functools.partial(assemble_kernel, peers, chunks),
        grid_spec=pltpu.PrefetchScalarGridSpec(
            num_scalar_prefetch=1,
            grid=(1,),
            in_specs=[whole_spec(x) for x in operands],
            out_specs=[whole_spec(x) for x in out_shape],
        ),
        out_shape=out_shape,
        compiler_params=pltpu.CompilerParams(vmem_limit_bytes=VMEM_LIMIT),
        cost_estimate=cost(0, 0),
        name="assemble",
    )(order, *operands)


def unpack_kernel(size, scalars, *refs):
    take = taker(refs)
    blocks, m_refs = take(size), take(2)
    column_refs, scale_refs, (a_ref,) = take(2), take(2), take(1)
    width = blocks[0].shape[1]
    total = jnp.zeros((RANK, width), f32)
    for device in range(size):
        value = blocks[0][:RANK, :]
        for c in range(1, size):
            here = lax.rem(scalars[0] + c, size) == device
            value = jnp.where(here, blocks[c][:RANK, :], value)
        total = total + value.astype(f32)
    for side in range(2):
        for j in range(size):
            row = 2 * side * size + j
            square = total[row : row + 1, :] + total[row + size : row + size + 1, :]
            at = slice(j * width, (j + 1) * width)
            column = jnp.sqrt(square)
            column_refs[side][:, at] = column
            scale_refs[side][:, at] = m_refs[side][:, at] / column
    for c in range(size):
        device = lax.rem(scalars[0] + c, size)
        at = pl.ds(pl.multiple_of(device * width, HD), width)
        a_ref[:, at] = blocks[c][RANK:, :]


def unpack(k, blocks, rows, m_out, m_down):
    size = len(blocks)
    width = blocks[0].shape[1]
    wide = size * width
    row = jax.ShapeDtypeStruct((1, wide), f32)
    out_shape = [row] * 4 + [jax.ShapeDtypeStruct((RANK, wide), bf16)]
    tail = pl.BlockSpec((2 * RANK, width), lambda i, s: (rows // (2 * RANK), 0))
    return pl.pallas_call(
        functools.partial(unpack_kernel, size),
        grid_spec=pltpu.PrefetchScalarGridSpec(
            num_scalar_prefetch=1,
            grid=(1,),
            in_specs=[tail] * size + [whole_spec(m_out), whole_spec(m_down)],
            out_specs=[whole_spec(x) for x in out_shape],
        ),
        out_shape=out_shape,
        compiler_params=pltpu.CompilerParams(vmem_limit_bytes=VMEM_LIMIT),
        cost_estimate=cost(0, 0),
        name="unpack",
    )(k, *blocks, m_out, m_down)


def block_kernel(sizes, size, scalars, *refs):
    take = taker(refs)
    x_refs = take(size)
    a_ref, hid_ref, b_ref, out_scale_ref, gain_ref = take(5)
    cot_ref, down_scale_ref, scale_ref, wo_hbm, w_hbm, wd_hbm = take(6)
    hnorm_ref, resid_ref, raw_own_ref, low_ref, own_ref = take(5)
    act_ref, dz_ref, g_ref, dh_ref = take(4)
    total, through, dz_down, wo_all, w_all, wd_all, out_sem, sem, down_sem = take(9)
    k = scalars[0]
    rows, width = x_refs[0].shape
    part = rows // size
    starts = [sum(sizes[:j]) for j in range(len(sizes))]

    def out_copy(c):
        source = pl.ds(pl.multiple_of(lax.rem(k + c, size) * width, HD), width)
        return pltpu.make_async_copy(wo_hbm.at[source, :], wo_all.at[c], out_sem.at[c])

    def copies(j):
        both = pl.ds(2 * starts[j], 2 * sizes[j])
        one = pl.ds(starts[j], sizes[j])
        return (
            pltpu.make_async_copy(wd_hbm.at[one, :], wd_all.at[one, :], down_sem.at[j]),
            pltpu.make_async_copy(w_hbm.at[:, both], w_all.at[:, both], sem.at[j]),
        )

    for c in range(size):
        out_copy(c).start()
    for j in range(len(sizes)):
        for copy in copies(j):
            copy.start()
    for i in range(size):
        cot = cot_ref[i, 0].astype(f32)
        dz_down[i * part : (i + 1) * part, :] = (cot * down_scale_ref[...]).astype(bf16)

    mine = pl.ds(pl.multiple_of(k * part, 16), part)
    for c, x_ref in enumerate(x_refs):
        at = pl.ds(pl.multiple_of(lax.rem(k + c, size) * width, HD), width)
        own_ref[:, at] = x_ref[mine, :]
        out_copy(c).wait()
        x = x_ref[...]
        product = dot(x, wo_all[c])
        rank_part = dot_nt(x, a_ref[:, at])
        total[...] = total[...] + product if c else product
        through[...] = through[...] + rank_part if c else rank_part
    for piece in range(size):
        at = pl.ds(piece * part, part)
        low = through[at, :].astype(bf16)
        raw = total[at, :] + dot(low, b_ref[...])
        resid = hid_ref[piece, 0].astype(f32) + raw * out_scale_ref[...]
        inverse = lax.rsqrt(jnp.mean(resid * resid, axis=-1, keepdims=True) + EPS)
        hnorm_ref[at, :] = (resid * inverse * gain_ref[...]).astype(bf16)

        @pl.when(k == piece)
        def _(resid=resid, raw=raw, low=low):
            resid_ref[...] = resid
            raw_own_ref[...] = raw
            low_ref[...] = low

    def products(j):
        for copy in copies(j):
            copy.wait()
        both = slice(2 * starts[j], 2 * (starts[j] + sizes[j]))
        one = slice(starts[j], starts[j] + sizes[j])
        return dot(hnorm_ref[...], w_all[:, both]), dot_nt(dz_down[...], wd_all[one, :])

    ready = products(0)
    for j in range(len(sizes)):
        v, dact_all = ready
        if j + 1 < len(sizes):
            ready = products(j + 1)
        for i in range(sizes[j] // HD):
            hidden = starts[j] + i * HD
            gate_at = slice(2 * hidden, 2 * hidden + HD)
            up_at = slice(2 * hidden + HD, 2 * hidden + 2 * HD)
            raw_gate = v[:, 2 * i * HD : (2 * i + 1) * HD]
            raw_up = v[:, (2 * i + 1) * HD : (2 * i + 2) * HD]
            dact = dact_all[:, i * HD : (i + 1) * HD]
            scale_gate, scale_up = scale_ref[:, gate_at], scale_ref[:, up_at]
            gate = raw_gate * scale_gate
            up = raw_up * scale_up
            sigmoid = 1.0 / (1.0 + jnp.exp(-gate))
            silu = gate * sigmoid
            dgate = dact * up * (sigmoid + silu * (1.0 - sigmoid))
            dup = dact * silu
            act_ref[:, hidden : hidden + HD] = (silu * up).astype(bf16)
            g_ref[:, gate_at] = jnp.sum(dgate * raw_gate, axis=0, keepdims=True)
            g_ref[:, up_at] = jnp.sum(dup * raw_up, axis=0, keepdims=True)
            dz_ref[:, gate_at] = (dgate * scale_gate).astype(bf16)
            dz_ref[:, up_at] = (dup * scale_up).astype(bf16)
    dh_ref[...] = dot_nt(dz_ref[...], w_all[...]).astype(bf16)


def block(k, chunk, x, a_t, hidden, b2, out_scale, gain, cotangent, down_scale, scale, wo, w, wd):
    size, _, part, wide = hidden.shape
    rows, width = size * part, x[0].shape[1]
    ff = wd.shape[0]
    sizes = [ff]
    fixed = lambda *shape: pl.BlockSpec(shape, lambda i, s: (0,) * len(shape))
    view = pl.BlockSpec((size, 1, part, wide), lambda i, s: (0, chunk, 0, 0))
    shapes = [
        ((rows, wide), bf16),
        ((part, wide), f32),
        ((part, wide), f32),
        ((part, RANK), bf16),
        ((part, size * width), bf16),
        ((rows, ff), bf16),
        ((rows, 2 * ff), bf16),
        ((1, 2 * ff), f32),
        ((rows, wide), bf16),
    ]
    return pl.pallas_call(
        functools.partial(block_kernel, sizes, size),
        grid_spec=pltpu.PrefetchScalarGridSpec(
            num_scalar_prefetch=1,
            grid=(1,),
            in_specs=[fixed(rows, width)] * size
            + [
                fixed(RANK, size * width),
                view,
                fixed(RANK, wide),
                fixed(1, wide),
                fixed(1, wide),
                view,
                fixed(1, wide),
                fixed(1, 2 * ff),
            ]
            + [pl.BlockSpec(memory_space=pl.ANY)] * 3,
            out_specs=[fixed(*shape) for shape, _ in shapes],
            scratch_shapes=[
                pltpu.VMEM((rows, wide), f32),
                pltpu.VMEM((rows, RANK), f32),
                pltpu.VMEM((rows, wide), bf16),
                pltpu.VMEM((size, width, wide), bf16),
                pltpu.VMEM((wide, 2 * ff), bf16),
                pltpu.VMEM((ff, wide), bf16),
                pltpu.SemaphoreType.DMA((size,)),
                pltpu.SemaphoreType.DMA((len(sizes),)),
                pltpu.SemaphoreType.DMA((len(sizes),)),
            ],
        ),
        out_shape=[jax.ShapeDtypeStruct(shape, kind) for shape, kind in shapes],
        compiler_params=pltpu.CompilerParams(vmem_limit_bytes=60 * MIB),
        cost_estimate=cost(10 * rows * wide * ff, 6 * wide * ff),
        name="block",
    )(k, *x, a_t, hidden, b2, out_scale, gain, cotangent, down_scale, scale, wo, w, wd)


def back_out_kernel(scalars, *refs):
    take = taker(refs)
    earlier = take(len(refs) - 18)
    piece_ref, cot_ref, resid_ref, raw_ref, gain_ref, scale_ref = take(6)
    b_ref, own_ref, low_ref, w_ref, a_ref = take(5)
    dattn_ref, dresid_ref, dz_ref, g_ref, ap_ref, pb_ref = take(6)
    (through,) = take(1)

    @pl.when(pl.program_id(0) == 0)
    def _():
        grad = piece_ref[...].astype(f32)
        resid = resid_ref[...]
        inverse = lax.rsqrt(jnp.mean(resid * resid, axis=-1, keepdims=True) + EPS)
        scaled = grad * gain_ref[...]
        lean = jnp.mean(resid * scaled, axis=-1, keepdims=True)
        dresid = cot_ref[0, 0].astype(f32) + inverse * scaled
        dresid = dresid - resid * (inverse * inverse * inverse * lean)
        dresid_ref[...] = dresid
        dz = (dresid * scale_ref[...]).astype(bf16)
        dz_ref[...] = dz
        through[...] = dot_nt(dz, b_ref[...]).astype(bf16)
        sums = [
            jnp.sum(dresid * raw_ref[...], axis=0, keepdims=True),
            dot_tn(low_ref[...], dz),
            dot_tn(through[...], own_ref[...]),
        ]
        for i, ref in enumerate((g_ref, ap_ref, pb_ref)):
            ref[...] = sums[i] + earlier[i][...] if earlier else sums[i]

    dattn = dot_nt(dz_ref[...], w_ref[...]) + dot(through[...], a_ref[...])
    dattn_ref[0] = dattn.astype(bf16)


def back_out(k, chunk, piece, cotangent, resid, raw, gain, scale, b, own, low, w, a2_t, earlier):
    size = cotangent.shape[0]
    part, wide = resid.shape
    width = w.shape[0] // size
    fixed = lambda *shape: pl.BlockSpec(shape, lambda i, s: (0,) * len(shape))
    return pl.pallas_call(
        back_out_kernel,
        grid_spec=pltpu.PrefetchScalarGridSpec(
            num_scalar_prefetch=1,
            grid=(size,),
            in_specs=[fixed(*x.shape) for x in earlier]
            + [
                fixed(part, wide),
                pl.BlockSpec((1, 1, part, wide), lambda i, s: (s[0], chunk, 0, 0)),
                fixed(part, wide),
                fixed(part, wide),
                fixed(1, wide),
                fixed(1, wide),
                fixed(RANK, wide),
                fixed(*own.shape),
                fixed(part, RANK),
                pl.BlockSpec((width, wide), lambda i, s: (lax.rem(i + s[0], size), 0)),
                pl.BlockSpec((RANK, width), lambda i, s: (0, lax.rem(i + s[0], size))),
            ],
            out_specs=[
                pl.BlockSpec((1, part, width), lambda i, s: (i, 0, 0)),
                fixed(part, wide),
                fixed(part, wide),
                fixed(1, wide),
                fixed(RANK, wide),
                fixed(RANK, size * width),
            ],
            scratch_shapes=[pltpu.VMEM((part, RANK), bf16)],
        ),
        out_shape=[
            jax.ShapeDtypeStruct((size, part, width), bf16),
            jax.ShapeDtypeStruct((part, wide), f32),
            jax.ShapeDtypeStruct((part, wide), bf16),
            jax.ShapeDtypeStruct((1, wide), f32),
            jax.ShapeDtypeStruct((RANK, wide), f32),
            jax.ShapeDtypeStruct((RANK, size * width), f32),
        ],
        compiler_params=pltpu.CompilerParams(vmem_limit_bytes=VMEM_LIMIT),
        cost_estimate=cost(2 * part * width * size * wide, 2 * width * size * wide),
        name="back_out",
    )(k, *earlier, piece, cotangent, resid, raw, gain, scale, b, own, low, w, a2_t)


def unproject_kernel(heads, scalars, cos_ref, sin_ref, raw_ref, scale_ref, w_ref, *refs):
    take = taker(refs)
    grads = take(heads)
    dz_ref, g_ref, out_ref = refs[heads:]
    width = heads * HD

    @pl.when(pl.program_id(0) == 0)
    def _():
        for layer in range(3):
            for d in range(heads):
                at = pl.ds(pl.multiple_of(layer * width + (scalars[0] ^ d) * HD, HD), HD)
                grad = grads[d][layer].astype(f32)
                if layer != 1:
                    grad = grad * cos_ref[...] - pltpu.roll(grad, HALF, 1) * sin_ref[...]
                raw = raw_ref[:, at].astype(f32)
                g_ref[:, at] = jnp.sum(grad * raw, axis=0, keepdims=True)
                dz_ref[:, at] = (grad * scale_ref[:, at]).astype(bf16)

    out_ref[...] = dot_nt(dz_ref[...], w_ref[...]).astype(bf16)


def unproject(order, cosine, sine, raw, scale, w, grads):
    operands = [cosine, sine, raw, scale]
    rows, wide = raw.shape
    depth = w.shape[0]
    step = 8 * HD
    return pl.pallas_call(
        functools.partial(unproject_kernel, len(grads)),
        grid_spec=pltpu.PrefetchScalarGridSpec(
            num_scalar_prefetch=1,
            grid=(depth // step,),
            in_specs=[whole_spec(x) for x in operands]
            + [pl.BlockSpec((step, wide), lambda i, s: (i, 0))]
            + [whole_spec(x) for x in grads],
            out_specs=[
                whole_spec(raw),
                whole_spec(scale),
                pl.BlockSpec((rows, step), lambda i, s: (0, i)),
            ],
        ),
        out_shape=[
            jax.ShapeDtypeStruct(raw.shape, bf16),
            jax.ShapeDtypeStruct(scale.shape, f32),
            jax.ShapeDtypeStruct((rows, depth), bf16),
        ],
        compiler_params=pltpu.CompilerParams(vmem_limit_bytes=VMEM_LIMIT),
        cost_estimate=cost(2 * rows * wide * depth, 2 * wide * depth),
        name="unproject",
    )(order, *operands, w, *grads)


def shares_kernel(count, chunks, span, *refs):
    take = taker(refs)
    x_refs, dz_refs = take(chunks), take(chunks)
    a_ref, b_ref, w_ref, cross_ref, g_ref, m_ref, column_ref = take(7)
    share_a_ref, share_b_ref = take(2)
    low, up, radial = take(3)
    step = pl.program_id(0)
    wide = b_ref.shape[1]

    @pl.when(step == 0)
    def _():
        up[...] = jnp.zeros_like(up)
        radial[...] = jnp.zeros_like(radial)
        for c in range(chunks):
            low[c] = dot_nt(x_refs[c][...], a_ref[...]).astype(bf16)

    shrink = g_ref[...] * m_ref[...] / (column_ref[...] * column_ref[...] * column_ref[...])
    shape = (count * RANK, wide)
    column = lax.broadcasted_iota(jnp.int32, shape, 1) + step * wide
    layer_of = lax.rem(column // span, count)
    own = (lax.broadcasted_iota(jnp.int32, shape, 0) // RANK) == layer_of
    b_pad = jnp.where(own, jnp.concatenate([b_ref[...]] * count, axis=0), 0.0)
    b_low = b_pad.astype(bf16)
    ap = jnp.zeros(shape, f32)
    for c in range(chunks):
        dz = dz_refs[c][...]
        up[c] += dot_nt(dz, b_low)
        ap += dot_tn(low[c], dz)
    radial[...] += dot_nt((b_pad * shrink).astype(bf16), w_ref[...])
    ap = jnp.where(own, ap, 0.0)
    picked = ap[:RANK]
    for i in range(1, count):
        picked = picked + ap[i * RANK : (i + 1) * RANK]
    share_b_ref[...] = (SCALING * (picked - cross_ref[...] * shrink)).astype(bf16)

    @pl.when(step == pl.num_programs(0) - 1)
    def _():
        total = -radial[...]
        for c in range(chunks):
            total = total + dot_tn(up[c].astype(bf16), x_refs[c][...])
        share_a_ref[...] = (SCALING * total).astype(bf16)


def layer_shares(inputs, a_t, dz, b, span, merged, cross, g, magnitude, column):
    chunks = len(inputs)
    rows, depth = inputs[0].shape
    width = dz[0].shape[1]
    count = a_t.shape[0] // RANK
    step = width // count
    columns = lambda height: pl.BlockSpec((height, step), lambda i: (0, i))
    fixed = lambda x: pl.BlockSpec(x.shape, lambda i: (0, 0))
    return pl.pallas_call(
        functools.partial(shares_kernel, count, chunks, span),
        grid=(width // step,),
        in_specs=[fixed(x) for x in inputs]
        + [columns(rows)] * chunks
        + [fixed(a_t), columns(RANK), columns(depth), columns(RANK)]
        + [columns(1)] * 3,
        out_specs=[fixed(a_t), columns(RANK)],
        out_shape=[
            jax.ShapeDtypeStruct(a_t.shape, bf16),
            jax.ShapeDtypeStruct((RANK, width), bf16),
        ],
        scratch_shapes=[
            pltpu.VMEM((chunks, rows, count * RANK), bf16),
            pltpu.VMEM((chunks, rows, count * RANK), f32),
            pltpu.VMEM(a_t.shape, f32),
        ],
        compiler_params=pltpu.CompilerParams(vmem_limit_bytes=VMEM_LIMIT),
        cost_estimate=cost(rows * depth * 64, depth * width),
        name="shares",
    )(*inputs, *dz, a_t.astype(bf16), b, merged, cross, g, magnitude, column)


def down_kernel(chunks, *refs):
    take = taker(refs)
    act_refs = take(chunks)
    w_ref, cot_ref, scale_ref, a_ref, b_ref = take(5)
    raw_ref, g_ref, ap_ref, pb_ref = take(4)
    low, up = take(2)
    step = pl.program_id(0)
    rows = act_refs[0].shape[0]
    size, _, part, wide = cot_ref.shape

    @pl.when(step == 0)
    def _():
        up[...] = jnp.zeros_like(up)
        for c in range(chunks):
            low[c] = dot_nt(act_refs[c][...], a_ref[...]).astype(bf16)

    g = jnp.zeros((1, wide), f32)
    ap = jnp.zeros((RANK, wide), f32)
    b_low = b_ref[...].astype(bf16)
    for c in range(chunks):
        raw = dot(act_refs[c][...], w_ref[...])
        raw_ref[:, c] = raw.astype(bf16).reshape(size, part, wide)
        cot = cot_ref[:, c].reshape(rows, wide).astype(f32)
        g += jnp.sum(cot * raw, axis=0, keepdims=True)
        dz = (cot * scale_ref[...]).astype(bf16)
        up[c] += dot_nt(dz, b_low)
        ap += dot_tn(low[c], dz)
    g_ref[...] = g
    ap_ref[...] = ap.astype(bf16)

    @pl.when(step == pl.num_programs(0) - 1)
    def _():
        total = jnp.zeros(pb_ref.shape, f32)
        for c in range(chunks):
            total = total + dot_tn(up[c].astype(bf16), act_refs[c][...])
        pb_ref[...] = total.astype(bf16)


def down_project(acts, w, cotangent, scale, a_t, b):
    chunks = len(acts)
    rows, ff = acts[0].shape
    wide = w.shape[1]
    step = 2 * HD
    size, _, part, _ = cotangent.shape
    columns = lambda height: pl.BlockSpec((height, step), lambda i: (0, i))
    fixed = lambda *shape: pl.BlockSpec(shape, lambda i: (0,) * len(shape))
    view = pl.BlockSpec((size, chunks, part, step), lambda i: (0, 0, 0, i))
    return pl.pallas_call(
        functools.partial(down_kernel, chunks),
        grid=(wide // step,),
        in_specs=[fixed(rows, ff)] * chunks
        + [columns(ff), view, columns(1), fixed(RANK, ff), columns(RANK)],
        out_specs=[view, columns(1), columns(RANK), fixed(RANK, ff)],
        out_shape=[
            jax.ShapeDtypeStruct(cotangent.shape, bf16),
            jax.ShapeDtypeStruct((1, wide), f32),
            jax.ShapeDtypeStruct((RANK, wide), bf16),
            jax.ShapeDtypeStruct((RANK, ff), bf16),
        ],
        scratch_shapes=[
            pltpu.VMEM((chunks, rows, RANK), bf16),
            pltpu.VMEM((chunks, rows, RANK), f32),
        ],
        compiler_params=pltpu.CompilerParams(vmem_limit_bytes=VMEM_LIMIT),
        cost_estimate=cost(2 * chunks * rows * ff * wide, 2 * ff * wide),
        name="down_project",
    )(*acts, w, cotangent, scale, a_t.astype(bf16), b)


def pack_kernel(plan, scalars, *refs):
    out_ref = refs[-1]
    out_ref[...] = jnp.zeros_like(out_ref)
    for ref, (parts, placed, rows) in zip(refs[:-1], plan):
        height, width = ref.shape
        wide = width // parts
        lanes = slice(0, wide)
        if placed:
            lanes = pl.ds(pl.multiple_of(scalars[0] * wide, HD), wide)
        if height == 1:
            value = [ref[:, i * wide : (i + 1) * wide].astype(f32) for i in range(parts)]
            value.append(jnp.zeros((RANK - parts, wide), f32))
            value = jnp.concatenate(value, axis=0).astype(bf16)
            out_ref[rows[0] : rows[0] + RANK, lanes] = value
            continue
        for i in range(parts):
            for j in range(height // RANK):
                row = rows[i * (height // RANK) + j]
                value = ref[j * RANK : (j + 1) * RANK, i * wide : (i + 1) * wide].astype(bf16)
                out_ref[row : row + RANK, lanes] = value


def pack(k, height, width, *entries):
    arrays = [entry[0] for entry in entries]
    plan = [entry[1:] for entry in entries]
    return pl.pallas_call(
        functools.partial(pack_kernel, plan),
        grid_spec=pltpu.PrefetchScalarGridSpec(
            num_scalar_prefetch=1,
            grid=(1,),
            in_specs=[whole_spec(x) for x in arrays],
            out_specs=pl.BlockSpec((height, width), lambda i, s: (0, 0)),
        ),
        out_shape=jax.ShapeDtypeStruct((height, width), bf16),
        compiler_params=pltpu.CompilerParams(vmem_limit_bytes=VMEM_LIMIT),
        cost_estimate=cost(height * width, 4 * height * width),
        name="pack",
    )(k, *arrays)


def span_positions(row_ids, span_order, span_len):
    slot_ids = row_ids // span_len
    slot_table = jnp.arange(span_order.shape[0], dtype=jnp.int32)
    picked = jnp.sum(
        jnp.where(slot_ids[:, None] == slot_table[None, :], span_order[None, :], 0), axis=1
    )
    return picked * span_len + row_ids % span_len


def rotary_tables(positions):
    lane = np.arange(HD)
    frequency = (ROPE_BASE ** (-2.0 * (lane % HALF) / HD)).astype(np.float32)
    sign = np.where(lane < HALF, -1.0, 1.0).astype(np.float32)
    angles = positions.astype(f32)[:, None] * frequency[None, :]
    return jnp.cos(angles), jnp.sin(angles) * sign[None, :]


def pick_blocks(blocks, index):
    out = blocks[0]
    for i in range(1, len(blocks)):
        out = jnp.where(index == i, blocks[i], out)
    return out


def inverse_rms(values):
    return lax.rsqrt(jnp.mean(values * values, axis=-1, keepdims=True) + EPS)


def rms_backward(values, gain_vec, grad_in, inverse):
    scaled = grad_in * gain_vec
    return inverse * scaled - values * inverse * inverse * inverse * jnp.mean(
        values * scaled, axis=-1, keepdims=True
    )


def per_device(
    hidden_in,
    cotangent,
    segment_ids,
    padding,
    span_order,
    gain_attn,
    gain_mlp,
    w_query,
    w_key,
    w_value,
    w_out,
    w_gate,
    w_up,
    w_down,
    a_query,
    b_query,
    m_query,
    a_key,
    b_key,
    m_key,
    a_value,
    b_value,
    m_value,
    a_out,
    b_out,
    m_out,
    a_gate,
    b_gate,
    m_gate,
    a_up,
    b_up,
    m_up,
    a_down,
    b_down,
    m_down,
):
    rows, width = hidden_in.shape
    span_len = rows // 2
    near_width = w_query.shape[1]
    peers = near_width // HD
    n_mp = lax.axis_size("mp")
    n_seq = lax.axis_size("seq")
    n_doc = lax.axis_size("doc")
    groups = n_seq // peers
    copies = n_seq * n_doc
    share = rows // n_mp
    chunks = CHUNKS
    part = share // chunks
    k = lax.axis_index("mp")
    doc = lax.axis_index("doc")
    seq = lax.axis_index("seq")
    me = lax.rem(seq, peers)
    my_group = seq // peers
    order = jnp.reshape(me, (1,)).astype(jnp.int32)
    k_scalar = jnp.reshape(k, (1,)).astype(jnp.int32)

    slice_rows = near_width // n_doc
    wo_slice = lax.dynamic_slice_in_dim(w_out, doc * slice_rows, slice_rows, 0)
    wo_all = lax.all_gather(wo_slice, ("mp", "doc"), axis=0, tiled=True)

    slots = [
        2 * (my_group * peers + (me ^ d)) + half for d in range(peers) for half in range(2)
    ]
    slots += [
        2 * (g * peers + (me ^ d)) + half
        for g in range(groups)
        for d in range(peers)
        for half in range(2)
    ]
    slots = jnp.stack(slots)
    table = jnp.arange(span_order.shape[0], dtype=jnp.int32)
    places = jnp.sum(jnp.where(slots[:, None] == table[None, :], span_order[None, :], 0), axis=1)
    scalars = jnp.concatenate([places, k_scalar]).astype(jnp.int32)
    row_ids = jnp.arange(rows, dtype=jnp.int32) + seq * rows
    cosine, sine = rotary_tables(span_positions(row_ids, span_order, span_len))
    codes = seq_exchange([segment_ids * 2 + padding] * peers)
    (hidden_next,) = after([hidden_in], *codes)

    a_heads = jnp.stack([a_key.T, a_value.T, a_query.T])
    b_heads = [b_key, b_value, b_query]
    m_heads = jnp.concatenate([m_key, m_value, m_query])[None, :]
    blocks, normed, wh_low, raw_heads, column_heads, scale_heads, cross_heads = project_heads(
        order,
        hidden_next,
        gain_attn[None, :],
        (w_key, w_value, w_query),
        a_heads,
        jnp.stack(b_heads),
        jnp.stack([m_key, m_value, m_query])[:, None, :],
        cosine,
        sine,
    )
    heads = seq_exchange(blocks)

    codes = [x.reshape(rows, 1) for x in codes]
    w_out_next, w_down_next, w_gate_next, w_up_next = after(
        [w_out, w_down, w_gate, w_up], raw_heads
    )
    (
        square_out,
        cross_out,
        square_down,
        cross_down,
        wd_low,
        wgu_low,
        cross_gu,
        column_gu,
        scale_gu,
        m_gu,
        b_gu,
    ) = merge_others(
        (w_out_next, a_out.T, b_out),
        (w_down_next, a_down.T, b_down),
        (w_gate_next, a_gate.T, b_gate, m_gate[None, :]),
        (w_up_next, a_up.T, b_up, m_up[None, :]),
    )

    extra = []
    if groups > 1:
        members = [[g * peers + i for g in range(groups)] for i in range(peers)]
        gather = lambda x: lax.all_gather(
            x[None], "seq", axis=0, tiled=True, axis_index_groups=members
        )
        extra = [gather(jnp.stack([x[:2] for x in heads])), gather(jnp.stack(codes))]
    heads_next = after(heads, square_out)
    o_blocks, lse = attention_forward(
        scalars, heads_next, codes, extra, groups, n_mp, chunks
    )
    o_heads = seq_exchange(o_blocks)
    near_chunks = assemble(order, o_heads, square_out, square_down, a_out.T, chunks)

    def chunked(values):
        return values.reshape(n_mp, chunks, part, values.shape[-1])

    hid_view, cot_view = chunked(hidden_in), chunked(cotangent)
    b_out_low = b_out.astype(bf16)
    acts, hnorms, dz_gus, dh_chunks = [], [], [], []
    resid_own, raw_out_own, out_low_own, near_own = [], [], [], []
    g_gu = 0.0
    lines = ([near_chunks[0]], [near_chunks[0]])
    for step in range(1, n_mp):
        line_step(*lines, step)
    gathered_chunks = [line_blocks(*lines)]
    for c in range(1, chunks):
        (near_next,) = after([near_chunks[c]], wo_all, *gathered_chunks[0])
        others = lax.all_gather(near_next, "mp", axis=0)
        gathered_chunks.append(
            [near_chunks[c]]
            + [
                lax.dynamic_index_in_dim(others, lax.rem(k + i, n_mp), 0, keepdims=False)
                for i in range(1, n_mp)
            ]
        )
    column_out, column_down, scale_out, scale_down, a_out_low = unpack(
        k_scalar, gathered_chunks[0], n_mp * part, m_out[None, :], m_down[None, :]
    )
    a_out_twice = SCALING * a_out_low
    for c in range(chunks):
        gathered = gathered_chunks[c]
        if c > 0:
            gathered = after(gathered, dh_chunks[-1])
        hnorm, resid, raw_out, out_low, own, act, dz_gu, g, dh = block(
            k_scalar,
            c,
            gathered,
            a_out_low,
            hid_view,
            (SCALING * b_out).astype(bf16),
            scale_out,
            gain_mlp[None, :],
            cot_view,
            scale_down,
            scale_gu,
            wo_all,
            wgu_low,
            wd_low,
        )
        g_gu = g_gu + g
        dh_chunks.append(dh)
        acts.append(act)
        hnorms.append(hnorm)
        dz_gus.append(dz_gu)
        resid_own.append(resid)
        raw_out_own.append(raw_out)
        out_low_own.append(out_low)
        near_own.append(own)

    def scatter(parts):
        return lax.psum_scatter(parts, "mp", scatter_dimension=0, tiled=True)

    pieces = [scatter(x) for x in dh_chunks]

    arrived, dresid_own, dz_out = [], [], []
    out_sums = ()
    earlier = dh_chunks[-1]
    for c in range(chunks):
        (own_piece,) = after([pieces[c]], earlier)
        dattn, dresid, dz, *out_sums = back_out(
            k_scalar,
            c,
            own_piece,
            cot_view,
            resid_own[c],
            raw_out_own[c],
            gain_mlp[None, :],
            scale_out,
            b_out_low,
            near_own[c],
            out_low_own[c],
            wo_all,
            a_out_twice,
            out_sums,
        )
        arrived.append(dattn[0])
        (dattn,) = after([dattn], *pieces)
        for shift in range(1, n_mp):
            pairs = [(i, (i + shift) % n_mp) for i in range(n_mp)]
            arrived.append(lax.ppermute(dattn[shift], "mp", pairs))
        dresid_own.append(dresid)
        dz_out.append(dz)
        earlier = dz
        if c == 0:
            acts_next = after(acts, dz)
            raw_down, g_down, ap_down, pb_down = down_project(
                acts_next, wd_low, cot_view, scale_down, a_down.T, b_down
            )
            earlier = g_down
    arrived = jnp.concatenate(arrived, axis=0)
    by_head = [arrived[:, h * HD : (h + 1) * HD] for h in range(peers)]
    grad_blocks = seq_exchange([pick_blocks(by_head, me ^ d) for d in range(peers)])
    dresid_own = jnp.concatenate(dresid_own, axis=0)
    g_out, ap_out, pb_out = out_sums

    grads, dkv = attention_backward(
        scalars, heads_next, codes, extra, o_blocks, grad_blocks, lse, groups, n_mp, chunks
    )
    if groups > 1:
        members = [[g * peers + i for g in range(groups)] for i in range(peers)]
        dkv = lax.psum_scatter(
            dkv, "seq", scatter_dimension=0, tiled=True, axis_index_groups=members
        )
        grads = [jnp.concatenate([dkv[0, d], grads[d]], axis=0) for d in range(peers)]
    head_grads = seq_exchange(grads)

    hnorms_next, dz_gus_next = after([tuple(hnorms), tuple(dz_gus)], grads[0])
    share_a_gu, share_b_gu = layer_shares(
        hnorms_next,
        jnp.concatenate([a_gate.T, a_up.T], axis=0),
        dz_gus_next,
        b_gu,
        HD,
        wgu_low,
        cross_gu,
        g_gu,
        m_gu,
        column_gu,
    )
    (raw_down,) = after([raw_down], *grad_blocks)
    down_own = scatter(raw_down.reshape(rows, width))
    head_grads = after(head_grads, share_a_gu)

    dz_heads, g_heads, dnormed = unproject(
        order, cosine, sine, raw_heads, scale_heads, wh_low, head_grads
    )
    dnormed_own = scatter(dnormed)

    (down_own,) = after([down_own], dnormed)
    result = jnp.concatenate(resid_own, axis=0) + down_own.astype(f32) * scale_down
    hidden_own = lax.dynamic_slice_in_dim(hidden_in, k * share, share, 0).astype(f32)


    share_a_heads, share_b_heads = layer_shares(
        after([normed], result),
        a_heads.reshape(3 * RANK, width),
        [dz_heads],
        jnp.concatenate(b_heads, axis=1),
        near_width,
        wh_low,
        cross_heads,
        g_heads,
        m_heads,
        column_heads,
    )
    parts = n_doc * peers
    part_rows = 3 * RANK
    summed = [(u // 2) * part_rows + (u % 2) * RANK for u in range(2 * parts)]
    apart = [u * part_rows + 2 * RANK for u in range(parts)]
    totals = pack(
        k_scalar,
        parts * part_rows,
        width,
        (share_a_gu, 1, False, summed[0:2]),
        (ap_down, 1, False, summed[2:3]),
        (cross_out / copies, 1, False, summed[3:4]),
        (cross_down / copies, 1, False, summed[4:5]),
        (ap_out, 1, False, summed[5:6]),
        (jnp.concatenate([g_down, g_out], axis=1), 2, False, summed[6:7]),
        (pb_out, 1, False, summed[7:8]),
        (share_a_heads, 1, False, summed[8:11]),
        (share_b_heads, 3, True, summed[11:14]),
        (g_heads, 3, True, summed[14:15]),
        (share_b_gu, 2, False, apart[0:2]),
        (pb_down, 1, False, apart[2:3]),
        (g_gu, 2, False, apart[3:4]),
    )
    totals = spread_join(spread_sum(doc_halve(totals), peers, ["mp"], 2 * RANK), peers)
    hidden_inverse = inverse_rms(hidden_own)
    (totals,) = after([totals], dnormed_own, result, hidden_inverse)
    totals = doc_join(totals).astype(f32)

    def unit(index, rows=RANK):
        return totals[summed[index] : summed[index] + rows]

    def own_columns(values):
        return lax.dynamic_slice_in_dim(values, k * near_width, near_width, 1)

    def unit_apart(index, rows=RANK):
        return totals[apart[index] : apart[index] + rows, : w_gate.shape[1]]

    grad_input = dresid_own + rms_backward(
        hidden_own, gain_attn, dnormed_own.astype(f32), hidden_inverse
    )

    total_g_down, total_g_out = unit(6, 2)[:1], unit(6, 2)[1:]
    shrink_out = total_g_out * m_out / (column_out * column_out * column_out)
    shrink_down = total_g_down * m_down / (column_down * column_down * column_down)
    turned_out = (b_out * shrink_out).astype(bf16)
    radial_out = dot_nt(turned_out, w_out) + SCALING * dot(
        dot_nt(turned_out, b_out.astype(bf16)), a_out.T
    )
    radial_down = dot_nt((b_down * shrink_down).astype(bf16), wd_low)
    grad_a_out = SCALING * (own_columns(unit(7)) - radial_out)
    grad_a_down = SCALING * (unit_apart(2) - radial_down)
    grad_b_out = SCALING * (unit(5) - unit(3) * shrink_out)
    grad_b_down = SCALING * (unit(2) - unit(4) * shrink_down)
    g_rows = own_columns(unit(14, 3))
    g_rows = [
        g_rows[i] / column_heads[0, i * near_width : (i + 1) * near_width] for i in range(3)
    ]
    both = jnp.concatenate([unit_apart(0), unit_apart(1)], axis=1)
    g_both = jnp.concatenate([unit_apart(3, 2)[:1], unit_apart(3, 2)[1:]], axis=1)
    grad_m_gate, grad_m_up = separate(g_both / column_gu)
    grad_b_gate, grad_b_up = separate(both)
    return (
        result,
        grad_input,
        unit(10).T,
        own_columns(unit(13)),
        g_rows[2],
        unit(8).T,
        own_columns(unit(11)),
        g_rows[0],
        unit(9).T,
        own_columns(unit(12)),
        g_rows[1],
        grad_a_out.T,
        grad_b_out,
        (total_g_out / column_out)[0],
        unit(0).T,
        grad_b_gate,
        grad_m_gate[0],
        unit(1).T,
        grad_b_up,
        grad_m_up[0],
        grad_a_down.T,
        grad_b_down,
        (total_g_down / column_down)[0],
    )


def solution(mesh):
    rows = P(("doc", "seq"))
    split_columns = (P(None, "mp"), P(None, "mp"))
    column_layer = (P(), P(None, "mp"), P("mp"))
    row_layer = (P("mp", None), P(), P())
    in_specs = (
        P(("doc", "seq"), None),
        P(("doc", "seq"), None),
        rows,
        rows,
        P(),
        P(),
        P(),
        P(None, "mp"),
        P(None, "mp"),
        P(None, "mp"),
        P("mp", None),
        *split_columns,
        P("mp", None),
        *column_layer,
        *column_layer,
        *column_layer,
        *row_layer,
        *column_layer,
        *column_layer,
        *row_layer,
    )
    out_specs = (
        P(("doc", "seq", "mp"), None),
        P(("doc", "seq", "mp"), None),
        *column_layer,
        *column_layer,
        *column_layer,
        *row_layer,
        *column_layer,
        *column_layer,
        *row_layer,
    )
    return jax.shard_map(
        per_device, mesh=mesh, in_specs=in_specs, out_specs=out_specs, check_vma=False
    )
```
